32 devices in a mesh: dp: 16 (over z, y, x), tensor: 2 (over core).
Axes of the slice: x: 2, y: 2, z: 4, core: 2. Of those that a mesh axis runs over, the one named last changes fastest.
Arguments:
- inputs: bfloat16 [16384, 1024], P('dp'), may hold values from -6 to 6
- cotangent: bfloat16 [16384, 1024], P('dp'), may hold values from -6 to 6
- segment_ids: int32 [16384], P('dp'), may hold values from 0 to 127, never falling along the last dimension, each value on 1 to 512 neighbouring positions
- attn_gain: float32 [1024], replicated, may hold values from 0.25 to 1.75
- w_query: bfloat16 [1024, 1024], P(None, 'tensor'), may hold values from -0.1875 to 0.1875
- w_key: bfloat16 [1024, 512], P(None, 'tensor'), may hold values from -0.1875 to 0.1875
- w_value: bfloat16 [1024, 512], P(None, 'tensor'), may hold values from -0.1875 to 0.1875
- query_gain: float32 [64], replicated, may hold values from 0.25 to 1.75
- key_gain: float32 [64], replicated, may hold values from 0.25 to 1.75
- w_output: bfloat16 [1024, 1024], P(None, 'tensor'), may hold values from -0.5 to 0.5
- ffn_gain: float32 [1024], replicated, may hold values from 0.25 to 1.75
- w_gate: bfloat16 [1024, 4608], P(None, 'tensor'), may hold values from -0.1875 to 0.1875
- w_up: bfloat16 [1024, 4608], P(None, 'tensor'), may hold values from -0.1875 to 0.1875
- w_down: bfloat16 [1024, 4608], P(None, 'tensor'), may hold values from -0.09375 to 0.09375
Outputs:
- block_out: bfloat16 [16384, 1024], P('dp')
- grad_inputs: bfloat16 [16384, 1024], P('dp')
- grad_attn_gain: float32 [1024], P('dp')
- grad_w_query: float32 [1024, 1024], P('dp', 'tensor')
- grad_w_key: float32 [1024, 512], P('dp', 'tensor')
- grad_w_value: float32 [1024, 512], P('dp', 'tensor')
- grad_query_gain: float32 [64], replicated
- grad_key_gain: float32 [64], replicated
- grad_w_output: float32 [1024, 1024], P('dp', 'tensor')
- grad_ffn_gain: float32 [1024], P('dp')
- grad_w_gate: float32 [1024, 4608], P('dp', 'tensor')
- grad_w_up: float32 [1024, 4608], P('dp', 'tensor')
- grad_w_down: float32 [1024, 4608], P('dp', 'tensor')
The draws below stay inside these ranges and needn't reach their ends.
Inputs may be any that keep to these rules, and one draw needn't show every extreme that they name: `segment_ids`: ids never fall along the tokens; each document has 1 to 512 tokens, one of them exactly 512.
All inputs are finite; a program needn't handle non-finite values.
Results may differ from the reference program's by a relative error of at most 0.014.
The reference program's roundings to bfloat16 on the way count: a program that leaves them out, or rounds other values in their place, can miss the bound.
Values sent between devices are 32-bit elements; how exact they have to be, the bound alone decides.
No kernel may reach another device: no remote copies, remote signals or barrier semaphores. Data moves between devices by JAX's collectives and lax.ppermute only.
A program may use at most 192 MiB of HBM per device.

```python
import math
import jax
import jax.numpy as jnp
import numpy as np
from jax import lax

D = 1024
HEADS = 16
KV_HEADS = 8
HEAD_DIM = 64
FF = 4608
SEQ = 1024
SEQS = 16
TOKENS = 16384
QW = 1024
KW = 512
N_DP = 16


def steps_of(rng, shape, pieces, low, largest):
    level, own = 1.0, jax.random.fold_in(rng, 6)
    for position, blocks in pieces:
        steps = jnp.exp(jax.random.uniform(jax.random.fold_in(own, position), (blocks,), jnp.float32, low / len(pieces), largest / len(pieces)))
        level = level * jnp.repeat(steps, shape[position] // blocks).reshape([-1 if axis == position else 1 for axis in range(len(shape))])
    return level


def length_profile(amount, total, most, skew):
    portions = [(1 << 20) // math.isqrt(rank ** skew) + 1 for rank in range(2, amount + 1)]
    spare, counts = total - most - (amount - 1), [1] * (amount - 1)
    while spare > 0:
        free = [i for i in range(amount - 1) if counts[i] < most]
        pool, remaining = sum([portions[i] for i in free]), spare
        for i in free:
            extra = min(most - counts[i], max(1, remaining * portions[i] // pool), spare)
            counts[i] = counts[i] + extra
            spare = spare - extra
    return np.array([most] + counts)


def uneven_parts(rng, amount, total, limit, lean):
    if amount == 2:
        one = jax.random.randint(rng, (), max(1, total - limit), min(limit, total - 1) + 1)
        return jnp.stack([one, total - one])
    sizes = jnp.asarray(length_profile(amount, total, limit, lean), jnp.int32)
    pairs = (amount - 1) // 2
    giver, receiver = sizes[1:1 + 2 * pairs:2], sizes[2:2 + 2 * pairs:2]
    room = jnp.minimum(giver - 1, limit - receiver)
    passed = jax.random.randint(jax.random.fold_in(rng, 1), (pairs,), 0, 1 << 20) % (room + 1)
    sizes = sizes.at[1:1 + 2 * pairs:2].set(giver - passed).at[2:2 + 2 * pairs:2].set(receiver + passed)
    return sizes[jax.random.permutation(jax.random.fold_in(rng, 2), amount)]


def normal_values(rng, shape, deviation, reach, cuts=(), kind=jnp.bfloat16):
    values = deviation * jax.random.normal(rng, shape, jnp.float32)
    if cuts:
        values = values * steps_of(rng, shape, cuts, -0.22, 0.18)
    return jnp.clip(values, -reach, reach).astype(kind)


def setup_inputs(seed: int = 0) -> dict:
    key_of = jax.random.split(jax.random.key(seed), 15)
    return {
        "inputs": normal_values(key_of[0], (TOKENS, D), 1.0, 6.0, ((0, 16),)),
        "cotangent": normal_values(key_of[1], (TOKENS, D), 1.0, 6.0, ((0, 16),)),
        "segment_ids": jnp.searchsorted(jnp.cumsum(uneven_parts(key_of[2], 8 * N_DP, TOKENS, SEQ // 2, 2)), jnp.arange(TOKENS), side="right").astype(jnp.int32),
        "attn_gain": jnp.clip(1.0 + 0.15 * jax.random.normal(key_of[3], (D,), jnp.float32), 0.25, 1.75),
        "w_query": normal_values(key_of[4], (D, QW), D ** -0.5, 0.1875, ((1, 2),)),
        "w_key": normal_values(key_of[5], (D, KW), D ** -0.5, 0.1875, ((1, 2),)),
        "w_value": normal_values(key_of[6], (D, KW), D ** -0.5, 0.1875, ((1, 2),)),
        "query_gain": jnp.clip(1.0 + 0.15 * jax.random.normal(key_of[7], (HEAD_DIM,), jnp.float32), 0.25, 1.75),
        "key_gain": jnp.clip(1.0 + 0.15 * jax.random.normal(key_of[8], (HEAD_DIM,), jnp.float32), 0.25, 1.75),
        "w_output": normal_values(key_of[9], (D, QW), (QW // 8) ** -0.5, 0.5, ((1, 2),)),
        "ffn_gain": jnp.clip(1.0 + 0.15 * jax.random.normal(key_of[10], (D,), jnp.float32), 0.25, 1.75),
        "w_gate": normal_values(key_of[11], (D, FF), D ** -0.5, 0.1875, ((1, 2),)),
        "w_up": normal_values(key_of[12], (D, FF), D ** -0.5, 0.1875, ((1, 2),)),
        "w_down": normal_values(key_of[13], (D, FF), FF ** -0.5, 0.09375, ((1, 2),)),
    }


epsilon = 1e-05
rope_base = 1000000.0
masked_score = -1e+30
highest = lax.Precision.HIGHEST

@jax.custom_vjp
def low(v):
    return lax.optimization_barrier(v.astype(jnp.bfloat16)).astype(jnp.float32)

@jax.custom_vjp
def low_back(v):
    return v

def low_keep(v):
    return (low(v), None)

def low_pass(kept, grad):
    return (grad,)

def back_keep(v):
    return (v, None)

def back_low(kept, grad):
    return (low(grad),)
low.defvjp(low_keep, low_pass)
low_back.defvjp(back_keep, back_low)

def rms_scale(values, scales):
    return values * lax.rsqrt(lax.optimization_barrier(jnp.mean(values * values, axis=-1, keepdims=True)) + epsilon) * scales

def rope_tables(segments):
    length = segments.shape[0]
    places = jnp.arange(length, dtype=jnp.int32)
    earlier = jnp.concatenate([segments[:1] - 1, segments[:-1]])
    starts = lax.cummax(jnp.where(segments != earlier, places, 0), axis=0)
    offsets = (places - starts).astype(jnp.float32)
    halves = HEAD_DIM // 2
    inverse = rope_base ** (-2.0 * jnp.arange(halves, dtype=jnp.float32) / HEAD_DIM)
    angles = offsets[:, None] * inverse[None, :]
    return (jnp.cos(angles), jnp.sin(angles))

def rotate(values, cosine, sine):
    halves = HEAD_DIM // 2
    first = values[..., :halves]
    second = values[..., halves:]
    cos_wide = cosine[:, None, :]
    sin_wide = sine[:, None, :]
    return jnp.concatenate([first * cos_wide - second * sin_wide, second * cos_wide + first * sin_wide], axis=-1)

def head_piece(linear, scales, cosine, sine):
    row_count = linear.shape[0]
    head_count = linear.shape[1] // HEAD_DIM
    shaped = linear.reshape(row_count, head_count, HEAD_DIM)
    return rotate(rms_scale(shaped, scales), cosine, sine).reshape(row_count, head_count * HEAD_DIM)

def attend(query, key_rot, value_rot, segments, offset):
    span = min(512, SEQ)
    groups = HEADS // KV_HEADS
    q_block = lax.dynamic_slice_in_dim(query, offset, span, 0).reshape(span, KV_HEADS, groups, HEAD_DIM)
    scores = jnp.einsum('qkgd,skd->kgqs', q_block, key_rot, precision=highest) * HEAD_DIM ** (-0.5)
    scores = low_back(scores)
    row_ids = offset + jnp.arange(span, dtype=jnp.int32)
    col_ids = jnp.arange(SEQ, dtype=jnp.int32)
    row_segs = lax.dynamic_slice_in_dim(segments, offset, span, 0)
    allowed = (row_segs[:, None] == segments[None, :]) & (col_ids[None, :] <= row_ids[:, None])
    scores = jnp.where(allowed, scores, masked_score)
    row_max = lax.optimization_barrier(jnp.max(scores, axis=-1, keepdims=True))
    powers = jnp.exp(scores - row_max)
    probs = low(powers / lax.optimization_barrier(jnp.sum(powers, axis=-1, keepdims=True)))
    mixed = jnp.einsum('kgqs,skd->qkgd', probs, value_rot, precision=highest)
    return mixed.reshape(span, HEADS * HEAD_DIM)

def forward(inputs, params, segments):
    attn_gain, w_query, w_key, w_value, query_gain, key_gain, w_output, ffn_gain, w_gate, w_up, w_down = params
    cosine, sine = rope_tables(segments)
    normed = low(rms_scale(inputs, attn_gain))
    query_lin = jnp.dot(normed, w_query, precision=highest)
    key_lin = jnp.dot(normed, w_key, precision=highest)
    value_lin = jnp.dot(normed, w_value, precision=highest)
    query = low(head_piece(low_back(query_lin), query_gain, cosine, sine))
    key_rot = low(head_piece(low_back(key_lin), key_gain, cosine, sine)).reshape(SEQ, KV_HEADS, HEAD_DIM)
    value_rot = low(low_back(value_lin)).reshape(SEQ, KV_HEADS, HEAD_DIM)
    span = min(512, SEQ)
    offsets = jnp.arange(SEQ // span, dtype=jnp.int32) * span
    step_fn = jax.checkpoint(attend)
    mixed = lax.map(lambda offset: step_fn(query, key_rot, value_rot, segments, offset), offsets)
    mixed = low(low_back(mixed.reshape(SEQ, HEADS * HEAD_DIM)))
    attn_out = low_back(jnp.dot(mixed, w_output.T, precision=highest))
    middle = inputs + attn_out
    normed_two = low(rms_scale(middle, ffn_gain))
    gate = low_back(jnp.dot(normed_two, w_gate, precision=highest))
    upper = low_back(jnp.dot(normed_two, w_up, precision=highest))
    hidden = low(jax.nn.silu(gate) * upper)
    return middle + jnp.dot(hidden, w_down.T, precision=highest)

def reference(inputs, cotangent, segment_ids, attn_gain, w_query, w_key, w_value, query_gain, key_gain, w_output, ffn_gain, w_gate, w_up, w_down):
    params = tuple((item.astype(jnp.float32) for item in (attn_gain, w_query, w_key, w_value, query_gain, key_gain, w_output, ffn_gain, w_gate, w_up, w_down)))
    input_rows = inputs.astype(jnp.float32).reshape(SEQS, SEQ, D)
    cot_rows = cotangent.astype(jnp.float32).reshape(SEQS, SEQ, D)
    seg_rows = segment_ids.reshape(SEQS, SEQ)

    def step(totals, item):
        input_row, cot_row, seg_row = item

        def single(first_arg, *rest):
            return forward(first_arg, rest, seg_row)
        result, back_fn = jax.vjp(single, input_row, *params)
        grads = back_fn(cot_row)
        totals = tuple((left + right for left, right in zip(totals, grads[1:])))
        return (totals, (result.astype(jnp.bfloat16), grads[0].astype(jnp.bfloat16)))
    zeros = tuple((jnp.zeros(item.shape, jnp.float32) for item in params))
    totals, (results, grad_rows) = lax.scan(step, zeros, (input_rows, cot_rows, seg_rows))
    return (results.reshape(TOKENS, D), grad_rows.reshape(TOKENS, D), totals[0], totals[1], totals[2], totals[3], totals[4], totals[5], totals[6], totals[7], totals[8], totals[9], totals[10])
```

```python
import jax
import jax.numpy as jnp
from jax import lax
from jax.sharding import PartitionSpec as P

HEAD_DIM = 64


epsilon = 1e-05
rope_base = 1000000.0
masked_score = -1e30


def rms_scale(values, scales):
    return values * lax.rsqrt(jnp.mean(values * values, axis=-1, keepdims=True) + epsilon) * scales


def rope_tables(segments):
    length = segments.shape[0]
    places = jnp.arange(length, dtype=jnp.int32)
    earlier = jnp.concatenate([segments[:1] - 1, segments[:-1]])
    starts = lax.cummax(jnp.where(segments != earlier, places, 0), axis=0)
    offsets = (places - starts).astype(jnp.float32)
    halves = HEAD_DIM // 2
    inverse = rope_base ** (-2.0 * jnp.arange(halves, dtype=jnp.float32) / HEAD_DIM)
    angles = offsets[:, None] * inverse[None, :]
    return (jnp.cos(angles), jnp.sin(angles))


def rotate(values, cosine, sine):
    halves = HEAD_DIM // 2
    first = values[..., :halves]
    second = values[..., halves:]
    cos_wide = cosine[:, None, :]
    sin_wide = sine[:, None, :]
    return jnp.concatenate(
        [first * cos_wide - second * sin_wide, second * cos_wide + first * sin_wide], axis=-1
    )


def head_piece(linear, scales, cosine, sine):
    row_count = linear.shape[0]
    head_count = linear.shape[1] // HEAD_DIM
    shaped = linear.reshape(row_count, head_count, HEAD_DIM)
    return rotate(rms_scale(shaped, scales), cosine, sine).reshape(row_count, head_count * HEAD_DIM)


def matmul(left, right):
    return jnp.dot(left, right, preferred_element_type=jnp.float32)


def matmul_bt(left, right):
    return lax.dot_general(
        left, right, (((1,), (1,)), ((), ())), preferred_element_type=jnp.float32
    )


def matmul_at(left, right):
    return lax.dot_general(
        left, right, (((0,), (0,)), ((), ())), preferred_element_type=jnp.float32
    )


def swap_add(values):
    pairs = [(0, 1), (1, 0)]
    return values + lax.ppermute(values, "tensor", pairs)


def bit_orders(bits):
    if bits == 4:
        return ((0, 1, 2, 3), (1, 2, 0, 3), (2, 0, 1, 3))
    names = tuple(range(bits))
    return tuple(names[turn % bits :] + names[: turn % bits] for turn in range(3))


def halving_scatter(values, order):
    devices = lax.axis_size("dp")
    me = lax.axis_index("dp")
    rows, columns = values.shape
    bits = len(order)
    addends = [values.reshape((2,) * bits + (rows // devices, columns))]
    left = list(range(bits - 1, -1, -1))
    for bit in order:
        axis = left.index(bit)
        mine = (me >> bit) & 1

        def take(array, which):
            return lax.dynamic_index_in_dim(array, which, axis, keepdims=False)

        send = sum(take(item, 1 - mine) for item in addends[1:]) + take(addends[0], 1 - mine)
        pairs = [(i, i ^ (1 << bit)) for i in range(devices)]
        received = lax.ppermute(send, "dp", pairs)
        addends = [take(item, mine) for item in addends] + [received]
        left.remove(bit)
    return sum(addends[1:]) + addends[0]


def cut_points(columns):
    tiles = columns // 128
    if tiles < 3:
        return [0, columns]
    one = -(-tiles // 3)
    return [0, one * 128, min(2 * one, tiles) * 128, columns] if 2 * one < tiles else [0, one * 128, columns]


def scatter_weight(values):
    devices = lax.axis_size("dp")
    orders = bit_orders(devices.bit_length() - 1)
    cuts = cut_points(values.shape[1])
    parts = [
        halving_scatter(values[:, low:high], orders[turn % 3])
        for turn, (low, high) in enumerate(zip(cuts[:-1], cuts[1:]))
    ]
    return jnp.concatenate(parts, axis=1)


def per_device(
    inputs,
    cotangent,
    segment_ids,
    attn_gain,
    w_query,
    w_key,
    w_value,
    query_gain,
    key_gain,
    w_output,
    ffn_gain,
    w_gate,
    w_up,
    w_down,
):
    seq_len = inputs.shape[0]
    span = min(512, seq_len)
    count = seq_len // span
    scale = HEAD_DIM ** (-0.5)
    head_count = w_query.shape[1] // HEAD_DIM
    kv_count = w_key.shape[1] // HEAD_DIM
    groups = head_count // kv_count
    input_full = inputs.astype(jnp.float32)
    normed, norm_back = jax.vjp(rms_scale, input_full, attn_gain)
    normed_b = normed.astype(jnp.bfloat16)
    query_lin = matmul(normed_b, w_query)
    key_lin = matmul(normed_b, w_key)
    value_lin = matmul(normed_b, w_value)
    cosine, sine = rope_tables(segment_ids)
    query_rot, query_back = jax.vjp(
        lambda linear, scales: head_piece(linear, scales, cosine, sine), query_lin, query_gain
    )
    key_rot, key_back = jax.vjp(
        lambda linear, scales: head_piece(linear, scales, cosine, sine), key_lin, key_gain
    )
    q_four = query_rot.astype(jnp.bfloat16).reshape(seq_len, kv_count, groups, HEAD_DIM)
    k_three = key_rot.astype(jnp.bfloat16).reshape(seq_len, kv_count, HEAD_DIM)
    v_three = value_lin.astype(jnp.bfloat16).reshape(seq_len, kv_count, HEAD_DIM)

    def scores_of(offset, finish):
        raw = (
            jnp.einsum(
                "qkgd,skd->kgqs",
                q_four[offset:finish],
                k_three[:finish],
                preferred_element_type=jnp.float32,
            )
            * scale
        )
        row_ids = offset + jnp.arange(finish - offset, dtype=jnp.int32)
        col_ids = jnp.arange(finish, dtype=jnp.int32)
        allowed = (segment_ids[offset:finish, None] == segment_ids[None, :finish]) & (
            col_ids[None, :] <= row_ids[:, None]
        )
        return jnp.where(allowed, raw, masked_score)

    pieces = []
    log_sums = []
    for number in range(count):
        offset = number * span
        finish = offset + span
        scores = scores_of(offset, finish)
        row_max = jnp.max(scores, axis=-1, keepdims=True)
        powers = jnp.exp(scores - row_max)
        totals = jnp.sum(powers, axis=-1, keepdims=True)
        probs = powers / totals
        log_sums.append(row_max + jnp.log(totals))
        mixed_part = jnp.einsum(
            "kgqs,skd->qkgd",
            probs.astype(jnp.bfloat16),
            v_three[:finish],
            preferred_element_type=jnp.float32,
        )
        pieces.append(mixed_part.reshape(span, head_count * HEAD_DIM))
    mixed_b = jnp.concatenate(pieces, axis=0).astype(jnp.bfloat16)
    attn_out = swap_add(matmul_bt(mixed_b, w_output))
    middle = input_full + attn_out
    normed_two, norm_two_back = jax.vjp(rms_scale, middle, ffn_gain)
    normed_two_b = normed_two.astype(jnp.bfloat16)
    gate = matmul(normed_two_b, w_gate)
    upper = matmul(normed_two_b, w_up)
    hidden, swish_back = jax.vjp(lambda left, right: jax.nn.silu(left) * right, gate, upper)
    hidden_b = hidden.astype(jnp.bfloat16)
    ffn_out = swap_add(matmul_bt(hidden_b, w_down))
    block_out = (middle + ffn_out).astype(jnp.bfloat16)
    grad_w_down = matmul_at(cotangent, hidden_b)
    grad_hidden = matmul(cotangent, w_down)
    grad_gate, grad_upper = swish_back(grad_hidden)
    grad_gate_b = grad_gate.astype(jnp.bfloat16)
    grad_upper_b = grad_upper.astype(jnp.bfloat16)
    grad_w_gate = matmul_at(normed_two_b, grad_gate_b)
    grad_w_up = matmul_at(normed_two_b, grad_upper_b)
    grad_normed_two = swap_add(
        matmul_bt(grad_gate_b, w_gate) + matmul_bt(grad_upper_b, w_up)
    )
    grad_from_two, grad_ffn_gain = norm_two_back(grad_normed_two)
    grad_middle = cotangent.astype(jnp.float32) + grad_from_two
    grad_branch = grad_middle.astype(jnp.bfloat16)
    grad_w_output = matmul_at(grad_branch, mixed_b)
    grad_mixed = matmul(grad_branch, w_output).astype(jnp.bfloat16)
    grad_four = grad_mixed.reshape(seq_len, kv_count, groups, HEAD_DIM)
    query_grads = []
    grad_keys = jnp.zeros((seq_len, kv_count, HEAD_DIM), jnp.float32)
    grad_values = jnp.zeros((seq_len, kv_count, HEAD_DIM), jnp.float32)
    for number in range(count):
        offset = number * span
        finish = offset + span
        scores = scores_of(offset, finish)
        probs = jnp.exp(scores - log_sums[number])
        grad_block = grad_four[offset:finish]
        grad_probs = jnp.einsum(
            "qkgd,skd->kgqs", grad_block, v_three[:finish], preferred_element_type=jnp.float32
        )
        center = jnp.sum(grad_probs * probs, axis=-1, keepdims=True)
        grad_scores = (probs * (grad_probs - center)).astype(jnp.bfloat16)
        query_part = (
            jnp.einsum(
                "kgqs,skd->qkgd", grad_scores, k_three[:finish], preferred_element_type=jnp.float32
            )
            * scale
        )
        query_grads.append(query_part.reshape(span, head_count * HEAD_DIM))
        key_part = (
            jnp.einsum(
                "kgqs,qkgd->skd",
                grad_scores,
                q_four[offset:finish],
                preferred_element_type=jnp.float32,
            )
            * scale
        )
        grad_keys = grad_keys.at[:finish].add(key_part)
        value_part = jnp.einsum(
            "kgqs,qkgd->skd",
            probs.astype(jnp.bfloat16),
            grad_block,
            preferred_element_type=jnp.float32,
        )
        grad_values = grad_values.at[:finish].add(value_part)
    grad_query_rot = jnp.concatenate(query_grads, axis=0)
    grad_query_lin, grad_query_gain = query_back(grad_query_rot)
    grad_key_lin, grad_key_gain = key_back(grad_keys.reshape(seq_len, kv_count * HEAD_DIM))
    grad_query_b = grad_query_lin.astype(jnp.bfloat16)
    grad_key_b = grad_key_lin.astype(jnp.bfloat16)
    grad_value_b = grad_values.reshape(seq_len, kv_count * HEAD_DIM).astype(jnp.bfloat16)
    grad_w_query = matmul_at(normed_b, grad_query_b)
    grad_w_key = matmul_at(normed_b, grad_key_b)
    grad_w_value = matmul_at(normed_b, grad_value_b)
    grad_normed = swap_add(
        matmul_bt(grad_query_b, w_query)
        + matmul_bt(grad_key_b, w_key)
        + matmul_bt(grad_value_b, w_value)
    )
    grad_from_one, grad_attn_gain = norm_back(grad_normed)
    grad_inputs = (grad_middle + grad_from_one).astype(jnp.bfloat16)
    gain_totals = lax.psum((grad_query_gain, grad_key_gain), ("dp", "tensor"))
    grad_three = jnp.concatenate([grad_w_query, grad_w_key, grad_w_value], axis=1)
    sum_down = scatter_weight(grad_w_down)
    sum_gate = scatter_weight(grad_w_gate)
    sum_up = scatter_weight(grad_w_up)
    sum_output = scatter_weight(grad_w_output)
    sum_three = scatter_weight(grad_three)
    q_width, k_width = w_query.shape[1], w_key.shape[1]
    sum_query = sum_three[:, :q_width]
    sum_key = sum_three[:, q_width : q_width + k_width]
    sum_value = sum_three[:, q_width + k_width :]
    sum_attn_gain = lax.psum_scatter(grad_attn_gain, "dp", scatter_dimension=0, tiled=True)
    sum_ffn_gain = lax.psum_scatter(grad_ffn_gain, "dp", scatter_dimension=0, tiled=True)
    return (
        block_out,
        grad_inputs,
        sum_attn_gain,
        sum_query,
        sum_key,
        sum_value,
        gain_totals[0],
        gain_totals[1],
        sum_output,
        sum_ffn_gain,
        sum_gate,
        sum_up,
        sum_down,
    )


def solution(mesh):
    placed = (
        P("dp", None),
        P("dp", None),
        P("dp"),
        P(),
        P(None, "tensor"),
        P(None, "tensor"),
        P(None, "tensor"),
        P(),
        P(),
        P(None, "tensor"),
        P(),
        P(None, "tensor"),
        P(None, "tensor"),
        P(None, "tensor"),
    )
    return jax.shard_map(
        per_device,
        mesh=mesh,
        in_specs=placed,
        out_specs=(
            P("dp", None),
            P("dp", None),
            P("dp"),
            P("dp", "tensor"),
            P("dp", "tensor"),
            P("dp", "tensor"),
            P(),
            P(),
            P("dp", "tensor"),
            P("dp"),
            P("dp", "tensor"),
            P("dp", "tensor"),
            P("dp", "tensor"),
        ),
        check_vma=False,
    )
```

```python
import functools

import jax
import jax.numpy as jnp
from jax import lax
from jax.experimental import pallas as pl
from jax.experimental.pallas import tpu as pltpu
from jax.sharding import PartitionSpec as P

HEAD_DIM = 64
LANES = 128
WINDOW = 512
BLOCK = 256
epsilon = 1e-05
rope_base = 1000000.0
masked_score = -1e30
f32 = jnp.float32
bf16 = jnp.bfloat16
NN = (((1,), (0,)), ((), ()))
NT = (((1,), (1,)), ((), ()))


def mm(left, right, dims=NN):
    return lax.dot_general(left, right, dims, preferred_element_type=f32)


def ones_by_head():
    row = lax.broadcasted_iota(jnp.int32, (LANES, LANES), 0)
    col = lax.broadcasted_iota(jnp.int32, (LANES, LANES), 1)
    return jnp.where((row >> 6) == (col >> 6), 1.0, 0.0).astype(bf16)


def head_sums(values, ones):
    high = values.astype(bf16)
    rest = (values - high.astype(f32)).astype(bf16)
    return mm(high, ones) + mm(rest, ones)


def swap_halves(values):
    lane = lax.broadcasted_iota(jnp.int32, values.shape, 1)
    return jnp.where((lane & 63) < 32, pltpu.roll(values, 96, 1), pltpu.roll(values, 32, 1))


def first_head(values):
    return lax.broadcasted_iota(jnp.int32, values.shape, 1) < 64


def stack_heads(pair):
    first = first_head(pair)
    zero = jnp.zeros_like(pair)
    return jnp.concatenate([jnp.where(first, pair, zero), jnp.where(first, zero, pair)], axis=0)


def pick_heads(stacked):
    rows = stacked.shape[0] // 2
    top = stacked[:rows]
    return jnp.where(first_head(top), top, stacked[rows:])


def column(row):
    return jnp.broadcast_to(row.astype(f32), (8, row.shape[1])).T[:, :1].astype(jnp.int32)


def twice(gain):
    return jnp.concatenate([gain, gain], axis=1)


def key_range(number):
    low = max(0, (number * BLOCK - (WINDOW - 1)) // BLOCK * BLOCK)
    return low, (number + 1) * BLOCK


def forward_kernel(
    x_ref, gain_ref, wq_ref, wk_ref, wv_ref, qg_ref, kg_ref, segr_ref, rate_ref, wo_ref,
    part_ref, normed_ref, lin_ref, q_ref, k_ref, v_ref, mixed_ref, cos_ref, sin_ref, bias_ref, segc_ref,
):
    rows = x_ref.shape[0]
    segc_ref[...] = column(segr_ref[...])
    query_gain, key_gain = twice(qg_ref[...]), twice(kg_ref[...])
    q_pairs = wq_ref.shape[1] // LANES
    k_pairs = wk_ref.shape[1] // LANES
    blocks = rows // BLOCK
    ones = ones_by_head()

    def project(step, carry):
        at = pl.ds(pl.multiple_of(step * BLOCK, BLOCK), BLOCK)
        x = x_ref[at, :].astype(f32)
        scale = lax.rsqrt(jnp.mean(x * x, axis=-1, keepdims=True) + epsilon)
        normed = (x * scale * gain_ref[...]).astype(bf16)
        normed_ref[at, :] = normed
        begins = jnp.sum((segr_ref[...] < segc_ref[at, :]).astype(f32), axis=-1, keepdims=True)
        places = (step * BLOCK + lax.broadcasted_iota(jnp.int32, (BLOCK, 1), 0)).astype(f32)
        angles = (places - begins) * rate_ref[...]
        lane = lax.broadcasted_iota(jnp.int32, angles.shape, 1)
        cosine, sine = jnp.cos(angles), jnp.sin(angles)
        sine = jnp.where((lane & 63) < 32, -sine, sine)
        cos_ref[at, :] = cosine
        sin_ref[at, :] = sine

        def rotated(linear, gain):
            unit = linear * lax.rsqrt(head_sums(linear * linear, ones) * (1.0 / HEAD_DIM) + epsilon)
            scaled = unit * gain
            return scaled * cosine + swap_halves(scaled) * sine

        queries = mm(normed, wq_ref[...])
        lin_ref[at, : q_pairs * LANES] = queries
        for pair in range(q_pairs):
            part = queries[:, pair * LANES : (pair + 1) * LANES]
            q_ref[pair, at, :] = (rotated(part, query_gain).astype(bf16).astype(f32) * HEAD_DIM**-0.5).astype(bf16)
        keys = mm(normed, wk_ref[...])
        lin_ref[at, q_pairs * LANES :] = keys
        values = mm(normed, wv_ref[...])
        for pair in range(k_pairs):
            part = slice(pair * LANES, (pair + 1) * LANES)
            for ref, both in ((k_ref, rotated(keys[:, part], key_gain)), (v_ref, values[:, part])):
                other = pltpu.roll(both, 64, 1)
                first = first_head(both)
                ref[2 * pair, at, :] = jnp.where(first, both, other).astype(bf16)
                ref[2 * pair + 1, at, :] = jnp.where(first, other, both).astype(bf16)
        return carry

    lax.fori_loop(0, blocks, project, 0)

    for number in range(blocks):
        low, high = key_range(number)
        at = slice(number * BLOCK, (number + 1) * BLOCK)
        span = high - low
        row_ids = number * BLOCK + lax.broadcasted_iota(jnp.int32, (BLOCK, span), 0)
        col_ids = low + lax.broadcasted_iota(jnp.int32, (BLOCK, span), 1)
        allowed = (segc_ref[at, :] == segr_ref[:, low:high]) & (col_ids <= row_ids)
        bias_ref[:, :span] = jnp.where(allowed, 0.0, masked_score)

        def head(pair, carry):
            stacked = stack_heads(q_ref[pair, at, :])
            scores = mm(stacked, k_ref[pair, low:high, :], NT)
            bias = bias_ref[:, :span]
            powers = jnp.exp(scores + jnp.concatenate([bias, bias], axis=0))
            totals = jnp.sum(powers, axis=-1, keepdims=True)
            probs = (powers * (1.0 / totals)).astype(bf16)
            mixed = pick_heads(mm(probs, v_ref[pair, low:high, :]))
            lanes = pl.ds(pl.multiple_of(pair * LANES, LANES), LANES)
            mixed_ref[at, lanes] = mixed.astype(bf16)
            return carry

        lax.fori_loop(0, q_pairs, head, 0)
        part_ref[at, :] = mm(mixed_ref[at, :], wo_ref[...], NT)


def backward_kernel(
    gb_ref, wo_ref, lin_ref, q_ref, k_ref, v_ref, qg_ref, kg_ref, cos_ref, sin_ref, segr_ref,
    gq_ref, gk_ref, gv_ref, gains_ref, bias_ref, gm_ref, dq_ref, dk_ref, dv_ref, segc_ref,
):
    rows = gb_ref.shape[0]
    segc_ref[...] = column(segr_ref[...])
    query_gain, key_gain = twice(qg_ref[...]), twice(kg_ref[...])
    q_pairs = q_ref.shape[0]
    k_pairs = q_pairs // 2
    blocks = rows // BLOCK
    ones = ones_by_head()

    for number in range(blocks):
        at = slice(number * BLOCK, (number + 1) * BLOCK)
        mixed = mm(gb_ref[at, :], wo_ref[...]).astype(bf16)
        for pair in range(q_pairs):
            gm_ref[pair, at, :] = mixed[:, pair * LANES : (pair + 1) * LANES]

    for number in reversed(range(blocks)):
        low, high = key_range(number)
        at = slice(number * BLOCK, (number + 1) * BLOCK)
        span = high - low
        key_ids = low + lax.broadcasted_iota(jnp.int32, (span, BLOCK), 0)
        row_ids = number * BLOCK + lax.broadcasted_iota(jnp.int32, (span, BLOCK), 1)
        allowed = (segc_ref[low:high, :] == segr_ref[:, at]) & (key_ids <= row_ids)
        bias_ref[:span, :] = jnp.where(allowed, 0.0, masked_score)
        fresh_from = 0 if number == blocks - 1 else key_range(number + 1)[0]

        def head(pair, carry):
            queries = stack_heads(q_ref[pair, at, :])
            grads = stack_heads(gm_ref[pair, at, :])
            keys = k_ref[pair, low:high, :]
            values = v_ref[pair, low:high, :]
            bias = bias_ref[:span, :]
            powers = jnp.exp(mm(keys, queries, NT) + jnp.concatenate([bias, bias], axis=1))
            probs = powers * (1.0 / jnp.sum(powers, axis=0, keepdims=True))
            grad_probs = mm(values, grads, NT)
            center = jnp.sum(grad_probs * probs, axis=0, keepdims=True)
            grad_scores = (probs * (grad_probs - center)).astype(bf16)
            dq = lax.dot_general(grad_scores, keys, (((0,), (0,)), ((), ())), preferred_element_type=f32)
            dq_ref[pair, at, :] = pick_heads(dq) * HEAD_DIM**-0.5
            dk = mm(grad_scores, queries)
            dv = mm(probs.astype(bf16), grads)
            if number == blocks - 1:
                dk_ref[pair, low:high, :] = dk
                dv_ref[pair, low:high, :] = dv
            else:
                if low < fresh_from:
                    dk_ref[pair, low:fresh_from, :] = dk[: fresh_from - low]
                    dv_ref[pair, low:fresh_from, :] = dv[: fresh_from - low]
                start = max(low, fresh_from)
                dk_ref[pair, start:high, :] += dk[start - low :]
                dv_ref[pair, start:high, :] += dv[start - low :]
            return carry

        lax.fori_loop(0, q_pairs, head, 0)

    gains_ref[...] = jnp.zeros_like(gains_ref)

    def finish(step, carry):
        at = pl.ds(pl.multiple_of(step * BLOCK, BLOCK), BLOCK)
        cosine, sine = cos_ref[at, :], sin_ref[at, :]

        def linear_grad(grad, linear, gain, row):
            scale = lax.rsqrt(head_sums(linear * linear, ones) * (1.0 / HEAD_DIM) + epsilon)
            unit = linear * scale
            turned = grad * cosine - swap_halves(grad) * sine
            gains_ref[row : row + 1, :] += jnp.sum(turned * unit, axis=0, keepdims=True)
            inner = turned * gain
            return (scale * (inner - unit * (head_sums(inner * unit, ones) * (1.0 / HEAD_DIM)))).astype(bf16)

        for pair in range(q_pairs):
            lanes = slice(pair * LANES, (pair + 1) * LANES)
            gq_ref[at, lanes] = linear_grad(dq_ref[pair, at, :], lin_ref[at, lanes], query_gain, 0)
        for pair in range(k_pairs):
            lanes = slice(pair * LANES, (pair + 1) * LANES)
            wide = slice((q_pairs + pair) * LANES, (q_pairs + pair + 1) * LANES)

            def both(ref):
                one, two = ref[2 * pair, at, :], ref[2 * pair + 1, at, :]
                one = one + pltpu.roll(one, 64, 1)
                two = two + pltpu.roll(two, 64, 1)
                return jnp.where(first_head(one), one, two)

            gk_ref[at, lanes] = linear_grad(both(dk_ref), lin_ref[at, wide], key_gain, 1)
            gv_ref[at, lanes] = both(dv_ref).astype(bf16)
        return carry

    lax.fori_loop(0, blocks, finish, 0)


PARAMS = pltpu.CompilerParams(vmem_limit_bytes=56 * 1024 * 1024)
COST = pl.CostEstimate(flops=1000, bytes_accessed=1000, transcendentals=0)


def call(kernel, outs, scratch, *operands):
    return pl.pallas_call(kernel, out_shape=outs, scratch_shapes=scratch, compiler_params=PARAMS, cost_estimate=COST)(*operands)


def attention_forward(inputs, attn_gain, w_query, w_key, w_value, query_gain, key_gain, segment_ids, w_output):
    rows, width = inputs.shape
    q_width, k_width = w_query.shape[1], w_key.shape[1]
    pairs = q_width // LANES
    shape = jax.ShapeDtypeStruct
    outs = (
        shape((rows, w_output.shape[0]), f32),
        shape((rows, width), bf16),
        shape((rows, q_width + k_width), f32),
        shape((pairs, rows, LANES), bf16),
        shape((pairs, rows, LANES), bf16),
        shape((pairs, rows, LANES), bf16),
        shape((rows, q_width), bf16),
        shape((rows, LANES), f32),
        shape((rows, LANES), f32),
    )
    span = min(rows, BLOCK + WINDOW)
    halves = HEAD_DIM // 2
    rates = rope_base ** (-2.0 * jnp.arange(halves, dtype=f32) / HEAD_DIM)
    return call(
        forward_kernel, outs, [pltpu.VMEM((BLOCK, span), f32), pltpu.VMEM((rows, 1), jnp.int32)],
        inputs, attn_gain[None, :], w_query, w_key, w_value, query_gain[None, :], key_gain[None, :],
        segment_ids[None, :], jnp.concatenate([rates] * 4)[None, :], w_output,
    )


def attention_backward(grad_branch, w_output, linear, query, key, value, query_gain, key_gain, tables, segment_ids):
    rows = grad_branch.shape[0]
    pairs = query.shape[0]
    q_width = pairs * LANES
    shape = jax.ShapeDtypeStruct
    outs = (
        shape((rows, q_width), bf16),
        shape((rows, q_width // 2), bf16),
        shape((rows, q_width // 2), bf16),
        shape((8, LANES), f32),
    )
    span = min(rows, BLOCK + WINDOW)
    scratch = [
        pltpu.VMEM((span, BLOCK), f32),
        pltpu.VMEM((pairs, rows, LANES), bf16),
        pltpu.VMEM((pairs, rows, LANES), f32),
        pltpu.VMEM((pairs, rows, LANES), f32),
        pltpu.VMEM((pairs, rows, LANES), f32),
        pltpu.VMEM((rows, 1), jnp.int32),
    ]
    return call(
        backward_kernel, outs, scratch,
        grad_branch, w_output, linear, query, key, value, query_gain[None, :], key_gain[None, :],
        *tables, segment_ids[None, :],
    )


def whole(shape):
    return pl.BlockSpec(shape, lambda step: (0,) * len(shape), pipeline_mode=pl.Buffered(1))


SMEM_SPEC = pl.BlockSpec(memory_space=pltpu.SMEM)
VMEM_SPEC = pl.BlockSpec(memory_space=pltpu.VMEM)


def gridded(kernel, steps, in_specs, out_specs, outs, operands, scratch=()):
    return pl.pallas_call(
        kernel,
        grid=(steps,),
        in_specs=in_specs,
        out_specs=out_specs,
        out_shape=outs,
        scratch_shapes=list(scratch),
        compiler_params=PARAMS,
        cost_estimate=COST,
    )(*operands)


def turn(values, places, scratch, out):
    groups = places.shape[0]
    each = scratch.shape[0] // groups
    turned = values.astype(f32).T
    for group in range(groups):
        place = pl.ds(pl.multiple_of(places[group], 8), each)
        scratch[place, :] = turned[group * each : (group + 1) * each]
    out[...] = scratch[...].astype(bf16)


def turn_kernel(places_ref, x_ref, out_ref, scratch):
    turn(x_ref[...], places_ref, scratch, out_ref)


def turned(values, places):
    rows, width = values.shape
    return gridded(
        turn_kernel, rows // BLOCK,
        [SMEM_SPEC, pl.BlockSpec((BLOCK, width), lambda step: (step, 0))],
        (pl.BlockSpec((width, BLOCK), lambda step: (0, step)),),
        (jax.ShapeDtypeStruct((width, rows), bf16),),
        (places, values), [pltpu.VMEM((width, BLOCK), f32)],
    )[0]


def middle_kernel(places_ref, x_ref, one_ref, two_ref, gain_ref, middle_ref, normed_ref, turned_ref, scratch):
    middle = x_ref[...].astype(f32) + (one_ref[...] + two_ref[...])
    scale = lax.rsqrt(jnp.mean(middle * middle, axis=-1, keepdims=True) + epsilon)
    normed = (middle * scale * gain_ref[...]).astype(bf16)
    middle_ref[...] = middle
    normed_ref[...] = normed
    turn(normed, places_ref, scratch, turned_ref)


def middle_norm(inputs, one, two, gain, places):
    rows, width = inputs.shape
    by_rows = pl.BlockSpec((BLOCK, width), lambda step: (step, 0))
    shape = jax.ShapeDtypeStruct
    return gridded(
        middle_kernel, rows // BLOCK,
        [SMEM_SPEC, by_rows, by_rows, by_rows, whole((1, width))],
        (by_rows, by_rows, pl.BlockSpec((width, BLOCK), lambda step: (0, step))),
        (shape((rows, width), f32), shape((rows, width), bf16), shape((width, rows), bf16)),
        (places, inputs, one, two, gain[None, :]), [pltpu.VMEM((width, BLOCK), f32)],
    )


def norm_back_kernel(value_ref, direct_ref, one_ref, two_ref, gain_ref, *out_refs):
    value = value_ref[...].astype(f32)
    grad = one_ref[...] + two_ref[...]
    scale = lax.rsqrt(jnp.mean(value * value, axis=-1, keepdims=True) + epsilon)
    unit = value * scale
    inner = grad * gain_ref[...]
    total = direct_ref[...].astype(f32) + scale * (inner - unit * jnp.mean(inner * unit, axis=-1, keepdims=True))
    for ref in out_refs[:-1]:
        ref[...] = total.astype(ref.dtype)
    gain_grad_ref = out_refs[-1]

    @pl.when(pl.program_id(0) == 0)
    def _():
        gain_grad_ref[...] = jnp.zeros_like(gain_grad_ref)

    gain_grad_ref[...] += jnp.sum(grad * unit, axis=0, keepdims=True)


def norm_back(value, direct, one, two, gain, types):
    rows, width = value.shape
    by_rows = pl.BlockSpec((BLOCK, width), lambda step: (step, 0))
    shape = jax.ShapeDtypeStruct
    return gridded(
        norm_back_kernel, rows // BLOCK,
        [by_rows] * 4 + [whole((1, width))],
        (by_rows,) * len(types) + (pl.BlockSpec((1, width), lambda step: (0, 0)),),
        tuple(shape((rows, width), kind) for kind in types) + (shape((1, width), f32),),
        (value, direct, one, two, gain[None, :]),
    )


def ffn_kernel(
    normed_ref, cot_ref, normed_t_ref, cot_t_ref, wg_ref, wu_ref, wd_ref,
    hidden_ref, gg_ref, gu_ref, pk_ref, ps_ref, qk_ref, qs_ref,
):
    half, block = qk_ref.shape
    gate = mm(normed_ref[...], wg_ref[...])
    upper = mm(normed_ref[...], wu_ref[...])
    grad = mm(cot_ref[...], wd_ref[...])
    share = 1.0 / (1.0 + jnp.exp(-gate))
    swish = gate * share
    hidden_ref[...] = (swish * upper).astype(bf16)
    gg_ref[...] = (grad * upper * (share * (1.0 + gate * (1.0 - share)))).astype(bf16)
    gu_ref[...] = (grad * swish).astype(bf16)
    qs_ref[...] = mm(cot_t_ref[half:, :], hidden_ref[...])
    ps_ref[:, :block] = mm(normed_t_ref[half:, :], gg_ref[...])
    ps_ref[:, block:] = mm(normed_t_ref[half:, :], gu_ref[...])
    qk_ref[...] = mm(cot_t_ref[:half, :], hidden_ref[...])
    pk_ref[:, :block] = mm(normed_t_ref[:half, :], gg_ref[...])
    pk_ref[:, block:] = mm(normed_t_ref[:half, :], gu_ref[...])


FBLOCK = 256


def units_kernel(normed_ref, cot_ref, wg_ref, wu_ref, wd_ref, hidden_ref, gg_ref, gu_ref):
    gate = mm(normed_ref[...], wg_ref[...])
    upper = mm(normed_ref[...], wu_ref[...])
    grad = mm(cot_ref[...], wd_ref[...])
    share = 1.0 / (1.0 + jnp.exp(-gate))
    swish = gate * share
    hidden_ref[...] = (swish * upper).astype(bf16)
    gg_ref[...] = (grad * upper * (share * (1.0 + gate * (1.0 - share)))).astype(bf16)
    gu_ref[...] = (grad * swish).astype(bf16)


def weights_kernel(
    normed_t_ref, cot_t_ref, hidden_ref, gg_ref, gu_ref, pk_ref, ps_ref, qk_ref, qs_ref,
):
    half, block = qk_ref.shape
    qs_ref[...] = mm(cot_t_ref[half:, :], hidden_ref[...])
    ps_ref[:, :block] = mm(normed_t_ref[half:, :], gg_ref[...])
    ps_ref[:, block:] = mm(normed_t_ref[half:, :], gu_ref[...])
    qk_ref[...] = mm(cot_t_ref[:half, :], hidden_ref[...])
    pk_ref[:, :block] = mm(normed_t_ref[:half, :], gg_ref[...])
    pk_ref[:, block:] = mm(normed_t_ref[:half, :], gu_ref[...])


def ffn_units(low, high, normed, cotangent, w_gate, w_up, w_down):
    rows, width = normed.shape
    base = low // FBLOCK
    units = pl.BlockSpec((rows, FBLOCK), lambda step: (0, step))
    weights = pl.BlockSpec((width, FBLOCK), lambda step: (0, base + step))
    return gridded(
        units_kernel, (high - low) // FBLOCK,
        [whole((rows, width))] * 2 + [weights] * 3,
        (units,) * 3,
        (jax.ShapeDtypeStruct((rows, high - low), bf16),) * 3,
        (normed, cotangent, w_gate, w_up, w_down),
    )


def ffn_weights(normed_t, cotangent_t, hidden, gg, gu):
    width, rows = normed_t.shape
    half = width // 2
    span = hidden.shape[1]
    shape = jax.ShapeDtypeStruct
    units = pl.BlockSpec((rows, FBLOCK), lambda step: (0, step))
    p_spec = pl.BlockSpec((half, 2 * FBLOCK), lambda step: (0, step))
    q_spec = pl.BlockSpec((half, FBLOCK), lambda step: (0, step))
    return gridded(
        weights_kernel, span // FBLOCK,
        [whole((width, rows))] * 2 + [units] * 3,
        (p_spec,) * 2 + (q_spec,) * 2,
        (shape((half, 2 * span), f32),) * 2 + (shape((half, span), f32),) * 2,
        (normed_t, cotangent_t, hidden, gg, gu),
    )


def ffn_part(low, high, normed, cotangent, normed_t, cotangent_t, w_gate, w_up, w_down):
    rows, width = normed.shape
    base = low // FBLOCK
    half = width // 2
    span = high - low
    shape = jax.ShapeDtypeStruct
    units = pl.BlockSpec((rows, FBLOCK), lambda step: (0, step))
    weights = pl.BlockSpec((width, FBLOCK), lambda step: (0, base + step))
    p_spec = pl.BlockSpec((half, 2 * FBLOCK), lambda step: (0, step))
    q_spec = pl.BlockSpec((half, FBLOCK), lambda step: (0, step))
    return gridded(
        ffn_kernel, span // FBLOCK,
        [whole((rows, width))] * 2 + [whole((width, rows))] * 2 + [weights] * 3,
        (units,) * 3 + (p_spec,) * 2 + (q_spec,) * 2,
        (shape((rows, span), bf16),) * 3 + (shape((half, 2 * span), f32),) * 2 + (shape((half, span), f32),) * 2,
        (normed, cotangent, normed_t, cotangent_t, w_gate, w_up, w_down),
    )


def products_kernel(starts, count, *refs):
    pieces = len(starts) - 1
    lefts = [refs[piece * count : (piece + 1) * count] for piece in range(pieces)]
    rights, out_ref = refs[pieces * count : (pieces + 1) * count], refs[(pieces + 1) * count]
    step = pl.program_id(0)
    columns = out_ref.shape[1]

    for piece in range(pieces):

        @pl.when((step >= starts[piece]) & (step < starts[piece + 1]))
        def _(piece=piece):
            def part(number, carry):
                at = pl.ds(pl.multiple_of(number * BLOCK, BLOCK), BLOCK)
                total = mm(lefts[piece][0][...], rights[0][at, :], NT)
                for left, right in zip(lefts[piece][1:], rights[1:]):
                    total += mm(left[...], right[at, :], NT)

                @pl.when(step == 0)
                def _():
                    out_ref[:, at] = total

                @pl.when(step > 0)
                def _():
                    out_ref[:, at] += total

                return carry

            lax.fori_loop(0, columns // BLOCK, part, 0)


def products(pieces, rights, block):
    count = len(rights)
    columns = rights[0].shape[0]
    rows = pieces[0][0].shape[0]
    starts = [0]
    left_specs = []
    for lefts in pieces:
        steps = lefts[0].shape[1] // block
        low = starts[-1]
        left_specs += [
            pl.BlockSpec((rows, block), lambda step, low=low, steps=steps: (0, jnp.clip(step - low, 0, steps - 1)))
        ] * count
        starts.append(low + steps)
    right_spec = pl.BlockSpec((columns, block), lambda step: (0, step))
    return gridded(
        functools.partial(products_kernel, tuple(starts), count), starts[-1],
        left_specs + [right_spec] * count,
        (pl.BlockSpec((rows, columns), lambda step: (0, 0)),),
        (jax.ShapeDtypeStruct((rows, columns), f32),),
        tuple(item for lefts in pieces for item in lefts) + tuple(rights),
    )[0]


def qkv_back_kernel(gq_ref, gk_ref, gv_ref, wq_ref, wk_ref, wv_ref, out_ref):
    def part(number, carry):
        at = pl.ds(pl.multiple_of(number * BLOCK, BLOCK), BLOCK)
        out_ref[:, at] = (
            mm(gq_ref[...], wq_ref[at, :], NT) + mm(gk_ref[...], wk_ref[at, :], NT) + mm(gv_ref[...], wv_ref[at, :], NT)
        )
        return carry

    lax.fori_loop(0, out_ref.shape[1] // BLOCK, part, 0)


def late_kernel(
    p_ref, q_ref, gb_ref, mixed_ref, normed_ref, gq_ref, gk_ref, gv_ref,
    pk_ref, ps_ref, qk_ref, qs_ref, scratch, turned_ref,
):
    half = pk_ref.shape[0]
    q_width, k_width = gq_ref.shape[1], gk_ref.shape[1]
    turn(normed_ref[...], p_ref, scratch, turned_ref)
    for ref, at in ((ps_ref, slice(half, 2 * half)), (pk_ref, slice(0, half))):
        ref[:, :q_width] = mm(turned_ref[at, :], gq_ref[...])
        ref[:, q_width : q_width + k_width] = mm(turned_ref[at, :], gk_ref[...])
        ref[:, q_width + k_width :] = mm(turned_ref[at, :], gv_ref[...])
    turn(gb_ref[...], q_ref, scratch, turned_ref)
    for ref, at in ((qs_ref, slice(half, 2 * half)), (qk_ref, slice(0, half))):
        ref[...] = mm(turned_ref[at, :], mixed_ref[...])


def late_weights(p_places, q_places, grad_branch, mixed, normed, gq, gk, gv):
    rows, width = normed.shape
    total = gq.shape[1] + 2 * gk.shape[1]
    half = width // 2
    shape = jax.ShapeDtypeStruct
    return pl.pallas_call(
        late_kernel,
        out_shape=(shape((half, total), f32),) * 2 + (shape((half, mixed.shape[1]), f32),) * 2,
        in_specs=[SMEM_SPEC] * 2 + [VMEM_SPEC] * 6,
        out_specs=(VMEM_SPEC,) * 4,
        scratch_shapes=[pltpu.VMEM((width, rows), f32), pltpu.VMEM((width, rows), bf16)],
        compiler_params=PARAMS,
        cost_estimate=COST,
    )(p_places, q_places, grad_branch, mixed, normed, gq, gk, gv)


def swap(values):
    return lax.ppermute(values, "tensor", [(0, 1), (1, 0)])


def physical(bit, core):
    return 1 - bit if core == 1 and bit < 2 else bit


class Layout:
    def __init__(self):
        self.devices = lax.axis_size("dp")
        self.bits = self.devices.bit_length() - 1
        me = lax.axis_index("dp")
        core = lax.axis_index("tensor")
        groups = jnp.arange(self.devices, dtype=jnp.int32)
        self.mine = self.label(me, core)
        self.numbers = self.label(groups, core)
        if self.bits == 4:
            self.p_order, self.q_order = (0, 1, 2, 3), (2, 0, 1, 3)
        else:
            self.p_order = tuple(range(self.bits))
            self.q_order = (2, 0, 1) + tuple(range(3, self.bits))

    def label(self, number, core):
        traded = (number & ~3) | ((number & 1) << 1) | ((number >> 1) & 1)
        return jnp.where(core == 1, traded, number).astype(jnp.int32)

    def bit(self, bit):
        return (self.mine >> bit) & 1

    def places(self, bit, each):
        which = ((self.numbers >> bit) & 1) ^ self.bit(bit)
        rest = ((self.numbers >> (bit + 1)) << bit) | (self.numbers & ((1 << bit) - 1))
        return (which * (self.devices // 2) + rest) * each

    def pairs(self, bit):
        return [
            (2 * i + core, 2 * (i ^ (1 << physical(bit, core))) + core) for i in range(self.devices) for core in range(2)
        ]


class Scatter:
    def __init__(self, layout, keep, send, order):
        self.layout = layout
        self.order = order
        self.left = [bit for bit in range(layout.bits - 1, -1, -1) if bit != order[0]]
        self.addends = [self.spread(keep)]
        self.send = self.spread(send)
        self.stage = 0

    def spread(self, values):
        groups = self.layout.devices // 2
        return values.reshape((2,) * (self.layout.bits - 1) + (values.shape[0] // groups, values.shape[1]))

    def exchange(self):
        self.addends.append(lax.ppermute(self.send, ("dp", "tensor"), self.layout.pairs(self.order[self.stage])))
        self.stage += 1

    def prepare(self):
        bit = self.order[self.stage]
        axis = self.left.index(bit)
        mine = self.layout.bit(bit)

        def take(array, which):
            return lax.dynamic_index_in_dim(array, which, axis, keepdims=False)

        self.send = functools.reduce(jnp.add, [take(item, 1 - mine) for item in self.addends])
        self.addends = [take(item, mine) for item in self.addends]
        self.left.remove(bit)

    def result(self):
        return functools.reduce(jnp.add, self.addends)


def after(values, earlier):
    if isinstance(earlier, list):
        earlier = [item.send for item in earlier]
    return lax.optimization_barrier((values, earlier))[0]


def exchange(group):
    for item in group:
        item.exchange()


def prepare(group, earlier=None):
    for item in group:
        if earlier is not None:
            item.addends[-1] = after(item.addends[-1], earlier)
        item.prepare()


def scatters(layout, halves):
    pk, ps, qk, qs = halves
    return [Scatter(layout, pk, ps, layout.p_order), Scatter(layout, qk, qs, layout.q_order)]


def hold(group, earlier):
    for item in group:
        item.send = after(item.send, earlier)


def per_device(
    inputs,
    cotangent,
    segment_ids,
    attn_gain,
    w_query,
    w_key,
    w_value,
    query_gain,
    key_gain,
    w_output,
    ffn_gain,
    w_gate,
    w_up,
    w_down,
):
    width = inputs.shape[1]
    units = w_gate.shape[1]
    layout = Layout()
    devices, bits = layout.devices, layout.bits
    each = width // devices
    me = lax.axis_index("dp")
    p_places = layout.places(layout.p_order[0], each)
    q_places = layout.places(layout.q_order[0], each)

    part, normed, linear, query, key, value, mixed, *tables = attention_forward(
        inputs, attn_gain, w_query, w_key, w_value, query_gain, key_gain, segment_ids, w_output
    )
    part_swapped = swap(part)
    cotangent_t = turned(after(cotangent, normed), q_places)
    part = after(part, cotangent_t)
    middle, normed_two, normed_two_t = middle_norm(inputs, part, part_swapped, ffn_gain, p_places)

    cut = (units // FBLOCK * 4 // 9) * FBLOCK
    block = FBLOCK
    one = ffn_part(0, cut, normed_two, cotangent, normed_two_t, cotangent_t, w_gate, w_up, w_down)
    early = scatters(layout, one[3:])
    exchange(early)
    two = ffn_units(cut, units, after(normed_two, early), cotangent, w_gate, w_up, w_down)
    grad_two = products([one[1:3], two[1:3]], (w_gate, w_up), block)
    grad_two_swapped = swap(grad_two)
    main = scatters(layout, ffn_weights(after(normed_two_t, grad_two), cotangent_t, *two))
    prepare(early, main)
    exchange(early)
    hold(main, early)
    exchange(main)
    grad_middle, grad_branch, grad_ffn_gain = norm_back(
        after(middle, main), cotangent, grad_two, grad_two_swapped, ffn_gain, (f32, bf16)
    )
    gq, gk, gv, gains = attention_backward(
        grad_branch, w_output, linear, query, key, value, query_gain, key_gain, tables, segment_ids
    )
    last = scatters(layout, late_weights(p_places, q_places, grad_branch, mixed, normed, gq, gk, gv))
    prepare(early, last)
    exchange(early)
    grad_one = call(
        qkv_back_kernel, jax.ShapeDtypeStruct(inputs.shape, f32), [], after(gq, early), gk, gv, w_query, w_key, w_value
    )
    prepare(main[1:], grad_one)
    exchange(main[1:])
    hold(last, main[1:])
    exchange(last)
    prepare(main[:1], last)
    exchange(main[:1])
    grad_one_swapped = swap(after(grad_one, main[:1]))
    prepare(early, main[:1])
    exchange(early)
    grad_inputs, grad_attn_gain = norm_back(
        inputs, after(grad_middle, early), grad_one, grad_one_swapped, attn_gain, (bf16,)
    )
    ffn = products([one[:1], after(two[:1], grad_inputs)], (w_down,), block)
    ffn_swapped = swap(ffn)
    small = jnp.concatenate(
        [
            grad_attn_gain.reshape(-1, LANES) * 0.5,
            grad_ffn_gain.reshape(-1, LANES) * 0.5,
            jnp.pad(gains[:2, :HEAD_DIM] + gains[:2, HEAD_DIM:], ((0, 6), (0, LANES - HEAD_DIM))),
        ]
    )
    small = small + swap(small)
    small = small + lax.ppermute(small, ("dp", "tensor"), layout.pairs(0))
    prepare(main[1:], ffn)
    exchange(main[1:])
    prepare(last, main[1:])
    exchange(last)
    prepare(main[:1], last)
    exchange(main[:1])
    block_out = (middle + (after(ffn, main[:1]) + ffn_swapped)).astype(bf16)
    for bit in range(1, bits):
        small = small + lax.ppermute(small, ("dp", "tensor"), layout.pairs(bit))
    while early[0].stage < bits:
        prepare(early)
        exchange(early)
    while main[0].stage < bits:
        prepare(main)
        exchange(main)
    while last[0].stage < bits:
        prepare(last)
        exchange(last)
    sum_early = [item.result() for item in early]
    sum_main = [item.result() for item in main]
    sum_last = [item.result() for item in last]
    lines = width // LANES
    sum_attn_gain = lax.dynamic_slice_in_dim(small[:lines].reshape(width), me * each, each)
    sum_ffn_gain = lax.dynamic_slice_in_dim(small[lines : 2 * lines].reshape(width), me * each, each)

    blocks = jnp.concatenate([sum_early[0], sum_main[0]], axis=1).reshape(each, units // FBLOCK, 2, FBLOCK)
    q_width, k_width = w_query.shape[1], w_key.shape[1]
    return (
        block_out,
        grad_inputs,
        sum_attn_gain,
        sum_last[0][:, :q_width],
        sum_last[0][:, q_width : q_width + k_width],
        sum_last[0][:, q_width + k_width :],
        small[2 * lines, :HEAD_DIM],
        small[2 * lines + 1, :HEAD_DIM],
        sum_last[1],
        sum_ffn_gain,
        blocks[:, :, 0].reshape(each, units),
        blocks[:, :, 1].reshape(each, units),
        jnp.concatenate([sum_early[1], sum_main[1]], axis=1),
    )


def solution(mesh):
    placed = (
        P("dp", None),
        P("dp", None),
        P("dp"),
        P(),
        P(None, "tensor"),
        P(None, "tensor"),
        P(None, "tensor"),
        P(),
        P(),
        P(None, "tensor"),
        P(),
        P(None, "tensor"),
        P(None, "tensor"),
        P(None, "tensor"),
    )
    return jax.shard_map(
        per_device,
        mesh=mesh,
        in_specs=placed,
        out_specs=(
            P("dp", None),
            P("dp", None),
            P("dp"),
            P("dp", "tensor"),
            P("dp", "tensor"),
            P("dp", "tensor"),
            P(),
            P(),
            P("dp", "tensor"),
            P("dp"),
            P("dp", "tensor"),
            P("dp", "tensor"),
            P("dp", "tensor"),
        ),
        check_vma=False,
    )
```

```python
import functools

import jax
import jax.numpy as jnp
from jax import lax
from jax.experimental import pallas as pl
from jax.experimental.pallas import tpu as pltpu
from jax.sharding import PartitionSpec as P

HEAD_DIM = 64
LANES = 128
WINDOW = 512
BLOCK = 256
epsilon = 1e-05
rope_base = 1000000.0
masked_score = -1e30
f32 = jnp.float32
bf16 = jnp.bfloat16
NN = (((1,), (0,)), ((), ()))
NT = (((1,), (1,)), ((), ()))


def mm(left, right, dims=NN):
    return lax.dot_general(left, right, dims, preferred_element_type=f32)


def ones_by_head():
    row = lax.broadcasted_iota(jnp.int32, (LANES, LANES), 0)
    col = lax.broadcasted_iota(jnp.int32, (LANES, LANES), 1)
    return jnp.where((row >> 6) == (col >> 6), 1.0, 0.0).astype(bf16)


def head_sums(values, ones):
    high = values.astype(bf16)
    rest = (values - high.astype(f32)).astype(bf16)
    return mm(high, ones) + mm(rest, ones)


def swap_halves(values):
    lane = lax.broadcasted_iota(jnp.int32, values.shape, 1)
    return jnp.where((lane & 63) < 32, pltpu.roll(values, 96, 1), pltpu.roll(values, 32, 1))


def first_head(values):
    return lax.broadcasted_iota(jnp.int32, values.shape, 1) < 64


def stack_heads(pair):
    first = first_head(pair)
    zero = jnp.zeros_like(pair)
    return jnp.concatenate([jnp.where(first, pair, zero), jnp.where(first, zero, pair)], axis=0)


def pick_heads(stacked):
    rows = stacked.shape[0] // 2
    top = stacked[:rows]
    return jnp.where(first_head(top), top, stacked[rows:])


def column(row):
    return jnp.broadcast_to(row.astype(f32), (8, row.shape[1])).T[:, :1].astype(jnp.int32)


def twice(gain):
    return jnp.concatenate([gain, gain], axis=1)


def key_range(number):
    low = max(0, (number * BLOCK - (WINDOW - 1)) // BLOCK * BLOCK)
    return low, (number + 1) * BLOCK


def forward_kernel(
    x_ref, gain_ref, wq_ref, wk_ref, wv_ref, qg_ref, kg_ref, segr_ref, rate_ref, wo_ref,
    upper_ref, lower_ref, normed_ref, lin_ref, q_ref, k_ref, v_ref, mixed_ref, cos_ref, sin_ref, bias_ref, segc_ref,
):
    rows = x_ref.shape[0]
    segc_ref[...] = column(segr_ref[...])
    query_gain, key_gain = twice(qg_ref[...]), twice(kg_ref[...])
    q_pairs = wq_ref.shape[1] // LANES
    k_pairs = wk_ref.shape[1] // LANES
    blocks = rows // BLOCK
    ones = ones_by_head()

    def project(step, carry):
        at = pl.ds(pl.multiple_of(step * BLOCK, BLOCK), BLOCK)
        x = x_ref[at, :].astype(f32)
        scale = lax.rsqrt(jnp.mean(x * x, axis=-1, keepdims=True) + epsilon)
        normed = (x * scale * gain_ref[...]).astype(bf16)
        normed_ref[at, :] = normed
        begins = jnp.sum((segr_ref[...] < segc_ref[at, :]).astype(f32), axis=-1, keepdims=True)
        places = (step * BLOCK + lax.broadcasted_iota(jnp.int32, (BLOCK, 1), 0)).astype(f32)
        angles = (places - begins) * rate_ref[...]
        lane = lax.broadcasted_iota(jnp.int32, angles.shape, 1)
        cosine, sine = jnp.cos(angles), jnp.sin(angles)
        sine = jnp.where((lane & 63) < 32, -sine, sine)
        cos_ref[at, :] = cosine
        sin_ref[at, :] = sine

        def rotated(linear, gain):
            unit = linear * lax.rsqrt(head_sums(linear * linear, ones) * (1.0 / HEAD_DIM) + epsilon)
            scaled = unit * gain
            return scaled * cosine + swap_halves(scaled) * sine

        queries = mm(normed, wq_ref[...])
        lin_ref[at, : q_pairs * LANES] = queries
        for pair in range(q_pairs):
            part = queries[:, pair * LANES : (pair + 1) * LANES]
            q_ref[pair, at, :] = (rotated(part, query_gain).astype(bf16).astype(f32) * HEAD_DIM**-0.5).astype(bf16)
        keys = mm(normed, wk_ref[...])
        lin_ref[at, q_pairs * LANES :] = keys
        values = mm(normed, wv_ref[...])
        for pair in range(k_pairs):
            part = slice(pair * LANES, (pair + 1) * LANES)
            for ref, both in ((k_ref, rotated(keys[:, part], key_gain)), (v_ref, values[:, part])):
                other = pltpu.roll(both, 64, 1)
                first = first_head(both)
                ref[2 * pair, at, :] = jnp.where(first, both, other).astype(bf16)
                ref[2 * pair + 1, at, :] = jnp.where(first, other, both).astype(bf16)
        return carry

    lax.fori_loop(0, blocks, project, 0)

    for number in range(blocks):
        low, high = key_range(number)
        at = slice(number * BLOCK, (number + 1) * BLOCK)
        span = high - low
        row_ids = number * BLOCK + lax.broadcasted_iota(jnp.int32, (BLOCK, span), 0)
        col_ids = low + lax.broadcasted_iota(jnp.int32, (BLOCK, span), 1)
        allowed = (segc_ref[at, :] == segr_ref[:, low:high]) & (col_ids <= row_ids)
        bias_ref[:, :span] = jnp.where(allowed, 0.0, masked_score)

        def head(pair, carry):
            stacked = stack_heads(q_ref[pair, at, :])
            scores = mm(stacked, k_ref[pair, low:high, :], NT)
            bias = bias_ref[:, :span]
            powers = jnp.exp(scores + jnp.concatenate([bias, bias], axis=0))
            totals = jnp.sum(powers, axis=-1, keepdims=True)
            probs = (powers * (1.0 / totals)).astype(bf16)
            mixed = pick_heads(mm(probs, v_ref[pair, low:high, :]))
            lanes = pl.ds(pl.multiple_of(pair * LANES, LANES), LANES)
            mixed_ref[at, lanes] = mixed.astype(bf16)
            return carry

        lax.fori_loop(0, q_pairs, head, 0)
        half = upper_ref.shape[0]
        part_ref = upper_ref if number * BLOCK < half else lower_ref
        part_ref[number * BLOCK % half : number * BLOCK % half + BLOCK, :] = mm(mixed_ref[at, :], wo_ref[...], NT)


def backward_kernel(
    gb_ref, wo_ref, q_lin_ref, k_lin_ref, q_ref, k_ref, v_ref, qg_ref, kg_ref, cos_ref, sin_ref, segr_ref,
    gq_ref, gk_ref, gv_ref, gains_ref, bias_ref, gm_ref, dq_ref, dk_ref, dv_ref, segc_ref,
):
    rows = gb_ref.shape[0]
    segc_ref[...] = column(segr_ref[...])
    query_gain, key_gain = twice(qg_ref[...]), twice(kg_ref[...])
    q_pairs = q_ref.shape[0]
    k_pairs = q_pairs // 2
    blocks = rows // BLOCK
    ones = ones_by_head()

    for number in range(blocks):
        at = slice(number * BLOCK, (number + 1) * BLOCK)
        mixed = mm(gb_ref[at, :], wo_ref[...]).astype(bf16)
        for pair in range(q_pairs):
            gm_ref[pair, at, :] = mixed[:, pair * LANES : (pair + 1) * LANES]

    for number in reversed(range(blocks)):
        low, high = key_range(number)
        at = slice(number * BLOCK, (number + 1) * BLOCK)
        span = high - low
        key_ids = low + lax.broadcasted_iota(jnp.int32, (span, BLOCK), 0)
        row_ids = number * BLOCK + lax.broadcasted_iota(jnp.int32, (span, BLOCK), 1)
        allowed = (segc_ref[low:high, :] == segr_ref[:, at]) & (key_ids <= row_ids)
        bias_ref[:span, :] = jnp.where(allowed, 0.0, masked_score)
        fresh_from = 0 if number == blocks - 1 else key_range(number + 1)[0]

        def head(pair, carry):
            queries = stack_heads(q_ref[pair, at, :])
            grads = stack_heads(gm_ref[pair, at, :])
            keys = k_ref[pair, low:high, :]
            values = v_ref[pair, low:high, :]
            bias = bias_ref[:span, :]
            powers = jnp.exp(mm(keys, queries, NT) + jnp.concatenate([bias, bias], axis=1))
            probs = powers * (1.0 / jnp.sum(powers, axis=0, keepdims=True))
            grad_probs = mm(values, grads, NT)
            center = jnp.sum(grad_probs * probs, axis=0, keepdims=True)
            grad_scores = (probs * (grad_probs - center)).astype(bf16)
            dq = lax.dot_general(grad_scores, keys, (((0,), (0,)), ((), ())), preferred_element_type=f32)
            dq_ref[pair, at, :] = pick_heads(dq) * HEAD_DIM**-0.5
            dk = mm(grad_scores, queries)
            dv = mm(probs.astype(bf16), grads)
            if number == blocks - 1:
                dk_ref[pair, low:high, :] = dk
                dv_ref[pair, low:high, :] = dv
            else:
                if low < fresh_from:
                    dk_ref[pair, low:fresh_from, :] = dk[: fresh_from - low]
                    dv_ref[pair, low:fresh_from, :] = dv[: fresh_from - low]
                start = max(low, fresh_from)
                dk_ref[pair, start:high, :] += dk[start - low :]
                dv_ref[pair, start:high, :] += dv[start - low :]
            return carry

        lax.fori_loop(0, q_pairs, head, 0)

    gains_ref[...] = jnp.zeros_like(gains_ref)

    def finish(step, carry):
        at = pl.ds(pl.multiple_of(step * BLOCK, BLOCK), BLOCK)
        cosine, sine = cos_ref[at, :], sin_ref[at, :]

        def linear_grad(grad, linear, gain, row):
            scale = lax.rsqrt(head_sums(linear * linear, ones) * (1.0 / HEAD_DIM) + epsilon)
            unit = linear * scale
            turned = grad * cosine - swap_halves(grad) * sine
            gains_ref[row : row + 1, :] += jnp.sum(turned * unit, axis=0, keepdims=True)
            inner = turned * gain
            return (scale * (inner - unit * (head_sums(inner * unit, ones) * (1.0 / HEAD_DIM)))).astype(bf16)

        for pair in range(q_pairs):
            lanes = slice(pair * LANES, (pair + 1) * LANES)
            gq_ref[at, lanes] = linear_grad(dq_ref[pair, at, :], q_lin_ref[at, lanes], query_gain, 0)
        for pair in range(k_pairs):
            lanes = slice(pair * LANES, (pair + 1) * LANES)

            def both(ref):
                one, two = ref[2 * pair, at, :], ref[2 * pair + 1, at, :]
                one = one + pltpu.roll(one, 64, 1)
                two = two + pltpu.roll(two, 64, 1)
                return jnp.where(first_head(one), one, two)

            gk_ref[at, lanes] = linear_grad(both(dk_ref), k_lin_ref[at, lanes], key_gain, 1)
            gv_ref[at, lanes] = both(dv_ref).astype(bf16)
        return carry

    lax.fori_loop(0, blocks, finish, 0)


PARAMS = pltpu.CompilerParams(vmem_limit_bytes=56 * 1024 * 1024)
SHARE = 1.0


def cost(time):
    return pl.CostEstimate(flops=int(time * SHARE * 1e9) + 1000, bytes_accessed=1000, transcendentals=0)


def call(kernel, outs, scratch, *operands):
    return pl.pallas_call(
        kernel, out_shape=outs, scratch_shapes=scratch, compiler_params=PARAMS, cost_estimate=cost(30)
    )(*operands)


def attention_forward(inputs, attn_gain, w_query, w_key, w_value, query_gain, key_gain, segment_ids, w_output):
    rows, width = inputs.shape
    q_width, k_width = w_query.shape[1], w_key.shape[1]
    pairs = q_width // LANES
    shape = jax.ShapeDtypeStruct
    outs = (
        shape((rows // 2, w_output.shape[0]), f32),
        shape((rows // 2, w_output.shape[0]), f32),
        shape((rows, width), bf16),
        shape((rows, q_width + k_width), f32),
        shape((pairs, rows, LANES), bf16),
        shape((pairs, rows, LANES), bf16),
        shape((pairs, rows, LANES), bf16),
        shape((rows, q_width), bf16),
        shape((rows, LANES), f32),
        shape((rows, LANES), f32),
    )
    span = min(rows, BLOCK + WINDOW)
    halves = HEAD_DIM // 2
    rates = rope_base ** (-2.0 * jnp.arange(halves, dtype=f32) / HEAD_DIM)
    return call(
        forward_kernel, outs, [pltpu.VMEM((BLOCK, span), f32), pltpu.VMEM((rows, 1), jnp.int32)],
        inputs, attn_gain[None, :], w_query, w_key, w_value, query_gain[None, :], key_gain[None, :],
        segment_ids[None, :], jnp.concatenate([rates] * 4)[None, :], w_output,
    )


def attention_backward(
    k_pair, grad_branch, w_output, linear, query, key, value, query_gain, key_gain, tables, segment_ids
):
    rows, width = grad_branch.shape
    shape = jax.ShapeDtypeStruct
    outs = (
        shape((rows, 2 * LANES), bf16),
        shape((rows, LANES), bf16),
        shape((rows, LANES), bf16),
        shape((8, LANES), f32),
    )
    span = min(rows, BLOCK + WINDOW)
    scratch = [
        pltpu.VMEM((span, BLOCK), f32),
        pltpu.VMEM((2, rows, LANES), bf16),
        pltpu.VMEM((2, rows, LANES), f32),
        pltpu.VMEM((2, rows, LANES), f32),
        pltpu.VMEM((2, rows, LANES), f32),
        pltpu.VMEM((rows, 1), jnp.int32),
    ]
    heads = query.shape[0]

    def fixed(block, *place):
        return pl.BlockSpec(block, lambda step: place, pipeline_mode=pl.Buffered(1))

    pairs = fixed((2, rows, LANES), k_pair, 0, 0)
    small = fixed((1, HEAD_DIM), 0, 0)
    table = fixed((rows, LANES), 0, 0)
    return pl.pallas_call(
        backward_kernel,
        grid=(1,),
        in_specs=[
            fixed((rows, width), 0, 0), fixed((width, 2 * LANES), 0, k_pair),
            fixed((rows, 2 * LANES), 0, k_pair), fixed((rows, LANES), 0, heads + k_pair),
            pairs, pairs, pairs, small, small, table, table, fixed((1, rows), 0, 0),
        ],
        out_specs=tuple(fixed(item.shape, 0, 0) for item in outs),
        out_shape=outs,
        scratch_shapes=scratch,
        compiler_params=PARAMS,
        cost_estimate=cost(18),
    )(
        grad_branch, w_output, linear, linear, query, key, value, query_gain[None, :], key_gain[None, :],
        *tables, segment_ids[None, :],
    )


def whole(shape):
    return pl.BlockSpec(shape, lambda step: (0,) * len(shape), pipeline_mode=pl.Buffered(1))


SMEM_SPEC = pl.BlockSpec(memory_space=pltpu.SMEM)
VMEM_SPEC = pl.BlockSpec(memory_space=pltpu.VMEM)


def gridded(time, kernel, steps, in_specs, out_specs, outs, operands, scratch=()):
    return pl.pallas_call(
        kernel,
        grid=(steps,),
        in_specs=in_specs,
        out_specs=out_specs,
        out_shape=outs,
        scratch_shapes=list(scratch),
        compiler_params=PARAMS,
        cost_estimate=cost(time),
    )(*operands)


def turn(values, places, scratch, out):
    groups = places.shape[0]
    each = scratch.shape[0] // groups
    turned = values.astype(f32).T
    for group in range(groups):
        place = pl.ds(pl.multiple_of(places[group], 8), each)
        scratch[place, :] = turned[group * each : (group + 1) * each]
    out[...] = scratch[: out.shape[0], :].astype(bf16)


def widen_kernel(x_ref, out_ref):
    out_ref[...] = x_ref[...].astype(f32)


def widened(values):
    rows, width = values.shape
    by_rows = pl.BlockSpec((BLOCK, width), lambda step: (step, 0))
    return gridded(
        4, widen_kernel, rows // BLOCK, [by_rows], (by_rows,), (jax.ShapeDtypeStruct((rows, width), f32),), (values,)
    )[0]


def turn_kernel(places_ref, x_ref, *refs):
    *narrow_refs, out_ref, scratch = refs
    for ref in narrow_refs:
        ref[...] = x_ref[...].astype(bf16)
    turn(x_ref[...], places_ref, scratch, out_ref)


def turned(values, places, narrow=False):
    rows, width = values.shape
    shape = jax.ShapeDtypeStruct
    by_rows = pl.BlockSpec((BLOCK, width), lambda step: (step, 0))
    outs = ((by_rows,), (shape((rows, width), bf16),)) if narrow else ((), ())
    return gridded(
        4, turn_kernel, rows // BLOCK,
        [SMEM_SPEC, by_rows],
        outs[0] + (pl.BlockSpec((width // 2, BLOCK), lambda step: (0, step)),),
        outs[1] + (shape((width // 2, rows), bf16),),
        (places, values), [pltpu.VMEM((width, BLOCK), f32)],
    )


def of_halves(refs):
    if len(refs) == 2:
        return refs[0][...] + refs[1][...]
    early = pl.program_id(0) < pl.num_programs(0) // 2
    return jnp.where(early, refs[0][...] + refs[2][...], refs[1][...] + refs[3][...])


def half_specs(pieces, rows, width):
    steps = rows // BLOCK
    if pieces == 2:
        return [pl.BlockSpec((BLOCK, width), lambda step: (step, 0))] * 2
    upper = pl.BlockSpec((BLOCK, width), lambda step: (jnp.minimum(step, steps // 2 - 1), 0))
    lower = pl.BlockSpec((BLOCK, width), lambda step: (jnp.maximum(step - steps // 2, 0), 0))
    return [upper, lower, upper, lower]


def middle_kernel(x_ref, *refs):
    gain_ref, middle_ref, normed_ref, wide_ref = refs[-4:]
    middle = x_ref[...].astype(f32) + of_halves(refs[:-4])
    scale = lax.rsqrt(jnp.mean(middle * middle, axis=-1, keepdims=True) + epsilon)
    normed = (middle * scale * gain_ref[...]).astype(bf16)
    middle_ref[...] = middle
    normed_ref[...] = normed
    wide_ref[...] = normed.astype(f32)


def middle_norm(inputs, one, two, gain):
    rows, width = inputs.shape
    by_rows = pl.BlockSpec((BLOCK, width), lambda step: (step, 0))
    shape = jax.ShapeDtypeStruct
    return gridded(
        10, middle_kernel, rows // BLOCK,
        [by_rows] + half_specs(len(one) + len(two), rows, width) + [whole((1, width))],
        (by_rows,) * 3,
        (shape((rows, width), f32), shape((rows, width), bf16), shape((rows, width), f32)),
        (inputs, *one, *two, gain[None, :]),
    )


def norm_back_kernel(parts, value_ref, direct_ref, *refs):
    grad = of_halves(refs[:parts])
    gain_ref, *out_refs, gain_grad_ref = refs[parts:]
    value = value_ref[...].astype(f32)
    scale = lax.rsqrt(jnp.mean(value * value, axis=-1, keepdims=True) + epsilon)
    unit = value * scale
    inner = grad * gain_ref[...]
    total = direct_ref[...].astype(f32) + scale * (inner - unit * jnp.mean(inner * unit, axis=-1, keepdims=True))
    for ref in out_refs:
        ref[...] = total.astype(ref.dtype)

    @pl.when(pl.program_id(0) == 0)
    def _():
        gain_grad_ref[...] = jnp.zeros_like(gain_grad_ref)

    gain_grad_ref[...] += jnp.sum(grad * unit, axis=0, keepdims=True)


def norm_back(value, direct, one, two, gain, types):
    rows, width = value.shape
    steps = rows // BLOCK
    by_rows = pl.BlockSpec((BLOCK, width), lambda step: (step, 0))
    shape = jax.ShapeDtypeStruct
    return gridded(
        9, functools.partial(norm_back_kernel, len(one) + len(two)), steps,
        [by_rows, by_rows] + half_specs(len(one) + len(two), rows, width) + [whole((1, width))],
        (by_rows,) * len(types) + (pl.BlockSpec((1, width), lambda step: (0, 0)),),
        tuple(shape((rows, width), kind) for kind in types) + (shape((1, width), f32),),
        (value, direct, *one, *two, gain[None, :]),
    )


FBLOCK = 256


def unit_gradients(normed, cotangent, wg_ref, wu_ref, wd_ref):
    gate = mm(normed, wg_ref[...])
    upper = mm(normed, wu_ref[...])
    grad = mm(cotangent, wd_ref[...])
    share = 0.5 * jnp.tanh(0.5 * gate) + 0.5
    swish = gate * share
    return (
        (swish * upper).astype(bf16),
        (grad * upper * (share + swish * (1.0 - share))).astype(bf16),
        (grad * swish).astype(bf16),
    )


def units_kernel(normed_ref, cot_ref, wg_ref, wu_ref, wd_ref, hidden_ref, gg_ref, gu_ref):
    hidden_ref[...], gg_ref[...], gu_ref[...] = unit_gradients(normed_ref[...], cot_ref[...], wg_ref, wu_ref, wd_ref)


def ffn_units(normed, cotangent, w_gate, w_up, w_down):
    rows, width = normed.shape
    total = w_gate.shape[1]
    units = pl.BlockSpec((rows, FBLOCK), lambda step: (0, step))
    weights = pl.BlockSpec((width, FBLOCK), lambda step: (0, step))
    return gridded(
        21, units_kernel, total // FBLOCK,
        [whole((rows, width))] * 2 + [weights] * 3,
        (units,) * 3,
        (jax.ShapeDtypeStruct((rows, total), bf16),) * 3,
        (normed, cotangent, w_gate, w_up, w_down),
    )


def partner_kernel(
    wide_ref, cot_ref, cot_t_ref, own_t_ref, own_ref, wg_ref, wu_ref, wd_ref,
    gg_ref, gu_ref, keep_ref, send_ref, normed_ref,
):
    half = keep_ref.shape[0]

    @pl.when(pl.program_id(0) == 0)
    def _():
        normed_ref[...] = wide_ref[...].astype(bf16)

    hidden, gg_ref[...], gu_ref[...] = unit_gradients(normed_ref[...], cot_ref[...], wg_ref, wu_ref, wd_ref)
    total = mm(own_t_ref[...], own_ref[...]) + mm(cot_t_ref[...], hidden)
    keep_ref[...] = total[:half]
    send_ref[...] = total[half:]


def partner_units(normed, cotangent, cotangent_t, own_t, own_hidden, w_gate, w_up, w_down):
    rows, width = normed.shape
    total = w_gate.shape[1]
    units = pl.BlockSpec((rows, FBLOCK), lambda step: (0, step))
    weights = pl.BlockSpec((width, FBLOCK), lambda step: (0, step))
    grads = pl.BlockSpec((width // 4, FBLOCK), lambda step: (0, step))
    shape = jax.ShapeDtypeStruct
    return gridded(
        27, partner_kernel, total // FBLOCK,
        [whole((rows, width))] * 2 + [whole((width // 2, rows))] * 2 + [units] + [weights] * 3,
        (units,) * 2 + (grads,) * 2,
        (shape((rows, total), bf16),) * 2 + (shape((width // 4, total), f32),) * 2,
        (normed, cotangent, cotangent_t, own_t, own_hidden, w_gate, w_up, w_down),
        [pltpu.VMEM((rows, width), bf16)],
    )


def pair_kernel(one_t_ref, two_t_ref, one_ref, two_ref, keep_ref, send_ref):
    half = keep_ref.shape[0]
    total = mm(one_t_ref[...], one_ref[...]) + mm(two_t_ref[...], two_ref[...])
    keep_ref[...] = total[:half]
    send_ref[...] = total[half:]


def pair_weights(one_t, two_t, one, two):
    half, rows = one_t.shape
    total = one.shape[1]
    block = 3 * FBLOCK
    units = pl.BlockSpec((rows, block), lambda step: (0, step))
    grads = pl.BlockSpec((half // 2, block), lambda step: (0, step))
    return gridded(
        10, pair_kernel, total // block,
        [whole((half, rows))] * 2 + [units] * 2, (grads,) * 2,
        (jax.ShapeDtypeStruct((half // 2, total), f32),) * 2, (one_t, two_t, one, two),
    )


def products_kernel(count, *refs):
    lefts, rights, outs = refs[:count], refs[count : 2 * count], refs[2 * count :]
    total = mm(lefts[0][...], rights[0][...], NT)
    for left, right in zip(lefts[1:], rights[1:]):
        total += mm(left[...], right[...], NT)
    each = total.shape[0] // len(outs)
    for number, ref in enumerate(outs):
        ref[...] = total[number * each : (number + 1) * each]


def products(lefts, rights, pieces, time=12):
    rows, columns = lefts[0].shape[0], rights[0].shape[0]
    out = pl.BlockSpec((rows // pieces, BLOCK), lambda step: (0, step))
    return gridded(
        time, functools.partial(products_kernel, len(lefts)), columns // BLOCK,
        [whole(item.shape) for item in lefts]
        + [pl.BlockSpec((BLOCK, item.shape[1]), lambda step: (step, 0)) for item in rights],
        (out,) * pieces, (jax.ShapeDtypeStruct((rows // pieces, columns), f32),) * pieces, tuple(lefts) + tuple(rights),
    )


def turned_kernel(places_ref, left_ref, *refs):
    rights, (keep_ref, send_ref, scratch, turned_ref) = refs[:-4], refs[-4:]
    half = keep_ref.shape[0]
    turn(left_ref[...], places_ref, scratch, turned_ref)
    low = 0
    for right in rights:
        high = low + right.shape[1]
        send_ref[:, low:high] = mm(turned_ref[half:, :], right[...])
        keep_ref[:, low:high] = mm(turned_ref[:half, :], right[...])
        low = high


def turned_weights(places, left, rights):
    rows, width = left.shape
    total = sum(item.shape[1] for item in rights)
    return pl.pallas_call(
        turned_kernel,
        out_shape=(jax.ShapeDtypeStruct((width // 2, total), f32),) * 2,
        in_specs=[SMEM_SPEC] + [VMEM_SPEC] * (1 + len(rights)),
        out_specs=(VMEM_SPEC,) * 2,
        scratch_shapes=[pltpu.VMEM((width, rows), f32), pltpu.VMEM((width, rows), bf16)],
        compiler_params=PARAMS,
        cost_estimate=cost(6),
    )(places, left, *rights)


def swap(values):
    return lax.ppermute(values, "tensor", [(0, 1), (1, 0)])


LABELS = ((0, 1, 2), (2, 0, 1))
DOWN_LABELS = ((0, 1, 2), (2, 0, 1))
LATE_LABELS = ((0, 1, 2), (1, 0, 2))


class Layout:
    def __init__(self, rows, labels):
        self.labels = labels
        self.devices = lax.axis_size("dp")
        self.bits = self.devices.bit_length() - 1
        core = lax.axis_index("tensor")
        self.mine = self.label(lax.axis_index("dp"), core)
        numbers = self.label(jnp.arange(self.devices, dtype=jnp.int32), core)
        each = rows // self.devices
        first = (numbers & 1) ^ self.bit(0)
        second = ((numbers >> 1) & 1) ^ self.bit(1)
        self.halves = (first * (self.devices // 2) + (numbers >> 1)) * each
        self.quarters = (first * (self.devices // 2) + second * (self.devices // 4) + (numbers >> 2)) * each

    def label(self, number, core):
        first, second = (
            (number & ~7) | functools.reduce(jnp.bitwise_or, [((number >> self.labels[one][bit]) & 1) << bit for bit in range(3)])
            for one in range(2)
        )
        return jnp.where(core == 1, second, first).astype(jnp.int32)

    def bit(self, bit):
        return (self.mine >> bit) & 1

    def exchange(self, values, bit):
        own = [self.labels[core][bit] if bit < 3 else bit for core in range(2)]
        pairs = [(2 * i + core, 2 * (i ^ (1 << own[core])) + core) for i in range(self.devices) for core in range(2)]
        return lax.ppermute(values, ("dp", "tensor"), pairs)


class Scatter:
    def __init__(self, layout, keep, send, first):
        self.layout = layout
        self.stage = first
        self.left = list(range(layout.bits - 1, first, -1))
        self.addends = [self.spread(keep)]
        self.send = self.spread(send)

    def spread(self, values):
        return values.reshape((2,) * len(self.left) + (-1, values.shape[1]))

    def exchange(self):
        self.addends.append(self.layout.exchange(self.send, self.stage))
        self.stage += 1

    def prepare(self, earlier=None):
        mine = self.layout.bit(self.stage)
        axis = self.left.index(self.stage)
        if earlier is not None:
            self.addends[-1] = after(self.addends[-1], earlier)

        def take(array, which):
            return lax.dynamic_index_in_dim(array, which, axis, keepdims=False)

        self.send = functools.reduce(jnp.add, [take(item, 1 - mine) for item in self.addends])
        self.addends = [take(item, mine) for item in self.addends]
        self.left.remove(self.stage)
        self.exchange()
        return self.send

    def result(self):
        return functools.reduce(jnp.add, self.addends)


def finish(scatter, earlier):
    while scatter.stage < scatter.layout.bits:
        earlier = scatter.prepare(earlier)
    scatter.addends[-1] = after(scatter.addends[-1], earlier)
    total = scatter.result()
    return total, total


def after(values, earlier):
    return lax.optimization_barrier((values, earlier))[0]


def per_device(
    inputs,
    cotangent,
    segment_ids,
    attn_gain,
    w_query,
    w_key,
    w_value,
    query_gain,
    key_gain,
    w_output,
    ffn_gain,
    w_gate,
    w_up,
    w_down,
):
    width = inputs.shape[1]
    units = w_gate.shape[1]
    layout = Layout(width, LABELS)
    layout_down = Layout(width, DOWN_LABELS)
    layout_late = Layout(width, LATE_LABELS)
    devices, bits = layout.devices, layout.bits
    each = width // devices
    me = lax.axis_index("dp")

    cotangent_wide = widened(cotangent)
    cotangent_far = layout.exchange(cotangent_wide, 0)
    *part, normed, linear, query, key, value, mixed, cosine, sine = attention_forward(
        after(inputs, cotangent_wide), attn_gain, w_query, w_key, w_value, query_gain, key_gain, segment_ids, w_output
    )
    part_swapped = [swap(item) for item in part]
    (cotangent_t,) = turned(after(cotangent, normed), layout_down.quarters)
    middle, normed_two, normed_wide = middle_norm(inputs, after(part, cotangent_t), part_swapped, ffn_gain)
    normed_far = layout.exchange(after(normed_wide, cotangent_far), 0)
    hidden, gg, gu = ffn_units(after(normed_two, normed_wide), cotangent, w_gate, w_up, w_down)
    cotangent_far, cotangent_far_t = turned(after(cotangent_far, hidden), layout_down.quarters, True)
    grad_two = products((after(gg, cotangent_far_t), gu), (w_gate, w_up), 2)
    grad_two_swapped = [swap(item) for item in grad_two]
    (normed_two_t,) = turned(after(normed_two, grad_two), layout.quarters)
    far_gg, far_gu, keep, send = partner_units(
        after(normed_far, normed_two_t), cotangent_far, cotangent_far_t, cotangent_t, hidden, w_gate, w_up, w_down
    )
    down = Scatter(layout_down, keep, send, 1)
    down.exchange()
    (normed_far_t,) = turned(after(normed_far, send), layout.quarters)
    gate = Scatter(layout, *pair_weights(normed_two_t, normed_far_t, gg, far_gg), 1)
    gate.exchange()
    upper = Scatter(layout, *pair_weights(after(normed_two_t, gate.send), normed_far_t, gu, far_gu), 1)
    upper.exchange()
    grad_middle, grad_branch, grad_ffn_gain = norm_back(
        after(middle, upper.send), cotangent, grad_two, grad_two_swapped, ffn_gain, (f32, bf16)
    )
    token = down.prepare(grad_branch)

    def heads_back(k_pair, token):
        return attention_backward(
            k_pair, after(grad_branch, token), w_output, linear, query, key, value, query_gain, key_gain,
            (cosine, sine), segment_ids,
        )

    back = [heads_back(0, token)]
    token = gate.prepare(back[0])
    token = down.prepare(token)
    for k_pair in range(1, w_key.shape[1] // LANES):
        back.append(heads_back(k_pair, token))
        token = back[-1]
    gq, gk, gv, gains = zip(*back)
    gains = sum(gains)
    three = Scatter(layout_late, *turned_weights(layout_late.halves, normed, gq + gk + gv), 0)
    three.exchange()
    w_parts = [
        weight[:, at : at + piece.shape[1]]
        for weight, pieces in ((w_query, gq), (w_key, gk), (w_value, gv))
        for piece, at in zip(pieces, range(0, weight.shape[1], pieces[0].shape[1]))
    ]
    grad_one = products((after(gq[0], three.send),) + gq[1:] + gk + gv, w_parts, 1)
    grad_one_swapped = [swap(item) for item in grad_one]
    ffn = products((after(hidden, grad_one),), (w_down,), 1, 60)[0]
    token = upper.prepare(ffn)
    token = three.prepare(token)
    token = gate.prepare(token)
    sum_down, token = finish(down, token)
    output = Scatter(layout_late, *turned_weights(layout_late.halves, after(grad_branch, token), (mixed,)), 0)
    output.exchange()
    token = three.prepare(output.send)
    grad_inputs, grad_attn_gain = norm_back(
        inputs, after(grad_middle, token), grad_one, grad_one_swapped, attn_gain, (bf16,)
    )
    small = jnp.concatenate(
        [
            grad_attn_gain.reshape(-1, LANES) * 0.5,
            grad_ffn_gain.reshape(-1, LANES) * 0.5,
            jnp.pad(gains[:2, :HEAD_DIM] + gains[:2, HEAD_DIM:], ((0, 6), (0, LANES - HEAD_DIM))),
        ]
    )
    small_swapped = swap(small)
    token = upper.prepare(small)
    small = small + after(small_swapped, token)
    small_far = layout.exchange(small, 0)
    sum_gate, token = finish(gate, small)
    ffn_swapped = swap(after(ffn, token))
    token = output.prepare(token)
    token = three.prepare(token)
    small = small + after(small_far, token)
    small_far = layout.exchange(small, 1)
    block_out = (middle + (ffn + after(ffn_swapped, small))).astype(bf16)
    sum_upper, token = finish(upper, block_out)
    token = output.prepare(token)
    small = small + after(small_far, token)
    small_far = layout.exchange(small, 2)
    sum_three, token = finish(three, small)
    token = output.prepare(token)
    small = small + after(small_far, token)
    for bit in range(3, bits):
        small = small + layout.exchange(small, bit)
    sum_output, _ = finish(output, token)
    lines = width // LANES
    sum_attn_gain = lax.dynamic_slice_in_dim(small[:lines].reshape(width), me * each, each)
    sum_ffn_gain = lax.dynamic_slice_in_dim(small[lines : 2 * lines].reshape(width), me * each, each)

    q_width, k_width = w_query.shape[1], w_key.shape[1]
    return (
        block_out,
        grad_inputs,
        sum_attn_gain,
        sum_three[:, :q_width],
        sum_three[:, q_width : q_width + k_width],
        sum_three[:, q_width + k_width :],
        small[2 * lines, :HEAD_DIM],
        small[2 * lines + 1, :HEAD_DIM],
        sum_output,
        sum_ffn_gain,
        sum_gate,
        sum_upper,
        sum_down,
    )


def solution(mesh):
    placed = (
        P("dp", None),
        P("dp", None),
        P("dp"),
        P(),
        P(None, "tensor"),
        P(None, "tensor"),
        P(None, "tensor"),
        P(),
        P(),
        P(None, "tensor"),
        P(),
        P(None, "tensor"),
        P(None, "tensor"),
        P(None, "tensor"),
    )
    return jax.shard_map(
        per_device,
        mesh=mesh,
        in_specs=placed,
        out_specs=(
            P("dp", None),
            P("dp", None),
            P("dp"),
            P("dp", "tensor"),
            P("dp", "tensor"),
            P("dp", "tensor"),
            P(),
            P(),
            P("dp", "tensor"),
            P("dp"),
            P("dp", "tensor"),
            P("dp", "tensor"),
            P("dp", "tensor"),
        ),
        check_vma=False,
    )
```

```python
import functools

import jax
import jax.numpy as jnp
from jax import lax
from jax.experimental import pallas as pl
from jax.experimental.pallas import tpu as pltpu
from jax.sharding import PartitionSpec as P

HEAD_DIM = 64
LANES = 128
WINDOW = 512
BLOCK = 256
epsilon = 1e-05
rope_base = 1000000.0
masked_score = -1e30
f32 = jnp.float32
bf16 = jnp.bfloat16
NN = (((1,), (0,)), ((), ()))
NT = (((1,), (1,)), ((), ()))


def mm(left, right, dims=NN):
    return lax.dot_general(left, right, dims, preferred_element_type=f32)


def ones_by_head():
    row = lax.broadcasted_iota(jnp.int32, (LANES, LANES), 0)
    col = lax.broadcasted_iota(jnp.int32, (LANES, LANES), 1)
    return jnp.where((row >> 6) == (col >> 6), 1.0, 0.0).astype(bf16)


def head_sums(values, ones):
    high = values.astype(bf16)
    rest = (values - high.astype(f32)).astype(bf16)
    return mm(high, ones) + mm(rest, ones)


def swap_halves(values):
    lane = lax.broadcasted_iota(jnp.int32, values.shape, 1)
    return jnp.where((lane & 63) < 32, pltpu.roll(values, 96, 1), pltpu.roll(values, 32, 1))


def first_head(values):
    return lax.broadcasted_iota(jnp.int32, values.shape, 1) < 64


def stack_heads(pair):
    first = first_head(pair)
    zero = jnp.zeros_like(pair)
    return jnp.concatenate([jnp.where(first, pair, zero), jnp.where(first, zero, pair)], axis=0)


def pick_heads(stacked):
    rows = stacked.shape[0] // 2
    top = stacked[:rows]
    return jnp.where(first_head(top), top, stacked[rows:])


def column(row):
    return jnp.broadcast_to(row.astype(f32), (8, row.shape[1])).T[:, :1].astype(jnp.int32)


def twice(gain):
    return jnp.concatenate([gain, gain], axis=1)


def key_range(number):
    low = max(0, (number * BLOCK - (WINDOW - 1)) // BLOCK * BLOCK)
    return low, (number + 1) * BLOCK


def forward_kernel(
    x_ref, gain_ref, wq_ref, wk_ref, wv_ref, qg_ref, kg_ref, segr_ref, rate_ref, wo_ref,
    upper_ref, lower_ref, normed_ref, lin_ref, q_ref, k_ref, v_ref, mixed_ref, cos_ref, sin_ref, bias_ref, segc_ref,
):
    rows = x_ref.shape[0]
    segc_ref[...] = column(segr_ref[...])
    query_gain, key_gain = twice(qg_ref[...]), twice(kg_ref[...])
    q_pairs = wq_ref.shape[1] // LANES
    k_pairs = wk_ref.shape[1] // LANES
    blocks = rows // BLOCK
    ones = ones_by_head()

    def project(step, carry):
        at = pl.ds(pl.multiple_of(step * BLOCK, BLOCK), BLOCK)
        x = x_ref[at, :].astype(f32)
        scale = lax.rsqrt(jnp.mean(x * x, axis=-1, keepdims=True) + epsilon)
        normed = (x * scale * gain_ref[...]).astype(bf16)
        normed_ref[at, :] = normed
        begins = jnp.sum((segr_ref[...] < segc_ref[at, :]).astype(f32), axis=-1, keepdims=True)
        places = (step * BLOCK + lax.broadcasted_iota(jnp.int32, (BLOCK, 1), 0)).astype(f32)
        angles = (places - begins) * rate_ref[...]
        lane = lax.broadcasted_iota(jnp.int32, angles.shape, 1)
        cosine, sine = jnp.cos(angles), jnp.sin(angles)
        sine = jnp.where((lane & 63) < 32, -sine, sine)
        cos_ref[at, :] = cosine
        sin_ref[at, :] = sine

        def rotated(linear, gain):
            unit = linear * lax.rsqrt(head_sums(linear * linear, ones) * (1.0 / HEAD_DIM) + epsilon)
            scaled = unit * gain
            return scaled * cosine + swap_halves(scaled) * sine

        queries = mm(normed, wq_ref[...])
        lin_ref[at, : q_pairs * LANES] = queries
        for pair in range(q_pairs):
            part = queries[:, pair * LANES : (pair + 1) * LANES]
            q_ref[pair, at, :] = (rotated(part, query_gain).astype(bf16).astype(f32) * HEAD_DIM**-0.5).astype(bf16)
        keys = mm(normed, wk_ref[...])
        lin_ref[at, q_pairs * LANES :] = keys
        values = mm(normed, wv_ref[...])
        for pair in range(k_pairs):
            part = slice(pair * LANES, (pair + 1) * LANES)
            for ref, both in ((k_ref, rotated(keys[:, part], key_gain)), (v_ref, values[:, part])):
                other = pltpu.roll(both, 64, 1)
                first = first_head(both)
                ref[2 * pair, at, :] = jnp.where(first, both, other).astype(bf16)
                ref[2 * pair + 1, at, :] = jnp.where(first, other, both).astype(bf16)
        return carry

    lax.fori_loop(0, blocks, project, 0)

    for number in range(blocks):
        low, high = key_range(number)
        at = slice(number * BLOCK, (number + 1) * BLOCK)
        span = high - low
        row_ids = number * BLOCK + lax.broadcasted_iota(jnp.int32, (BLOCK, span), 0)
        col_ids = low + lax.broadcasted_iota(jnp.int32, (BLOCK, span), 1)
        allowed = (segc_ref[at, :] == segr_ref[:, low:high]) & (col_ids <= row_ids)
        bias = jnp.where(allowed, 0.0, masked_score)
        bias_ref[:BLOCK, :span] = bias
        bias_ref[BLOCK:, :span] = bias

        def head(pair, carry):
            stacked = stack_heads(q_ref[pair, at, :])
            scores = mm(stacked, k_ref[pair, low:high, :], NT)
            powers = jnp.exp(scores + bias_ref[:, :span])
            totals = jnp.sum(powers, axis=-1, keepdims=True)
            probs = (powers * (1.0 / totals)).astype(bf16)
            mixed = pick_heads(mm(probs, v_ref[pair, low:high, :]))
            lanes = pl.ds(pl.multiple_of(pair * LANES, LANES), LANES)
            mixed_ref[at, lanes] = mixed.astype(bf16)
            return carry

        lax.fori_loop(0, q_pairs, head, 0, unroll=True)
        half = upper_ref.shape[0]
        part_ref = upper_ref if number * BLOCK < half else lower_ref
        part_ref[number * BLOCK % half : number * BLOCK % half + BLOCK, :] = mm(mixed_ref[at, :], wo_ref[...], NT)


def backward_kernel(
    gb_ref, wo_ref, q_lin_ref, k_lin_ref, q_ref, k_ref, v_ref, qg_ref, kg_ref, cos_ref, sin_ref, segr_ref,
    gq_ref, gk_ref, gv_ref, gains_ref, bias_ref, gm_ref, dq_ref, dk_ref, dv_ref, segc_ref,
):
    rows = gb_ref.shape[0]
    segc_ref[...] = column(segr_ref[...])
    query_gain, key_gain = twice(qg_ref[...]), twice(kg_ref[...])
    q_pairs = q_ref.shape[0]
    k_pairs = q_pairs // 2
    blocks = rows // BLOCK
    ones = ones_by_head()

    for number in range(blocks):
        at = slice(number * BLOCK, (number + 1) * BLOCK)
        mixed = mm(gb_ref[at, :], wo_ref[...]).astype(bf16)
        for pair in range(q_pairs):
            gm_ref[pair, at, :] = mixed[:, pair * LANES : (pair + 1) * LANES]

    for number in reversed(range(blocks)):
        low, high = key_range(number)
        at = slice(number * BLOCK, (number + 1) * BLOCK)
        span = high - low
        key_ids = low + lax.broadcasted_iota(jnp.int32, (span, BLOCK), 0)
        row_ids = number * BLOCK + lax.broadcasted_iota(jnp.int32, (span, BLOCK), 1)
        allowed = (segc_ref[low:high, :] == segr_ref[:, at]) & (key_ids <= row_ids)
        bias = jnp.where(allowed, 0.0, masked_score)
        bias_ref[:span, :BLOCK] = bias
        bias_ref[:span, BLOCK:] = bias
        fresh_from = 0 if number == blocks - 1 else key_range(number + 1)[0]

        def head(pair, carry):
            queries = stack_heads(q_ref[pair, at, :])
            grads = stack_heads(gm_ref[pair, at, :])
            keys = k_ref[pair, low:high, :]
            values = v_ref[pair, low:high, :]
            powers = jnp.exp(mm(keys, queries, NT) + bias_ref[:span, :])
            probs = powers * (1.0 / jnp.sum(powers, axis=0, keepdims=True))
            grad_probs = mm(values, grads, NT)
            center = jnp.sum(grad_probs * probs, axis=0, keepdims=True)
            grad_scores = (probs * (grad_probs - center)).astype(bf16)
            dq = lax.dot_general(grad_scores, keys, (((0,), (0,)), ((), ())), preferred_element_type=f32)
            dq_ref[pair, at, :] = pick_heads(dq) * HEAD_DIM**-0.5
            dk = mm(grad_scores, queries)
            dv = mm(probs.astype(bf16), grads)
            if number == blocks - 1:
                dk_ref[pair, low:high, :] = dk
                dv_ref[pair, low:high, :] = dv
            else:
                if low < fresh_from:
                    dk_ref[pair, low:fresh_from, :] = dk[: fresh_from - low]
                    dv_ref[pair, low:fresh_from, :] = dv[: fresh_from - low]
                start = max(low, fresh_from)
                dk_ref[pair, start:high, :] += dk[start - low :]
                dv_ref[pair, start:high, :] += dv[start - low :]
            return carry

        lax.fori_loop(0, q_pairs, head, 0, unroll=True)

    gains_ref[...] = jnp.zeros_like(gains_ref)

    def finish(step, carry):
        at = pl.ds(pl.multiple_of(step * BLOCK, BLOCK), BLOCK)
        cosine, sine = cos_ref[at, :], sin_ref[at, :]

        def linear_grad(grad, linear, gain, row):
            scale = lax.rsqrt(head_sums(linear * linear, ones) * (1.0 / HEAD_DIM) + epsilon)
            unit = linear * scale
            turned = grad * cosine - swap_halves(grad) * sine
            gains_ref[row : row + 1, :] += jnp.sum(turned * unit, axis=0, keepdims=True)
            inner = turned * gain
            return (scale * (inner - unit * (head_sums(inner * unit, ones) * (1.0 / HEAD_DIM)))).astype(bf16)

        for pair in range(q_pairs):
            lanes = slice(pair * LANES, (pair + 1) * LANES)
            gq_ref[at, lanes] = linear_grad(dq_ref[pair, at, :], q_lin_ref[at, lanes], query_gain, 0)
        for pair in range(k_pairs):
            lanes = slice(pair * LANES, (pair + 1) * LANES)

            def both(ref):
                one, two = ref[2 * pair, at, :], ref[2 * pair + 1, at, :]
                one = one + pltpu.roll(one, 64, 1)
                two = two + pltpu.roll(two, 64, 1)
                return jnp.where(first_head(one), one, two)

            gk_ref[at, lanes] = linear_grad(both(dk_ref), k_lin_ref[at, lanes], key_gain, 1)
            gv_ref[at, lanes] = both(dv_ref).astype(bf16)
        return carry

    lax.fori_loop(0, blocks, finish, 0)


PARAMS = pltpu.CompilerParams(vmem_limit_bytes=56 * 1024 * 1024)
SHARE = 1.0


def cost(time):
    return pl.CostEstimate(flops=int(time * SHARE * 1e9) + 1000, bytes_accessed=1000, transcendentals=0)


def call(kernel, outs, scratch, *operands):
    return pl.pallas_call(
        kernel, out_shape=outs, scratch_shapes=scratch, compiler_params=PARAMS, cost_estimate=cost(30)
    )(*operands)


def attention_forward(inputs, attn_gain, w_query, w_key, w_value, query_gain, key_gain, segment_ids, w_output):
    rows, width = inputs.shape
    q_width, k_width = w_query.shape[1], w_key.shape[1]
    pairs = q_width // LANES
    shape = jax.ShapeDtypeStruct
    outs = (
        shape((rows // 2, w_output.shape[0]), f32),
        shape((rows // 2, w_output.shape[0]), f32),
        shape((rows, width), bf16),
        shape((rows, q_width + k_width), f32),
        shape((pairs, rows, LANES), bf16),
        shape((pairs, rows, LANES), bf16),
        shape((pairs, rows, LANES), bf16),
        shape((rows, q_width), bf16),
        shape((rows, LANES), f32),
        shape((rows, LANES), f32),
    )
    span = min(rows, BLOCK + WINDOW)
    halves = HEAD_DIM // 2
    rates = rope_base ** (-2.0 * jnp.arange(halves, dtype=f32) / HEAD_DIM)
    return call(
        forward_kernel, outs, [pltpu.VMEM((2 * BLOCK, span), f32), pltpu.VMEM((rows, 1), jnp.int32)],
        inputs, attn_gain[None, :], w_query, w_key, w_value, query_gain[None, :], key_gain[None, :],
        segment_ids[None, :], jnp.concatenate([rates] * 4)[None, :], w_output,
    )


def attention_backward(
    k_pair, grad_branch, w_output, linear, query, key, value, query_gain, key_gain, tables, segment_ids
):
    rows, width = grad_branch.shape
    shape = jax.ShapeDtypeStruct
    outs = (
        shape((rows, 2 * LANES), bf16),
        shape((rows, LANES), bf16),
        shape((rows, LANES), bf16),
        shape((8, LANES), f32),
    )
    span = min(rows, BLOCK + WINDOW)
    scratch = [
        pltpu.VMEM((span, 2 * BLOCK), f32),
        pltpu.VMEM((2, rows, LANES), bf16),
        pltpu.VMEM((2, rows, LANES), f32),
        pltpu.VMEM((2, rows, LANES), f32),
        pltpu.VMEM((2, rows, LANES), f32),
        pltpu.VMEM((rows, 1), jnp.int32),
    ]
    heads = query.shape[0]

    def fixed(block, *place):
        return pl.BlockSpec(block, lambda step: place, pipeline_mode=pl.Buffered(1))

    pairs = fixed((2, rows, LANES), k_pair, 0, 0)
    small = fixed((1, HEAD_DIM), 0, 0)
    table = fixed((rows, LANES), 0, 0)
    return pl.pallas_call(
        backward_kernel,
        grid=(1,),
        in_specs=[
            fixed((rows, width), 0, 0), fixed((width, 2 * LANES), 0, k_pair),
            fixed((rows, 2 * LANES), 0, k_pair), fixed((rows, LANES), 0, heads + k_pair),
            pairs, pairs, pairs, small, small, table, table, fixed((1, rows), 0, 0),
        ],
        out_specs=tuple(fixed(item.shape, 0, 0) for item in outs),
        out_shape=outs,
        scratch_shapes=scratch,
        compiler_params=PARAMS,
        cost_estimate=cost(18),
    )(
        grad_branch, w_output, linear, linear, query, key, value, query_gain[None, :], key_gain[None, :],
        *tables, segment_ids[None, :],
    )


def whole(shape):
    return pl.BlockSpec(shape, lambda step: (0,) * len(shape), pipeline_mode=pl.Buffered(1))


SMEM_SPEC = pl.BlockSpec(memory_space=pltpu.SMEM)
VMEM_SPEC = pl.BlockSpec(memory_space=pltpu.VMEM)


def gridded(time, kernel, steps, in_specs, out_specs, outs, operands, scratch=()):
    return pl.pallas_call(
        kernel,
        grid=(steps,),
        in_specs=in_specs,
        out_specs=out_specs,
        out_shape=outs,
        scratch_shapes=list(scratch),
        compiler_params=PARAMS,
        cost_estimate=cost(time),
    )(*operands)


def turn(values, places, scratch, out):
    groups = places.shape[0]
    each = scratch.shape[0] // groups
    turned = values.astype(f32).T
    for group in range(groups):
        place = pl.ds(pl.multiple_of(places[group], 8), each)
        scratch[place, :] = turned[group * each : (group + 1) * each]
    out[...] = scratch[: out.shape[0], :].astype(bf16)


ROWS = 512


def widen_kernel(x_ref, out_ref):
    out_ref[...] = x_ref[...].astype(f32)


def widened(values):
    rows, width = values.shape
    by_rows = pl.BlockSpec((ROWS, width), lambda step: (step, 0))
    return gridded(
        4, widen_kernel, rows // ROWS, [by_rows], (by_rows,), (jax.ShapeDtypeStruct((rows, width), f32),), (values,)
    )[0]


def turn_kernel(places_ref, x_ref, *refs):
    *narrow_refs, out_ref, scratch = refs
    for ref in narrow_refs:
        ref[...] = x_ref[...].astype(bf16)
    turn(x_ref[...], places_ref, scratch, out_ref)


def turned(values, places, narrow=False):
    rows, width = values.shape
    shape = jax.ShapeDtypeStruct
    by_rows = pl.BlockSpec((ROWS, width), lambda step: (step, 0))
    outs = ((by_rows,), (shape((rows, width), bf16),)) if narrow else ((), ())
    return gridded(
        4, turn_kernel, rows // ROWS,
        [SMEM_SPEC, by_rows],
        outs[0] + (pl.BlockSpec((width // 2, ROWS), lambda step: (0, step)),),
        outs[1] + (shape((width // 2, rows), bf16),),
        (places, values), [pltpu.VMEM((width, ROWS), f32)],
    )


def of_halves(refs):
    if len(refs) == 2:
        return refs[0][...] + refs[1][...]
    early = pl.program_id(0) < pl.num_programs(0) // 2
    return jnp.where(early, refs[0][...] + refs[2][...], refs[1][...] + refs[3][...])


def half_specs(pieces, rows, width):
    steps = rows // ROWS
    if pieces == 2:
        return [pl.BlockSpec((ROWS, width), lambda step: (step, 0))] * 2
    upper = pl.BlockSpec((ROWS, width), lambda step: (jnp.minimum(step, steps // 2 - 1), 0))
    lower = pl.BlockSpec((ROWS, width), lambda step: (jnp.maximum(step - steps // 2, 0), 0))
    return [upper, lower, upper, lower]


def middle_kernel(x_ref, *refs):
    gain_ref, middle_ref, normed_ref, wide_ref = refs[-4:]
    middle = x_ref[...].astype(f32) + of_halves(refs[:-4])
    scale = lax.rsqrt(jnp.mean(middle * middle, axis=-1, keepdims=True) + epsilon)
    normed = (middle * scale * gain_ref[...]).astype(bf16)
    middle_ref[...] = middle
    normed_ref[...] = normed
    wide_ref[...] = normed.astype(f32)


def middle_norm(inputs, one, two, gain):
    rows, width = inputs.shape
    by_rows = pl.BlockSpec((ROWS, width), lambda step: (step, 0))
    shape = jax.ShapeDtypeStruct
    return gridded(
        10, middle_kernel, rows // ROWS,
        [by_rows] + half_specs(len(one) + len(two), rows, width) + [whole((1, width))],
        (by_rows,) * 3,
        (shape((rows, width), f32), shape((rows, width), bf16), shape((rows, width), f32)),
        (inputs, *one, *two, gain[None, :]),
    )


def norm_back_kernel(parts, value_ref, direct_ref, *refs):
    grad = of_halves(refs[:parts])
    gain_ref, *out_refs, gain_grad_ref = refs[parts:]
    value = value_ref[...].astype(f32)
    scale = lax.rsqrt(jnp.mean(value * value, axis=-1, keepdims=True) + epsilon)
    unit = value * scale
    inner = grad * gain_ref[...]
    total = direct_ref[...].astype(f32) + scale * (inner - unit * jnp.mean(inner * unit, axis=-1, keepdims=True))
    for ref in out_refs:
        ref[...] = total.astype(ref.dtype)

    @pl.when(pl.program_id(0) == 0)
    def _():
        gain_grad_ref[...] = jnp.zeros_like(gain_grad_ref)

    gain_grad_ref[...] += jnp.sum(grad * unit, axis=0, keepdims=True)


def norm_back(value, direct, one, two, gain, types):
    rows, width = value.shape
    steps = rows // ROWS
    by_rows = pl.BlockSpec((ROWS, width), lambda step: (step, 0))
    shape = jax.ShapeDtypeStruct
    return gridded(
        9, functools.partial(norm_back_kernel, len(one) + len(two)), steps,
        [by_rows, by_rows] + half_specs(len(one) + len(two), rows, width) + [whole((1, width))],
        (by_rows,) * len(types) + (pl.BlockSpec((1, width), lambda step: (0, 0)),),
        tuple(shape((rows, width), kind) for kind in types) + (shape((1, width), f32),),
        (value, direct, *one, *two, gain[None, :]),
    )


FBLOCK = 256


def unit_gradients(normed, cotangent, wg_ref, wu_ref, wd_ref):
    gate = mm(normed, wg_ref[...])
    upper = mm(normed, wu_ref[...])
    grad = mm(cotangent, wd_ref[...])
    share = 0.5 * jnp.tanh(0.5 * gate) + 0.5
    swish = gate * share
    return (
        (swish * upper).astype(bf16),
        (grad * upper * (share + swish * (1.0 - share))).astype(bf16),
        (grad * swish).astype(bf16),
    )


def units_kernel(normed_ref, cot_ref, wg_ref, wu_ref, wd_ref, hidden_ref, gg_ref, gu_ref):
    hidden_ref[...], gg_ref[...], gu_ref[...] = unit_gradients(normed_ref[...], cot_ref[...], wg_ref, wu_ref, wd_ref)


def ffn_units(normed, cotangent, w_gate, w_up, w_down):
    rows, width = normed.shape
    total = w_gate.shape[1]
    units = pl.BlockSpec((rows, FBLOCK), lambda step: (0, step))
    weights = pl.BlockSpec((width, FBLOCK), lambda step: (0, step))
    return gridded(
        21, units_kernel, total // FBLOCK,
        [whole((rows, width))] * 2 + [weights] * 3,
        (units,) * 3,
        (jax.ShapeDtypeStruct((rows, total), bf16),) * 3,
        (normed, cotangent, w_gate, w_up, w_down),
    )


def partner_kernel(
    wide_ref, cot_ref, cot_t_ref, own_t_ref, own_ref, wg_ref, wu_ref, wd_ref,
    gg_ref, gu_ref, keep_ref, send_ref, normed_ref,
):
    half = keep_ref.shape[0]

    @pl.when(pl.program_id(0) == 0)
    def _():
        normed_ref[...] = wide_ref[...].astype(bf16)

    hidden, gg_ref[...], gu_ref[...] = unit_gradients(normed_ref[...], cot_ref[...], wg_ref, wu_ref, wd_ref)
    total = mm(own_t_ref[...], own_ref[...]) + mm(cot_t_ref[...], hidden)
    keep_ref[...] = total[:half]
    send_ref[...] = total[half:]


def partner_units(normed, cotangent, cotangent_t, own_t, own_hidden, w_gate, w_up, w_down):
    rows, width = normed.shape
    total = w_gate.shape[1]
    units = pl.BlockSpec((rows, FBLOCK), lambda step: (0, step))
    weights = pl.BlockSpec((width, FBLOCK), lambda step: (0, step))
    grads = pl.BlockSpec((width // 4, FBLOCK), lambda step: (0, step))
    shape = jax.ShapeDtypeStruct
    return gridded(
        27, partner_kernel, total // FBLOCK,
        [whole((rows, width))] * 2 + [whole((width // 2, rows))] * 2 + [units] + [weights] * 3,
        (units,) * 2 + (grads,) * 2,
        (shape((rows, total), bf16),) * 2 + (shape((width // 4, total), f32),) * 2,
        (normed, cotangent, cotangent_t, own_t, own_hidden, w_gate, w_up, w_down),
        [pltpu.VMEM((rows, width), bf16)],
    )


def pair_kernel(one_t_ref, two_t_ref, one_ref, two_ref, keep_ref, send_ref):
    half = keep_ref.shape[0]
    total = mm(one_t_ref[...], one_ref[...]) + mm(two_t_ref[...], two_ref[...])
    keep_ref[...] = total[:half]
    send_ref[...] = total[half:]


def pair_weights(one_t, two_t, one, two):
    half, rows = one_t.shape
    total = one.shape[1]
    block = 3 * FBLOCK
    units = pl.BlockSpec((rows, block), lambda step: (0, step))
    grads = pl.BlockSpec((half // 2, block), lambda step: (0, step))
    return gridded(
        10, pair_kernel, total // block,
        [whole((half, rows))] * 2 + [units] * 2, (grads,) * 2,
        (jax.ShapeDtypeStruct((half // 2, total), f32),) * 2, (one_t, two_t, one, two),
    )


def products_kernel(count, *refs):
    lefts, rights, outs = refs[:count], refs[count : 2 * count], refs[2 * count :]
    total = mm(lefts[0][...], rights[0][...], NT)
    for left, right in zip(lefts[1:], rights[1:]):
        total += mm(left[...], right[...], NT)
    each = total.shape[0] // len(outs)
    for number, ref in enumerate(outs):
        ref[...] = total[number * each : (number + 1) * each]


def products(lefts, rights, pieces, time=12):
    rows, columns = lefts[0].shape[0], rights[0].shape[0]
    out = pl.BlockSpec((rows // pieces, BLOCK), lambda step: (0, step))
    return gridded(
        time, functools.partial(products_kernel, len(lefts)), columns // BLOCK,
        [whole(item.shape) for item in lefts]
        + [pl.BlockSpec((BLOCK, item.shape[1]), lambda step: (step, 0)) for item in rights],
        (out,) * pieces, (jax.ShapeDtypeStruct((rows // pieces, columns), f32),) * pieces, tuple(lefts) + tuple(rights),
    )


def join_kernel(middle_ref, *refs):
    refs[-1][...] = (middle_ref[...] + of_halves(refs[:-1])).astype(bf16)


def joined(middle, one, two):
    rows, width = middle.shape
    by_rows = pl.BlockSpec((ROWS, width), lambda step: (step, 0))
    return gridded(
        7, join_kernel, rows // ROWS,
        [by_rows] + half_specs(len(one) + len(two), rows, width), (by_rows,),
        (jax.ShapeDtypeStruct((rows, width), bf16),), (middle, *one, *two),
    )[0]


def turned_kernel(places_ref, left_ref, *refs):
    rights, (keep_ref, send_ref, scratch, turned_ref) = refs[:-4], refs[-4:]
    half = keep_ref.shape[0]
    turn(left_ref[...], places_ref, scratch, turned_ref)
    low = 0
    for right in rights:
        high = low + right.shape[1]
        send_ref[:, low:high] = mm(turned_ref[half:, :], right[...])
        keep_ref[:, low:high] = mm(turned_ref[:half, :], right[...])
        low = high


def turned_weights(places, left, rights, time=6):
    rows, width = left.shape
    total = sum(item.shape[1] for item in rights)
    return pl.pallas_call(
        turned_kernel,
        out_shape=(jax.ShapeDtypeStruct((width // 2, total), f32),) * 2,
        in_specs=[SMEM_SPEC] + [VMEM_SPEC] * (1 + len(rights)),
        out_specs=(VMEM_SPEC,) * 2,
        scratch_shapes=[pltpu.VMEM((width, rows), f32), pltpu.VMEM((width, rows), bf16)],
        compiler_params=PARAMS,
        cost_estimate=cost(time),
    )(places, left, *rights)


def swap(values):
    return lax.ppermute(values, "tensor", [(0, 1), (1, 0)])


LABELS = ((0, 1, 2), (2, 0, 1))
DOWN_LABELS = ((0, 1, 2), (2, 0, 1))
LATE_LABELS = ((0, 1, 2), (2, 0, 1))


class Layout:
    def __init__(self, rows, labels):
        self.labels = labels
        self.devices = lax.axis_size("dp")
        self.bits = self.devices.bit_length() - 1
        core = lax.axis_index("tensor")
        self.mine = self.label(lax.axis_index("dp"), core)
        numbers = self.label(jnp.arange(self.devices, dtype=jnp.int32), core)
        each = rows // self.devices
        first = (numbers & 1) ^ self.bit(0)
        second = ((numbers >> 1) & 1) ^ self.bit(1)
        self.halves = (first * (self.devices // 2) + (numbers >> 1)) * each
        self.quarters = (first * (self.devices // 2) + second * (self.devices // 4) + (numbers >> 2)) * each

    def label(self, number, core):
        first, second = (
            (number & ~7) | functools.reduce(jnp.bitwise_or, [((number >> self.labels[one][bit]) & 1) << bit for bit in range(3)])
            for one in range(2)
        )
        return jnp.where(core == 1, second, first).astype(jnp.int32)

    def bit(self, bit):
        return (self.mine >> bit) & 1

    def exchange(self, values, bit):
        own = [self.labels[core][bit] if bit < 3 else bit for core in range(2)]
        pairs = [(2 * i + core, 2 * (i ^ (1 << own[core])) + core) for i in range(self.devices) for core in range(2)]
        return lax.ppermute(values, ("dp", "tensor"), pairs)


class Scatter:
    def __init__(self, layout, keep, send, first):
        self.layout = layout
        self.stage = first
        self.left = list(range(layout.bits - 1, first, -1))
        self.addends = [self.spread(keep)]
        self.send = self.spread(send)

    def spread(self, values):
        return values.reshape((2,) * len(self.left) + (-1, values.shape[1]))

    def exchange(self):
        self.addends.append(self.layout.exchange(self.send, self.stage))
        self.stage += 1

    def prepare(self, earlier=None):
        mine = self.layout.bit(self.stage)
        axis = self.left.index(self.stage)
        if earlier is not None:
            self.addends[-1] = after(self.addends[-1], earlier)

        def take(array, which):
            return lax.dynamic_index_in_dim(array, which, axis, keepdims=False)

        self.send = functools.reduce(jnp.add, [take(item, 1 - mine) for item in self.addends])
        self.addends = [take(item, mine) for item in self.addends]
        self.left.remove(self.stage)
        self.exchange()
        return self.send

    def result(self):
        return functools.reduce(jnp.add, self.addends)


def finish(scatter, earlier):
    while scatter.stage < scatter.layout.bits:
        earlier = scatter.prepare(earlier)
    scatter.addends[-1] = after(scatter.addends[-1], earlier)
    total = scatter.result()
    return total, total


def after(values, earlier):
    return lax.optimization_barrier((values, earlier))[0]


def per_device(
    inputs,
    cotangent,
    segment_ids,
    attn_gain,
    w_query,
    w_key,
    w_value,
    query_gain,
    key_gain,
    w_output,
    ffn_gain,
    w_gate,
    w_up,
    w_down,
):
    width = inputs.shape[1]
    units = w_gate.shape[1]
    layout = Layout(width, LABELS)
    layout_down = Layout(width, DOWN_LABELS)
    layout_late = Layout(width, LATE_LABELS)
    devices, bits = layout.devices, layout.bits
    each = width // devices
    me = lax.axis_index("dp")

    cotangent_wide = widened(cotangent)
    cotangent_far = layout.exchange(cotangent_wide, 0)
    *part, normed, linear, query, key, value, mixed, cosine, sine = attention_forward(
        after(inputs, cotangent_wide), attn_gain, w_query, w_key, w_value, query_gain, key_gain, segment_ids, w_output
    )
    part_swapped = [swap(item) for item in part]
    (cotangent_t,) = turned(after(cotangent, normed), layout_down.quarters)
    middle, normed_two, normed_wide = middle_norm(inputs, after(part, cotangent_t), part_swapped, ffn_gain)
    normed_far = layout.exchange(after(normed_wide, cotangent_far), 0)
    hidden, gg, gu = ffn_units(after(normed_two, normed_wide), cotangent, w_gate, w_up, w_down)
    cotangent_far, cotangent_far_t = turned(after(cotangent_far, hidden), layout_down.quarters, True)
    grad_two = products((after(gg, cotangent_far_t), gu), (w_gate, w_up), 2)
    grad_two_swapped = [swap(item) for item in grad_two]
    (normed_two_t,) = turned(after(normed_two, grad_two), layout.quarters)
    far_gg, far_gu, keep, send = partner_units(
        after(normed_far, normed_two_t), cotangent_far, cotangent_far_t, cotangent_t, hidden, w_gate, w_up, w_down
    )
    down = Scatter(layout_down, keep, send, 1)
    down.exchange()
    (normed_far_t,) = turned(after(normed_far, send), layout.quarters)
    gate = Scatter(layout, *pair_weights(normed_two_t, normed_far_t, gg, far_gg), 1)
    gate.exchange()
    upper = Scatter(layout, *pair_weights(after(normed_two_t, gate.send), normed_far_t, gu, far_gu), 1)
    upper.exchange()
    grad_middle, grad_branch, grad_ffn_gain = norm_back(
        after(middle, upper.send), cotangent, grad_two, grad_two_swapped, ffn_gain, (f32, bf16)
    )
    token = down.prepare(grad_branch)

    def heads_back(k_pair, token):
        return attention_backward(
            k_pair, after(grad_branch, token), w_output, linear, query, key, value, query_gain, key_gain,
            (cosine, sine), segment_ids,
        )

    back = [heads_back(0, token)]
    ffn = products((after(hidden, back[0]),), (w_down,), 1)
    token = gate.prepare(ffn)
    token = down.prepare(token)
    for k_pair in range(1, w_key.shape[1] // LANES):
        back.append(heads_back(k_pair, token))
        token = back[-1]
    gq, gk, gv, gains = zip(*back)
    gains = sum(gains)
    three = Scatter(layout_late, *turned_weights(layout_late.halves, normed, gq + gk + gv), 0)
    three.exchange()
    sum_down, token = finish(down, three.send)
    w_parts = [
        weight[:, at : at + piece.shape[1]]
        for weight, pieces in ((w_query, gq), (w_key, gk), (w_value, gv))
        for piece, at in zip(pieces, range(0, weight.shape[1], pieces[0].shape[1]))
    ]
    grad_one = products((after(gq[0], token),) + gq[1:] + gk + gv, w_parts, 1)
    grad_one_swapped = [swap(item) for item in grad_one]
    token = gate.prepare(grad_one)
    output = Scatter(layout_late, *turned_weights(layout_late.halves, after(grad_branch, token), (mixed,), 60), 0)
    output.exchange()
    token = upper.prepare(output.send)
    token = three.prepare(token)
    grad_inputs, grad_attn_gain = norm_back(
        inputs, after(grad_middle, token), grad_one, grad_one_swapped, attn_gain, (bf16,)
    )
    small = jnp.concatenate(
        [
            grad_attn_gain.reshape(-1, LANES) * 0.5,
            grad_ffn_gain.reshape(-1, LANES) * 0.5,
            jnp.pad(gains[:2, :HEAD_DIM] + gains[:2, HEAD_DIM:], ((0, 6), (0, LANES - HEAD_DIM))),
        ]
    )
    small_far = swap(small)
    sum_gate, token = finish(gate, small)
    token = three.prepare(token)
    token = upper.prepare(token)
    token = output.prepare(token)
    small = small + after(small_far, token)
    small_far = layout.exchange(small, 0)
    ffn_swapped = [swap(after(item, small)) for item in ffn]
    token = three.prepare(small)
    token = output.prepare(token)
    small = small + after(small_far, token)
    small_far = layout.exchange(small, 1)
    block_out = joined(after(middle, small), ffn, ffn_swapped)
    sum_upper, token = finish(upper, block_out)
    token = output.prepare(token)
    small = small + after(small_far, token)
    small_far = layout.exchange(small, 2)
    sum_three, token = finish(three, small)
    small = small + after(small_far, token)
    for bit in range(3, bits):
        small = small + layout.exchange(small, bit)
    sum_output, _ = finish(output, token)
    lines = width // LANES
    sum_attn_gain = lax.dynamic_slice_in_dim(small[:lines].reshape(width), me * each, each)
    sum_ffn_gain = lax.dynamic_slice_in_dim(small[lines : 2 * lines].reshape(width), me * each, each)

    q_width, k_width = w_query.shape[1], w_key.shape[1]
    return (
        block_out,
        grad_inputs,
        sum_attn_gain,
        sum_three[:, :q_width],
        sum_three[:, q_width : q_width + k_width],
        sum_three[:, q_width + k_width :],
        small[2 * lines, :HEAD_DIM],
        small[2 * lines + 1, :HEAD_DIM],
        sum_output,
        sum_ffn_gain,
        sum_gate,
        sum_upper,
        sum_down,
    )


def solution(mesh):
    placed = (
        P("dp", None),
        P("dp", None),
        P("dp"),
        P(),
        P(None, "tensor"),
        P(None, "tensor"),
        P(None, "tensor"),
        P(),
        P(),
        P(None, "tensor"),
        P(),
        P(None, "tensor"),
        P(None, "tensor"),
        P(None, "tensor"),
    )
    return jax.shard_map(
        per_device,
        mesh=mesh,
        in_specs=placed,
        out_specs=(
            P("dp", None),
            P("dp", None),
            P("dp"),
            P("dp", "tensor"),
            P("dp", "tensor"),
            P("dp", "tensor"),
            P(),
            P(),
            P("dp", "tensor"),
            P("dp"),
            P("dp", "tensor"),
            P("dp", "tensor"),
            P("dp", "tensor"),
        ),
        check_vma=False,
    )
```

```python
import functools

import jax
import jax.numpy as jnp
from jax import lax
from jax.experimental import pallas as pl
from jax.experimental.pallas import tpu as pltpu
from jax.sharding import PartitionSpec as P

HEAD_DIM = 64
LANES = 128
WINDOW = 512
BLOCK = 256
epsilon = 1e-05
rope_base = 1000000.0
masked_score = -1e30
f32 = jnp.float32
bf16 = jnp.bfloat16
NN = (((1,), (0,)), ((), ()))
NT = (((1,), (1,)), ((), ()))


def mm(left, right, dims=NN):
    return lax.dot_general(left, right, dims, preferred_element_type=f32)


def ones_by_head():
    row = lax.broadcasted_iota(jnp.int32, (LANES, LANES), 0)
    col = lax.broadcasted_iota(jnp.int32, (LANES, LANES), 1)
    return jnp.where((row >> 6) == (col >> 6), 1.0, 0.0).astype(bf16)


def head_sums(values, ones):
    high = values.astype(bf16)
    rest = (values - high.astype(f32)).astype(bf16)
    return mm(high, ones) + mm(rest, ones)


def swap_halves(values):
    lane = lax.broadcasted_iota(jnp.int32, values.shape, 1)
    return jnp.where((lane & 63) < 32, pltpu.roll(values, 96, 1), pltpu.roll(values, 32, 1))


def first_head(values):
    return lax.broadcasted_iota(jnp.int32, values.shape, 1) < 64


def stack_heads(pair):
    first = first_head(pair)
    zero = jnp.zeros_like(pair)
    return jnp.concatenate([jnp.where(first, pair, zero), jnp.where(first, zero, pair)], axis=0)


def pick_heads(stacked):
    rows = stacked.shape[0] // 2
    top = stacked[:rows]
    return jnp.where(first_head(top), top, stacked[rows:])


def column(row):
    return jnp.broadcast_to(row.astype(f32), (8, row.shape[1])).T[:, :1].astype(jnp.int32)


def twice(gain):
    return jnp.concatenate([gain, gain], axis=1)


def key_range(number):
    low = max(0, (number * BLOCK - (WINDOW - 1)) // BLOCK * BLOCK)
    return low, (number + 1) * BLOCK


def forward_kernel(
    x_ref, gain_ref, wq_ref, wk_ref, wv_ref, qg_ref, kg_ref, segr_ref, rate_ref, wo_ref,
    upper_ref, lower_ref, normed_ref, lin_ref, q_ref, k_ref, v_ref, mixed_ref, cos_ref, sin_ref, bias_ref, segc_ref,
):
    rows = x_ref.shape[0]
    segc_ref[...] = column(segr_ref[...])
    query_gain, key_gain = twice(qg_ref[...]), twice(kg_ref[...])
    q_pairs = wq_ref.shape[1] // LANES
    k_pairs = wk_ref.shape[1] // LANES
    blocks = rows // BLOCK
    ones = ones_by_head()

    def project(step, carry):
        at = pl.ds(pl.multiple_of(step * BLOCK, BLOCK), BLOCK)
        x = x_ref[at, :].astype(f32)
        scale = lax.rsqrt(jnp.mean(x * x, axis=-1, keepdims=True) + epsilon)
        normed = (x * scale * gain_ref[...]).astype(bf16)
        normed_ref[at, :] = normed
        begins = jnp.sum((segr_ref[...] < segc_ref[at, :]).astype(f32), axis=-1, keepdims=True)
        places = (step * BLOCK + lax.broadcasted_iota(jnp.int32, (BLOCK, 1), 0)).astype(f32)
        angles = (places - begins) * rate_ref[...]
        lane = lax.broadcasted_iota(jnp.int32, angles.shape, 1)
        cosine, sine = jnp.cos(angles), jnp.sin(angles)
        sine = jnp.where((lane & 63) < 32, -sine, sine)
        cos_ref[at, :] = cosine
        sin_ref[at, :] = sine

        def rotated(linear, gain):
            unit = linear * lax.rsqrt(head_sums(linear * linear, ones) * (1.0 / HEAD_DIM) + epsilon)
            scaled = unit * gain
            return scaled * cosine + swap_halves(scaled) * sine

        queries = mm(normed, wq_ref[...])
        lin_ref[at, : q_pairs * LANES] = queries
        for pair in range(q_pairs):
            part = queries[:, pair * LANES : (pair + 1) * LANES]
            q_ref[pair, at, :] = (rotated(part, query_gain).astype(bf16).astype(f32) * HEAD_DIM**-0.5).astype(bf16)
        keys = mm(normed, wk_ref[...])
        lin_ref[at, q_pairs * LANES :] = keys
        values = mm(normed, wv_ref[...])
        for pair in range(k_pairs):
            part = slice(pair * LANES, (pair + 1) * LANES)
            for ref, both in ((k_ref, rotated(keys[:, part], key_gain)), (v_ref, values[:, part])):
                other = pltpu.roll(both, 64, 1)
                first = first_head(both)
                ref[2 * pair, at, :] = jnp.where(first, both, other).astype(bf16)
                ref[2 * pair + 1, at, :] = jnp.where(first, other, both).astype(bf16)
        return carry

    lax.fori_loop(0, blocks, project, 0)

    for number in range(blocks):
        low, high = key_range(number)
        at = slice(number * BLOCK, (number + 1) * BLOCK)
        span = high - low
        row_ids = number * BLOCK + lax.broadcasted_iota(jnp.int32, (BLOCK, span), 0)
        col_ids = low + lax.broadcasted_iota(jnp.int32, (BLOCK, span), 1)
        allowed = (segc_ref[at, :] == segr_ref[:, low:high]) & (col_ids <= row_ids)
        bias = jnp.where(allowed, 0.0, masked_score)
        bias_ref[:BLOCK, :span] = bias
        bias_ref[BLOCK:, :span] = bias

        def head(pair, carry):
            stacked = stack_heads(q_ref[pair, at, :])
            scores = mm(stacked, k_ref[pair, low:high, :], NT)
            powers = jnp.exp(scores + bias_ref[:, :span])
            totals = jnp.sum(powers, axis=-1, keepdims=True)
            probs = (powers * (1.0 / totals)).astype(bf16)
            mixed = pick_heads(mm(probs, v_ref[pair, low:high, :]))
            lanes = pl.ds(pl.multiple_of(pair * LANES, LANES), LANES)
            mixed_ref[at, lanes] = mixed.astype(bf16)
            return carry

        lax.fori_loop(0, q_pairs, head, 0, unroll=True)
        half = upper_ref.shape[0]
        part_ref = upper_ref if number * BLOCK < half else lower_ref
        part_ref[number * BLOCK % half : number * BLOCK % half + BLOCK, :] = mm(mixed_ref[at, :], wo_ref[...], NT)


def backward_kernel(
    gb_ref, wo_ref, q_lin_ref, k_lin_ref, q_ref, k_ref, v_ref, qg_ref, kg_ref, cos_ref, sin_ref, segr_ref,
    gq_ref, gk_ref, gv_ref, gains_ref, bias_ref, gm_ref, dq_ref, dk_ref, dv_ref, segc_ref,
):
    rows = gb_ref.shape[0]
    segc_ref[...] = column(segr_ref[...])
    query_gain, key_gain = twice(qg_ref[...]), twice(kg_ref[...])
    q_pairs = q_ref.shape[0]
    k_pairs = q_pairs // 2
    blocks = rows // BLOCK
    ones = ones_by_head()

    mixed = mm(gb_ref[...], wo_ref[...]).astype(bf16)
    for pair in range(q_pairs):
        gm_ref[pair] = mixed[:, pair * LANES : (pair + 1) * LANES]

    for number in reversed(range(blocks)):
        low, high = key_range(number)
        at = slice(number * BLOCK, (number + 1) * BLOCK)
        span = high - low
        key_ids = low + lax.broadcasted_iota(jnp.int32, (span, BLOCK), 0)
        row_ids = number * BLOCK + lax.broadcasted_iota(jnp.int32, (span, BLOCK), 1)
        allowed = (segc_ref[low:high, :] == segr_ref[:, at]) & (key_ids <= row_ids)
        bias = jnp.where(allowed, 0.0, masked_score)
        bias_ref[:span, :BLOCK] = bias
        bias_ref[:span, BLOCK:] = bias
        fresh_from = 0 if number == blocks - 1 else key_range(number + 1)[0]

        def head(pair, carry):
            queries = stack_heads(q_ref[pair, at, :])
            grads = stack_heads(gm_ref[pair, at, :])
            keys = k_ref[pair, low:high, :]
            values = v_ref[pair, low:high, :]
            powers = jnp.exp(mm(keys, queries, NT) + bias_ref[:span, :])
            probs = powers * (1.0 / jnp.sum(powers, axis=0, keepdims=True))
            grad_probs = mm(values, grads, NT)
            center = jnp.sum(grad_probs * probs, axis=0, keepdims=True)
            grad_scores = (probs * (grad_probs - center)).astype(bf16)
            dq = lax.dot_general(grad_scores, keys, (((0,), (0,)), ((), ())), preferred_element_type=f32)
            dq_ref[pair, at, :] = pick_heads(dq) * HEAD_DIM**-0.5
            dk = mm(grad_scores, queries)
            dv = mm(probs.astype(bf16), grads)
            if number == blocks - 1:
                dk_ref[pair, low:high, :] = dk
                dv_ref[pair, low:high, :] = dv
            else:
                if low < fresh_from:
                    dk_ref[pair, low:fresh_from, :] = dk[: fresh_from - low]
                    dv_ref[pair, low:fresh_from, :] = dv[: fresh_from - low]
                start = max(low, fresh_from)
                dk_ref[pair, start:high, :] += dk[start - low :]
                dv_ref[pair, start:high, :] += dv[start - low :]
            return carry

        lax.fori_loop(0, q_pairs, head, 0, unroll=True)

    gains_ref[...] = jnp.zeros_like(gains_ref)

    def finish(step, carry):
        at = pl.ds(pl.multiple_of(step * BLOCK, BLOCK), BLOCK)
        cosine, sine = cos_ref[at, :], sin_ref[at, :]

        def linear_grad(grad, linear, gain, row):
            scale = lax.rsqrt(head_sums(linear * linear, ones) * (1.0 / HEAD_DIM) + epsilon)
            unit = linear * scale
            turned = grad * cosine - swap_halves(grad) * sine
            gains_ref[row : row + 1, :] += jnp.sum(turned * unit, axis=0, keepdims=True)
            inner = turned * gain
            return (scale * (inner - unit * (head_sums(inner * unit, ones) * (1.0 / HEAD_DIM)))).astype(bf16)

        for pair in range(q_pairs):
            lanes = slice(pair * LANES, (pair + 1) * LANES)
            gq_ref[at, lanes] = linear_grad(dq_ref[pair, at, :], q_lin_ref[at, lanes], query_gain, 0)
        for pair in range(k_pairs):
            lanes = slice(pair * LANES, (pair + 1) * LANES)

            def both(ref):
                one, two = ref[2 * pair, at, :], ref[2 * pair + 1, at, :]
                one = one + pltpu.roll(one, 64, 1)
                two = two + pltpu.roll(two, 64, 1)
                return jnp.where(first_head(one), one, two)

            gk_ref[at, lanes] = linear_grad(both(dk_ref), k_lin_ref[at, lanes], key_gain, 1)
            gv_ref[at, lanes] = both(dv_ref).astype(bf16)
        return carry

    lax.fori_loop(0, blocks, finish, 0)


PARAMS = pltpu.CompilerParams(vmem_limit_bytes=56 * 1024 * 1024)
SHARE = 1.0


def cost(time):
    return pl.CostEstimate(flops=int(time * SHARE * 1e9) + 1000, bytes_accessed=1000, transcendentals=0)


def call(kernel, outs, scratch, *operands):
    return pl.pallas_call(
        kernel, out_shape=outs, scratch_shapes=scratch, compiler_params=PARAMS, cost_estimate=cost(30)
    )(*operands)


def attention_forward(inputs, attn_gain, w_query, w_key, w_value, query_gain, key_gain, segment_ids, w_output):
    rows, width = inputs.shape
    q_width, k_width = w_query.shape[1], w_key.shape[1]
    pairs = q_width // LANES
    shape = jax.ShapeDtypeStruct
    outs = (
        shape((rows // 2, w_output.shape[0]), f32),
        shape((rows // 2, w_output.shape[0]), f32),
        shape((rows, width), bf16),
        shape((rows, q_width + k_width), f32),
        shape((pairs, rows, LANES), bf16),
        shape((pairs, rows, LANES), bf16),
        shape((pairs, rows, LANES), bf16),
        shape((rows, q_width), bf16),
        shape((rows, LANES), f32),
        shape((rows, LANES), f32),
    )
    span = min(rows, BLOCK + WINDOW)
    halves = HEAD_DIM // 2
    rates = rope_base ** (-2.0 * jnp.arange(halves, dtype=f32) / HEAD_DIM)
    return call(
        forward_kernel, outs, [pltpu.VMEM((2 * BLOCK, span), f32), pltpu.VMEM((rows, 1), jnp.int32)],
        inputs, attn_gain[None, :], w_query, w_key, w_value, query_gain[None, :], key_gain[None, :],
        segment_ids[None, :], jnp.concatenate([rates] * 4)[None, :], w_output,
    )


def attention_backward(
    k_pair, grad_branch, w_output, linear, query, key, value, query_gain, key_gain, tables, segment_ids
):
    rows, width = grad_branch.shape
    shape = jax.ShapeDtypeStruct
    outs = (
        shape((rows, 2 * LANES), bf16),
        shape((rows, LANES), bf16),
        shape((rows, LANES), bf16),
        shape((8, LANES), f32),
    )
    span = min(rows, BLOCK + WINDOW)
    scratch = [
        pltpu.VMEM((span, 2 * BLOCK), f32),
        pltpu.VMEM((2, rows, LANES), bf16),
        pltpu.VMEM((2, rows, LANES), f32),
        pltpu.VMEM((2, rows, LANES), f32),
        pltpu.VMEM((2, rows, LANES), f32),
        pltpu.VMEM((rows, 1), jnp.int32),
    ]
    heads = query.shape[0]

    def fixed(block, *place):
        return pl.BlockSpec(block, lambda step: place, pipeline_mode=pl.Buffered(1))

    pairs = fixed((2, rows, LANES), k_pair, 0, 0)
    small = fixed((1, HEAD_DIM), 0, 0)
    table = fixed((rows, LANES), 0, 0)
    return pl.pallas_call(
        backward_kernel,
        grid=(1,),
        in_specs=[
            fixed((rows, width), 0, 0), fixed((width, 2 * LANES), 0, k_pair),
            fixed((rows, 2 * LANES), 0, k_pair), fixed((rows, LANES), 0, heads + k_pair),
            pairs, pairs, pairs, small, small, table, table, fixed((1, rows), 0, 0),
        ],
        out_specs=tuple(fixed(item.shape, 0, 0) for item in outs),
        out_shape=outs,
        scratch_shapes=scratch,
        compiler_params=PARAMS,
        cost_estimate=cost(18),
    )(
        grad_branch, w_output, linear, linear, query, key, value, query_gain[None, :], key_gain[None, :],
        *tables, segment_ids[None, :],
    )


def whole(shape):
    return pl.BlockSpec(shape, lambda step: (0,) * len(shape), pipeline_mode=pl.Buffered(1))


SMEM_SPEC = pl.BlockSpec(memory_space=pltpu.SMEM)
VMEM_SPEC = pl.BlockSpec(memory_space=pltpu.VMEM)


def gridded(time, kernel, steps, in_specs, out_specs, outs, operands, scratch=()):
    return pl.pallas_call(
        kernel,
        grid=(steps,),
        in_specs=in_specs,
        out_specs=out_specs,
        out_shape=outs,
        scratch_shapes=list(scratch),
        compiler_params=PARAMS,
        cost_estimate=cost(time),
    )(*operands)


def turn(values, places, scratch, out):
    groups = places.shape[0]
    each = scratch.shape[0] // groups
    turned = values.astype(f32).T
    for group in range(groups):
        place = pl.ds(pl.multiple_of(places[group], 8), each)
        scratch[place, :] = turned[group * each : (group + 1) * each]
    out[...] = scratch[: out.shape[0], :].astype(bf16)


ROWS = 512


def widen_kernel(x_ref, out_ref):
    out_ref[...] = x_ref[...].astype(f32)


def widened(values):
    rows, width = values.shape
    by_rows = pl.BlockSpec((ROWS, width), lambda step: (step, 0))
    return gridded(
        4, widen_kernel, rows // ROWS, [by_rows], (by_rows,), (jax.ShapeDtypeStruct((rows, width), f32),), (values,)
    )[0]


def turn_kernel(places_ref, x_ref, *refs):
    *narrow_refs, out_ref, scratch = refs
    for ref in narrow_refs:
        ref[...] = x_ref[...].astype(bf16)
    turn(x_ref[...], places_ref, scratch, out_ref)


def turned(values, places, narrow=False, part=2):
    rows, width = values.shape
    shape = jax.ShapeDtypeStruct
    by_rows = pl.BlockSpec((ROWS, width), lambda step: (step, 0))
    outs = ((by_rows,), (shape((rows, width), bf16),)) if narrow else ((), ())
    return gridded(
        4, turn_kernel, rows // ROWS,
        [SMEM_SPEC, by_rows],
        outs[0] + (pl.BlockSpec((width // part, ROWS), lambda step: (0, step)),),
        outs[1] + (shape((width // part, rows), bf16),),
        (places, values), [pltpu.VMEM((width, ROWS), f32)],
    )


def of_halves(refs):
    if len(refs) == 2:
        return refs[0][...] + refs[1][...]
    early = pl.program_id(0) < pl.num_programs(0) // 2
    return jnp.where(early, refs[0][...] + refs[2][...], refs[1][...] + refs[3][...])


def half_specs(pieces, rows, width):
    steps = rows // ROWS
    if pieces == 2:
        return [pl.BlockSpec((ROWS, width), lambda step: (step, 0))] * 2
    upper = pl.BlockSpec((ROWS, width), lambda step: (jnp.minimum(step, steps // 2 - 1), 0))
    lower = pl.BlockSpec((ROWS, width), lambda step: (jnp.maximum(step - steps // 2, 0), 0))
    return [upper, lower, upper, lower]


def middle_kernel(x_ref, *refs):
    gain_ref, middle_ref, normed_ref, wide_ref = refs[-4:]
    middle = x_ref[...].astype(f32) + of_halves(refs[:-4])
    scale = lax.rsqrt(jnp.mean(middle * middle, axis=-1, keepdims=True) + epsilon)
    normed = (middle * scale * gain_ref[...]).astype(bf16)
    middle_ref[...] = middle
    normed_ref[...] = normed
    wide_ref[...] = normed.astype(f32)


def middle_norm(inputs, one, two, gain):
    rows, width = inputs.shape
    by_rows = pl.BlockSpec((ROWS, width), lambda step: (step, 0))
    shape = jax.ShapeDtypeStruct
    return gridded(
        10, middle_kernel, rows // ROWS,
        [by_rows] + half_specs(len(one) + len(two), rows, width) + [whole((1, width))],
        (by_rows,) * 3,
        (shape((rows, width), f32), shape((rows, width), bf16), shape((rows, width), f32)),
        (inputs, *one, *two, gain[None, :]),
    )


def norm_back_kernel(parts, value_ref, direct_ref, *refs):
    grad = of_halves(refs[:parts])
    gain_ref, *out_refs, gain_grad_ref = refs[parts:]
    value = value_ref[...].astype(f32)
    scale = lax.rsqrt(jnp.mean(value * value, axis=-1, keepdims=True) + epsilon)
    unit = value * scale
    inner = grad * gain_ref[...]
    total = direct_ref[...].astype(f32) + scale * (inner - unit * jnp.mean(inner * unit, axis=-1, keepdims=True))
    for ref in out_refs:
        ref[...] = total.astype(ref.dtype)

    @pl.when(pl.program_id(0) == 0)
    def _():
        gain_grad_ref[...] = jnp.zeros_like(gain_grad_ref)

    gain_grad_ref[...] += jnp.sum(grad * unit, axis=0, keepdims=True)


def norm_back(value, direct, one, two, gain, types):
    rows, width = value.shape
    steps = rows // ROWS
    by_rows = pl.BlockSpec((ROWS, width), lambda step: (step, 0))
    shape = jax.ShapeDtypeStruct
    return gridded(
        9, functools.partial(norm_back_kernel, len(one) + len(two)), steps,
        [by_rows, by_rows] + half_specs(len(one) + len(two), rows, width) + [whole((1, width))],
        (by_rows,) * len(types) + (pl.BlockSpec((1, width), lambda step: (0, 0)),),
        tuple(shape((rows, width), kind) for kind in types) + (shape((1, width), f32),),
        (value, direct, *one, *two, gain[None, :]),
    )


FBLOCK = 256


def unit_gradients(normed, cotangent, wg_ref, wu_ref, wd_ref):
    gate = mm(normed, wg_ref[...])
    upper = mm(normed, wu_ref[...])
    grad = mm(cotangent, wd_ref[...])
    share = 0.5 * jnp.tanh(0.5 * gate) + 0.5
    swish = gate * share
    return (
        (swish * upper).astype(bf16),
        (grad * upper * (share + swish * (1.0 - share))).astype(bf16),
        (grad * swish).astype(bf16),
    )


def units_kernel(normed_ref, cot_ref, wg_ref, wu_ref, wd_ref, hidden_ref, gg_ref, gu_ref):
    hidden_ref[...], gg_ref[...], gu_ref[...] = unit_gradients(normed_ref[...], cot_ref[...], wg_ref, wu_ref, wd_ref)


def ffn_units(normed, cotangent, w_gate, w_up, w_down):
    rows, width = normed.shape
    total = w_gate.shape[1]
    units = pl.BlockSpec((rows, FBLOCK), lambda step: (0, step))
    weights = pl.BlockSpec((width, FBLOCK), lambda step: (0, step))
    return gridded(
        21, units_kernel, total // FBLOCK,
        [whole((rows, width))] * 2 + [weights] * 3,
        (units,) * 3,
        (jax.ShapeDtypeStruct((rows, total), bf16),) * 3,
        (normed, cotangent, w_gate, w_up, w_down),
    )


def partner_kernel(
    wide_ref, cot_ref, cot_t_ref, own_t_ref, own_ref, wg_ref, wu_ref, wd_ref,
    gg_ref, gu_ref, keep_ref, send_ref, normed_ref,
):
    half = keep_ref.shape[0]

    @pl.when(pl.program_id(0) == 0)
    def _():
        normed_ref[...] = wide_ref[...].astype(bf16)

    hidden, gg_ref[...], gu_ref[...] = unit_gradients(normed_ref[...], cot_ref[...], wg_ref, wu_ref, wd_ref)
    total = mm(own_t_ref[...], own_ref[...]) + mm(cot_t_ref[...], hidden)
    keep_ref[...] = total[:half]
    send_ref[...] = total[half:]


def partner_units(normed, cotangent, cotangent_t, own_t, own_hidden, w_gate, w_up, w_down):
    rows, width = normed.shape
    total = w_gate.shape[1]
    units = pl.BlockSpec((rows, FBLOCK), lambda step: (0, step))
    weights = pl.BlockSpec((width, FBLOCK), lambda step: (0, step))
    grads = pl.BlockSpec((width // 4, FBLOCK), lambda step: (0, step))
    shape = jax.ShapeDtypeStruct
    return gridded(
        27, partner_kernel, total // FBLOCK,
        [whole((rows, width))] * 2 + [whole((width // 2, rows))] * 2 + [units] + [weights] * 3,
        (units,) * 2 + (grads,) * 2,
        (shape((rows, total), bf16),) * 2 + (shape((width // 4, total), f32),) * 2,
        (normed, cotangent, cotangent_t, own_t, own_hidden, w_gate, w_up, w_down),
        [pltpu.VMEM((rows, width), bf16)],
    )


def pair_kernel(one_t_ref, two_t_ref, one_ref, two_ref, keep_ref, send_ref):
    half = keep_ref.shape[0]
    total = mm(one_t_ref[...], one_ref[...]) + mm(two_t_ref[...], two_ref[...])
    keep_ref[...] = total[:half]
    send_ref[...] = total[half:]


def pair_weights(one_t, two_t, one, two):
    half, rows = one_t.shape
    total = one.shape[1]
    block = 3 * FBLOCK
    units = pl.BlockSpec((rows, block), lambda step: (0, step))
    grads = pl.BlockSpec((half // 2, block), lambda step: (0, step))
    return gridded(
        10, pair_kernel, total // block,
        [whole((half, rows))] * 2 + [units] * 2, (grads,) * 2,
        (jax.ShapeDtypeStruct((half // 2, total), f32),) * 2, (one_t, two_t, one, two),
    )


def products_kernel(count, *refs):
    lefts, rights, outs = refs[:count], refs[count : 2 * count], refs[2 * count :]
    total = mm(lefts[0][...], rights[0][...], NT)
    for left, right in zip(lefts[1:], rights[1:]):
        total += mm(left[...], right[...], NT)
    each = total.shape[0] // len(outs)
    for number, ref in enumerate(outs):
        ref[...] = total[number * each : (number + 1) * each]


def products(lefts, rights, pieces, time=12):
    rows, columns = lefts[0].shape[0], rights[0].shape[0]
    out = pl.BlockSpec((rows // pieces, BLOCK), lambda step: (0, step))
    return gridded(
        time, functools.partial(products_kernel, len(lefts)), columns // BLOCK,
        [whole(item.shape) for item in lefts]
        + [pl.BlockSpec((BLOCK, item.shape[1]), lambda step: (step, 0)) for item in rights],
        (out,) * pieces, (jax.ShapeDtypeStruct((rows // pieces, columns), f32),) * pieces, tuple(lefts) + tuple(rights),
    )


def join_kernel(middle_ref, *refs):
    refs[-1][...] = (middle_ref[...] + of_halves(refs[:-1])).astype(bf16)


def joined(middle, one, two):
    rows, width = middle.shape
    by_rows = pl.BlockSpec((ROWS, width), lambda step: (step, 0))
    return gridded(
        7, join_kernel, rows // ROWS,
        [by_rows] + half_specs(len(one) + len(two), rows, width), (by_rows,),
        (jax.ShapeDtypeStruct((rows, width), bf16),), (middle, *one, *two),
    )[0]


def stacked_kernel(left_ref, *refs):
    rights, (keep_ref, send_ref) = refs[:-2], refs[-2:]
    half = keep_ref.shape[0]
    low = 0
    for right in rights:
        high = low + right.shape[1]
        total = mm(left_ref[...], right[...])
        keep_ref[:, low:high] = total[:half]
        send_ref[:, low:high] = total[half:]
        low = high


def stacked_weights(left_t, rights):
    width = left_t.shape[0]
    total = sum(item.shape[1] for item in rights)
    return pl.pallas_call(
        stacked_kernel,
        out_shape=(jax.ShapeDtypeStruct((width // 2, total), f32),) * 2,
        in_specs=[VMEM_SPEC] * (1 + len(rights)),
        out_specs=(VMEM_SPEC,) * 2,
        compiler_params=PARAMS,
        cost_estimate=cost(6),
    )(left_t, *rights)


def turned_kernel(places_ref, left_ref, *refs):
    rights, (keep_ref, send_ref, scratch, turned_ref) = refs[:-4], refs[-4:]
    half = keep_ref.shape[0]
    turn(left_ref[...], places_ref, scratch, turned_ref)
    low = 0
    for right in rights:
        high = low + right.shape[1]
        send_ref[:, low:high] = mm(turned_ref[half:, :], right[...])
        keep_ref[:, low:high] = mm(turned_ref[:half, :], right[...])
        low = high


def turned_weights(places, left, rights, time=6):
    rows, width = left.shape
    total = sum(item.shape[1] for item in rights)
    return pl.pallas_call(
        turned_kernel,
        out_shape=(jax.ShapeDtypeStruct((width // 2, total), f32),) * 2,
        in_specs=[SMEM_SPEC] + [VMEM_SPEC] * (1 + len(rights)),
        out_specs=(VMEM_SPEC,) * 2,
        scratch_shapes=[pltpu.VMEM((width, rows), f32), pltpu.VMEM((width, rows), bf16)],
        compiler_params=PARAMS,
        cost_estimate=cost(time),
    )(places, left, *rights)


def swap(values):
    return lax.ppermute(values, "tensor", [(0, 1), (1, 0)])


LABELS = ((0, 1, 2), (2, 0, 1))
DOWN_LABELS = ((0, 1, 2), (2, 0, 1))
LATE_LABELS = ((0, 1, 2), (2, 0, 1))


class Layout:
    def __init__(self, rows, labels):
        self.labels = labels
        self.devices = lax.axis_size("dp")
        self.bits = self.devices.bit_length() - 1
        core = lax.axis_index("tensor")
        self.mine = self.label(lax.axis_index("dp"), core)
        numbers = self.label(jnp.arange(self.devices, dtype=jnp.int32), core)
        each = rows // self.devices
        first = (numbers & 1) ^ self.bit(0)
        second = ((numbers >> 1) & 1) ^ self.bit(1)
        self.halves = (first * (self.devices // 2) + (numbers >> 1)) * each
        self.quarters = (first * (self.devices // 2) + second * (self.devices // 4) + (numbers >> 2)) * each

    def label(self, number, core):
        first, second = (
            (number & ~7) | functools.reduce(jnp.bitwise_or, [((number >> self.labels[one][bit]) & 1) << bit for bit in range(3)])
            for one in range(2)
        )
        return jnp.where(core == 1, second, first).astype(jnp.int32)

    def bit(self, bit):
        return (self.mine >> bit) & 1

    def exchange(self, values, bit):
        own = [self.labels[core][bit] if bit < 3 else bit for core in range(2)]
        pairs = [(2 * i + core, 2 * (i ^ (1 << own[core])) + core) for i in range(self.devices) for core in range(2)]
        return lax.ppermute(values, ("dp", "tensor"), pairs)


class Scatter:
    def __init__(self, layout, keep, send, first):
        self.layout = layout
        self.stage = first
        self.left = list(range(layout.bits - 1, first, -1))
        self.addends = [self.spread(keep)]
        self.send = self.spread(send)

    def spread(self, values):
        return values.reshape((2,) * len(self.left) + (-1, values.shape[1]))

    def exchange(self):
        self.addends.append(self.layout.exchange(self.send, self.stage))
        self.stage += 1

    def prepare(self, earlier=None):
        mine = self.layout.bit(self.stage)
        axis = self.left.index(self.stage)
        if earlier is not None:
            self.addends[-1] = after(self.addends[-1], earlier)

        def take(array, which):
            return lax.dynamic_index_in_dim(array, which, axis, keepdims=False)

        self.send = functools.reduce(jnp.add, [take(item, 1 - mine) for item in self.addends])
        self.addends = [take(item, mine) for item in self.addends]
        self.left.remove(self.stage)
        self.exchange()
        return self.send

    def result(self):
        return functools.reduce(jnp.add, self.addends)


def finish(scatter, earlier):
    while scatter.stage < scatter.layout.bits:
        earlier = scatter.prepare(earlier)
    scatter.addends[-1] = after(scatter.addends[-1], earlier)
    total = scatter.result()
    return total, total


def after(values, earlier):
    return lax.optimization_barrier((values, earlier))[0]


def per_device(
    inputs,
    cotangent,
    segment_ids,
    attn_gain,
    w_query,
    w_key,
    w_value,
    query_gain,
    key_gain,
    w_output,
    ffn_gain,
    w_gate,
    w_up,
    w_down,
):
    width = inputs.shape[1]
    units = w_gate.shape[1]
    layout = Layout(width, LABELS)
    layout_down = Layout(width, DOWN_LABELS)
    layout_late = Layout(width, LATE_LABELS)
    devices, bits = layout.devices, layout.bits
    each = width // devices
    me = lax.axis_index("dp")

    cotangent_wide = widened(cotangent)
    cotangent_far = layout.exchange(cotangent_wide, 0)
    *part, normed, linear, query, key, value, mixed, cosine, sine = attention_forward(
        after(inputs, cotangent_wide), attn_gain, w_query, w_key, w_value, query_gain, key_gain, segment_ids, w_output
    )
    part_swapped = [swap(item) for item in part]
    (cotangent_t,) = turned(after(cotangent, normed), layout_down.quarters)
    middle, normed_two, normed_wide = middle_norm(inputs, after(part, cotangent_t), part_swapped, ffn_gain)
    (normed_t,) = turned(after(normed, normed_wide), layout_late.halves, part=1)
    normed_far = layout.exchange(after(normed_wide, (cotangent_far, normed_t)), 0)
    hidden, gg, gu = ffn_units(after(normed_two, normed_wide), cotangent, w_gate, w_up, w_down)
    cotangent_far, cotangent_far_t = turned(after(cotangent_far, hidden), layout_down.quarters, True)
    grad_two = products((after(gg, cotangent_far_t), gu), (w_gate, w_up), 2)
    grad_two_swapped = [swap(item) for item in grad_two]
    (normed_two_t,) = turned(after(normed_two, grad_two), layout.quarters)
    far_gg, far_gu, keep, send = partner_units(
        after(normed_far, normed_two_t), cotangent_far, cotangent_far_t, cotangent_t, hidden, w_gate, w_up, w_down
    )
    down = Scatter(layout_down, keep, send, 1)
    down.exchange()
    (normed_far_t,) = turned(after(normed_far, send), layout.quarters)
    gate = Scatter(layout, *pair_weights(normed_two_t, normed_far_t, gg, far_gg), 1)
    gate.exchange()
    upper = Scatter(layout, *pair_weights(after(normed_two_t, gate.send), normed_far_t, gu, far_gu), 1)
    upper.exchange()
    grad_middle, grad_branch, grad_ffn_gain = norm_back(
        after(middle, upper.send), cotangent, grad_two, grad_two_swapped, ffn_gain, (f32, bf16)
    )
    token = down.prepare(grad_branch)

    def heads_back(k_pair, token):
        return attention_backward(
            k_pair, after(grad_branch, token), w_output, linear, query, key, value, query_gain, key_gain,
            (cosine, sine), segment_ids,
        )

    back = [heads_back(0, token)]
    ffn = products((after(hidden, back[0]),), (w_down,), 1)
    token = gate.prepare(ffn)
    token = down.prepare(token)
    for k_pair in range(1, w_key.shape[1] // LANES):
        back.append(heads_back(k_pair, token))
        token = back[-1]
    gq, gk, gv, gains = zip(*back)
    gains = sum(gains)
    three = Scatter(layout_late, *stacked_weights(normed_t, gq + gk + gv), 0)
    three.exchange()
    sum_down, token = finish(down, three.send)
    w_parts = [
        weight[:, at : at + piece.shape[1]]
        for weight, pieces in ((w_query, gq), (w_key, gk), (w_value, gv))
        for piece, at in zip(pieces, range(0, weight.shape[1], pieces[0].shape[1]))
    ]
    grad_one = products((after(gq[0], token),) + gq[1:] + gk + gv, w_parts, 1)
    grad_one_swapped = [swap(item) for item in grad_one]
    token = gate.prepare(grad_one)
    output = Scatter(layout_late, *turned_weights(layout_late.halves, after(grad_branch, token), (mixed,), 60), 0)
    output.exchange()
    token = upper.prepare(output.send)
    token = three.prepare(token)
    grad_inputs, grad_attn_gain = norm_back(
        inputs, after(grad_middle, token), grad_one, grad_one_swapped, attn_gain, (bf16,)
    )
    small = jnp.concatenate(
        [
            grad_attn_gain.reshape(-1, LANES) * 0.5,
            grad_ffn_gain.reshape(-1, LANES) * 0.5,
            jnp.pad(gains[:2, :HEAD_DIM] + gains[:2, HEAD_DIM:], ((0, 6), (0, LANES - HEAD_DIM))),
        ]
    )
    small_far = swap(small)
    sum_gate, token = finish(gate, small)
    token = three.prepare(token)
    token = upper.prepare(token)
    token = output.prepare(token)
    small = small + after(small_far, token)
    small_far = layout.exchange(small, 0)
    ffn_swapped = [swap(after(item, small)) for item in ffn]
    token = three.prepare(small)
    token = output.prepare(token)
    small = small + after(small_far, token)
    small_far = layout.exchange(small, 1)
    block_out = joined(after(middle, small), ffn, ffn_swapped)
    token = output.prepare(block_out)
    small = small + after(small_far, token)
    small_far = layout.exchange(small, 2)
    sum_upper, token = finish(upper, small)
    sum_output, token = finish(output, token)
    small = small + after(small_far, token)
    for bit in range(3, bits):
        small = small + layout.exchange(small, bit)
    sum_three, token = finish(three, token)
    lines = width // LANES
    sum_attn_gain = lax.dynamic_slice_in_dim(small[:lines].reshape(width), me * each, each)
    sum_ffn_gain = lax.dynamic_slice_in_dim(small[lines : 2 * lines].reshape(width), me * each, each)

    q_width, k_width = w_query.shape[1], w_key.shape[1]
    return (
        block_out,
        grad_inputs,
        sum_attn_gain,
        sum_three[:, :q_width],
        sum_three[:, q_width : q_width + k_width],
        sum_three[:, q_width + k_width :],
        small[2 * lines, :HEAD_DIM],
        small[2 * lines + 1, :HEAD_DIM],
        sum_output,
        sum_ffn_gain,
        sum_gate,
        sum_upper,
        sum_down,
    )


def solution(mesh):
    placed = (
        P("dp", None),
        P("dp", None),
        P("dp"),
        P(),
        P(None, "tensor"),
        P(None, "tensor"),
        P(None, "tensor"),
        P(),
        P(),
        P(None, "tensor"),
        P(),
        P(None, "tensor"),
        P(None, "tensor"),
        P(None, "tensor"),
    )
    return jax.shard_map(
        per_device,
        mesh=mesh,
        in_specs=placed,
        out_specs=(
            P("dp", None),
            P("dp", None),
            P("dp"),
            P("dp", "tensor"),
            P("dp", "tensor"),
            P("dp", "tensor"),
            P(),
            P(),
            P("dp", "tensor"),
            P("dp"),
            P("dp", "tensor"),
            P("dp", "tensor"),
            P("dp", "tensor"),
        ),
        check_vma=False,
    )
```

```python
import functools

import jax
import jax.numpy as jnp
from jax import lax
from jax.experimental import pallas as pl
from jax.experimental.pallas import tpu as pltpu
from jax.sharding import PartitionSpec as P

HEAD_DIM = 64
LANES = 128
WINDOW = 512
BLOCK = 256
epsilon = 1e-05
rope_base = 1000000.0
masked_score = -1e30
f32 = jnp.float32
bf16 = jnp.bfloat16
NN = (((1,), (0,)), ((), ()))
NT = (((1,), (1,)), ((), ()))


def mm(left, right, dims=NN):
    return lax.dot_general(left, right, dims, preferred_element_type=f32)


def ones_by_head():
    row = lax.broadcasted_iota(jnp.int32, (LANES, LANES), 0)
    col = lax.broadcasted_iota(jnp.int32, (LANES, LANES), 1)
    return jnp.where((row >> 6) == (col >> 6), 1.0, 0.0).astype(bf16)


def head_sums(values, ones):
    high = values.astype(bf16)
    rest = (values - high.astype(f32)).astype(bf16)
    return mm(high, ones) + mm(rest, ones)


def swap_halves(values):
    lane = lax.broadcasted_iota(jnp.int32, values.shape, 1)
    return jnp.where((lane & 63) < 32, pltpu.roll(values, 96, 1), pltpu.roll(values, 32, 1))


def first_head(values):
    return lax.broadcasted_iota(jnp.int32, values.shape, 1) < 64


def stack_heads(pair):
    first = first_head(pair)
    zero = jnp.zeros_like(pair)
    return jnp.concatenate([jnp.where(first, pair, zero), jnp.where(first, zero, pair)], axis=0)


def pick_heads(stacked):
    rows = stacked.shape[0] // 2
    top = stacked[:rows]
    return jnp.where(first_head(top), top, stacked[rows:])


def column(row):
    return jnp.broadcast_to(row.astype(f32), (8, row.shape[1])).T[:, :1].astype(jnp.int32)


def twice(gain):
    return jnp.concatenate([gain, gain], axis=1)


def key_range(number):
    low = max(0, (number * BLOCK - (WINDOW - 1)) // BLOCK * BLOCK)
    return low, (number + 1) * BLOCK


def forward_kernel(
    x_ref, gain_ref, wq_ref, wk_ref, wv_ref, qg_ref, kg_ref, segr_ref, rate_ref, wo_ref,
    upper_ref, lower_ref, normed_ref, lin_ref, q_ref, k_ref, v_ref, mixed_ref, cos_ref, sin_ref, bias_ref, segc_ref,
):
    rows = x_ref.shape[0]
    segc_ref[...] = column(segr_ref[...])
    query_gain, key_gain = twice(qg_ref[...]), twice(kg_ref[...])
    q_pairs = wq_ref.shape[1] // LANES
    k_pairs = wk_ref.shape[1] // LANES
    blocks = rows // BLOCK
    ones = ones_by_head()

    def project(step, carry):
        at = pl.ds(pl.multiple_of(step * BLOCK, BLOCK), BLOCK)
        x = x_ref[at, :].astype(f32)
        scale = lax.rsqrt(jnp.mean(x * x, axis=-1, keepdims=True) + epsilon)
        normed = (x * scale * gain_ref[...]).astype(bf16)
        normed_ref[at, :] = normed
        begins = jnp.sum((segr_ref[...] < segc_ref[at, :]).astype(f32), axis=-1, keepdims=True)
        places = (step * BLOCK + lax.broadcasted_iota(jnp.int32, (BLOCK, 1), 0)).astype(f32)
        angles = (places - begins) * rate_ref[...]
        lane = lax.broadcasted_iota(jnp.int32, angles.shape, 1)
        cosine, sine = jnp.cos(angles), jnp.sin(angles)
        sine = jnp.where((lane & 63) < 32, -sine, sine)
        cos_ref[at, :] = cosine
        sin_ref[at, :] = sine

        def rotated(linear, gain):
            unit = linear * lax.rsqrt(head_sums(linear * linear, ones) * (1.0 / HEAD_DIM) + epsilon)
            scaled = unit * gain
            return scaled * cosine + swap_halves(scaled) * sine

        queries = mm(normed, wq_ref[...])
        lin_ref[at, : q_pairs * LANES] = queries
        for pair in range(q_pairs):
            part = queries[:, pair * LANES : (pair + 1) * LANES]
            q_ref[pair, at, :] = (rotated(part, query_gain).astype(bf16).astype(f32) * HEAD_DIM**-0.5).astype(bf16)
        keys = mm(normed, wk_ref[...])
        lin_ref[at, q_pairs * LANES :] = keys
        values = mm(normed, wv_ref[...])
        for pair in range(k_pairs):
            part = slice(pair * LANES, (pair + 1) * LANES)
            for ref, both in ((k_ref, rotated(keys[:, part], key_gain)), (v_ref, values[:, part])):
                other = pltpu.roll(both, 64, 1)
                first = first_head(both)
                ref[2 * pair, at, :] = jnp.where(first, both, other).astype(bf16)
                ref[2 * pair + 1, at, :] = jnp.where(first, other, both).astype(bf16)
        return carry

    lax.fori_loop(0, blocks, project, 0, unroll=True)

    for number in range(blocks):
        low, high = key_range(number)
        at = slice(number * BLOCK, (number + 1) * BLOCK)
        span = high - low
        row_ids = number * BLOCK + lax.broadcasted_iota(jnp.int32, (BLOCK, span), 0)
        col_ids = low + lax.broadcasted_iota(jnp.int32, (BLOCK, span), 1)
        allowed = (segc_ref[at, :] == segr_ref[:, low:high]) & (col_ids <= row_ids)
        bias = jnp.where(allowed, 0.0, masked_score)
        bias_ref[:BLOCK, :span] = bias
        bias_ref[BLOCK:, :span] = bias

        def head(pair, carry):
            stacked = stack_heads(q_ref[pair, at, :])
            scores = mm(stacked, k_ref[pair, low:high, :], NT)
            powers = jnp.exp(scores + bias_ref[:, :span])
            totals = jnp.sum(powers, axis=-1, keepdims=True)
            probs = (powers * (1.0 / totals)).astype(bf16)
            mixed = pick_heads(mm(probs, v_ref[pair, low:high, :]))
            lanes = pl.ds(pl.multiple_of(pair * LANES, LANES), LANES)
            mixed_ref[at, lanes] = mixed.astype(bf16)
            return carry

        lax.fori_loop(0, q_pairs, head, 0, unroll=True)
        half = upper_ref.shape[0]
        part_ref = upper_ref if number * BLOCK < half else lower_ref
        part_ref[number * BLOCK % half : number * BLOCK % half + BLOCK, :] = mm(mixed_ref[at, :], wo_ref[...], NT)


def backward_kernel(
    gb_ref, wo_ref, q_lin_ref, k_lin_ref, q_ref, k_ref, v_ref, qg_ref, kg_ref, cos_ref, sin_ref, segr_ref,
    gq_ref, gk_ref, gv_ref, gains_ref, bias_ref, gm_ref, dq_ref, dk_ref, dv_ref, segc_ref,
):
    rows = gb_ref.shape[0]
    segc_ref[...] = column(segr_ref[...])
    query_gain, key_gain = twice(qg_ref[...]), twice(kg_ref[...])
    q_pairs = q_ref.shape[0]
    k_pairs = q_pairs // 2
    blocks = rows // BLOCK
    ones = ones_by_head()

    mixed = mm(gb_ref[...], wo_ref[...]).astype(bf16)
    for pair in range(q_pairs):
        gm_ref[pair] = mixed[:, pair * LANES : (pair + 1) * LANES]

    for number in reversed(range(blocks)):
        low, high = key_range(number)
        at = slice(number * BLOCK, (number + 1) * BLOCK)
        span = high - low
        key_ids = low + lax.broadcasted_iota(jnp.int32, (span, BLOCK), 0)
        row_ids = number * BLOCK + lax.broadcasted_iota(jnp.int32, (span, BLOCK), 1)
        allowed = (segc_ref[low:high, :] == segr_ref[:, at]) & (key_ids <= row_ids)
        bias = jnp.where(allowed, 0.0, masked_score)
        bias_ref[:span, :BLOCK] = bias
        bias_ref[:span, BLOCK:] = bias
        fresh_from = 0 if number == blocks - 1 else key_range(number + 1)[0]

        def head(pair, carry):
            queries = stack_heads(q_ref[pair, at, :])
            grads = stack_heads(gm_ref[pair, at, :])
            keys = k_ref[pair, low:high, :]
            values = v_ref[pair, low:high, :]
            powers = jnp.exp(mm(keys, queries, NT) + bias_ref[:span, :])
            probs = powers * (1.0 / jnp.sum(powers, axis=0, keepdims=True))
            grad_probs = mm(values, grads, NT)
            center = jnp.sum(grad_probs * probs, axis=0, keepdims=True)
            grad_scores = (probs * (grad_probs - center)).astype(bf16)
            dq = lax.dot_general(grad_scores, keys, (((0,), (0,)), ((), ())), preferred_element_type=f32)
            dq_ref[pair, at, :] = pick_heads(dq) * HEAD_DIM**-0.5
            dk = mm(grad_scores, queries)
            dv = mm(probs.astype(bf16), grads)
            if number == blocks - 1:
                dk_ref[pair, low:high, :] = dk
                dv_ref[pair, low:high, :] = dv
            else:
                if low < fresh_from:
                    dk_ref[pair, low:fresh_from, :] = dk[: fresh_from - low]
                    dv_ref[pair, low:fresh_from, :] = dv[: fresh_from - low]
                start = max(low, fresh_from)
                dk_ref[pair, start:high, :] += dk[start - low :]
                dv_ref[pair, start:high, :] += dv[start - low :]
            return carry

        lax.fori_loop(0, q_pairs, head, 0, unroll=True)

    gains_ref[...] = jnp.zeros_like(gains_ref)

    def finish(step, carry):
        at = pl.ds(pl.multiple_of(step * BLOCK, BLOCK), BLOCK)
        cosine, sine = cos_ref[at, :], sin_ref[at, :]

        def linear_grad(grad, linear, gain, row):
            scale = lax.rsqrt(head_sums(linear * linear, ones) * (1.0 / HEAD_DIM) + epsilon)
            unit = linear * scale
            turned = grad * cosine - swap_halves(grad) * sine
            gains_ref[row : row + 1, :] += jnp.sum(turned * unit, axis=0, keepdims=True)
            inner = turned * gain
            return (scale * (inner - unit * (head_sums(inner * unit, ones) * (1.0 / HEAD_DIM)))).astype(bf16)

        for pair in range(q_pairs):
            lanes = slice(pair * LANES, (pair + 1) * LANES)
            gq_ref[at, lanes] = linear_grad(dq_ref[pair, at, :], q_lin_ref[at, lanes], query_gain, 0)
        for pair in range(k_pairs):
            lanes = slice(pair * LANES, (pair + 1) * LANES)

            def both(ref):
                one, two = ref[2 * pair, at, :], ref[2 * pair + 1, at, :]
                one = one + pltpu.roll(one, 64, 1)
                two = two + pltpu.roll(two, 64, 1)
                return jnp.where(first_head(one), one, two)

            gk_ref[at, lanes] = linear_grad(both(dk_ref), k_lin_ref[at, lanes], key_gain, 1)
            gv_ref[at, lanes] = both(dv_ref).astype(bf16)
        return carry

    lax.fori_loop(0, blocks, finish, 0, unroll=True)


PARAMS = pltpu.CompilerParams(vmem_limit_bytes=56 * 1024 * 1024)
SHARE = 1.0


def cost(time):
    return pl.CostEstimate(flops=int(time * SHARE * 1e9) + 1000, bytes_accessed=1000, transcendentals=0)


def call(kernel, outs, scratch, *operands):
    return pl.pallas_call(
        kernel, out_shape=outs, scratch_shapes=scratch, compiler_params=PARAMS, cost_estimate=cost(30)
    )(*operands)


def attention_forward(inputs, attn_gain, w_query, w_key, w_value, query_gain, key_gain, segment_ids, w_output):
    rows, width = inputs.shape
    q_width, k_width = w_query.shape[1], w_key.shape[1]
    pairs = q_width // LANES
    shape = jax.ShapeDtypeStruct
    outs = (
        shape((rows // 2, w_output.shape[0]), f32),
        shape((rows // 2, w_output.shape[0]), f32),
        shape((rows, width), bf16),
        shape((rows, q_width + k_width), f32),
        shape((pairs, rows, LANES), bf16),
        shape((pairs, rows, LANES), bf16),
        shape((pairs, rows, LANES), bf16),
        shape((rows, q_width), bf16),
        shape((rows, LANES), f32),
        shape((rows, LANES), f32),
    )
    span = min(rows, BLOCK + WINDOW)
    halves = HEAD_DIM // 2
    rates = rope_base ** (-2.0 * jnp.arange(halves, dtype=f32) / HEAD_DIM)
    return call(
        forward_kernel, outs, [pltpu.VMEM((2 * BLOCK, span), f32), pltpu.VMEM((rows, 1), jnp.int32)],
        inputs, attn_gain[None, :], w_query, w_key, w_value, query_gain[None, :], key_gain[None, :],
        segment_ids[None, :], jnp.concatenate([rates] * 4)[None, :], w_output,
    )


def attention_backward(
    k_pair, grad_branch, w_output, linear, query, key, value, query_gain, key_gain, tables, segment_ids
):
    rows, width = grad_branch.shape
    shape = jax.ShapeDtypeStruct
    outs = (
        shape((rows, 2 * LANES), bf16),
        shape((rows, LANES), bf16),
        shape((rows, LANES), bf16),
        shape((8, LANES), f32),
    )
    span = min(rows, BLOCK + WINDOW)
    scratch = [
        pltpu.VMEM((span, 2 * BLOCK), f32),
        pltpu.VMEM((2, rows, LANES), bf16),
        pltpu.VMEM((2, rows, LANES), f32),
        pltpu.VMEM((2, rows, LANES), f32),
        pltpu.VMEM((2, rows, LANES), f32),
        pltpu.VMEM((rows, 1), jnp.int32),
    ]
    heads = query.shape[0]

    def fixed(block, *place):
        return pl.BlockSpec(block, lambda step: place, pipeline_mode=pl.Buffered(1))

    pairs = fixed((2, rows, LANES), k_pair, 0, 0)
    small = fixed((1, HEAD_DIM), 0, 0)
    table = fixed((rows, LANES), 0, 0)
    return pl.pallas_call(
        backward_kernel,
        grid=(1,),
        in_specs=[
            fixed((rows, width), 0, 0), fixed((width, 2 * LANES), 0, k_pair),
            fixed((rows, 2 * LANES), 0, k_pair), fixed((rows, LANES), 0, heads + k_pair),
            pairs, pairs, pairs, small, small, table, table, fixed((1, rows), 0, 0),
        ],
        out_specs=tuple(fixed(item.shape, 0, 0) for item in outs),
        out_shape=outs,
        scratch_shapes=scratch,
        compiler_params=PARAMS,
        cost_estimate=cost(18),
    )(
        grad_branch, w_output, linear, linear, query, key, value, query_gain[None, :], key_gain[None, :],
        *tables, segment_ids[None, :],
    )


def whole(shape):
    return pl.BlockSpec(shape, lambda step: (0,) * len(shape), pipeline_mode=pl.Buffered(1))


SMEM_SPEC = pl.BlockSpec(memory_space=pltpu.SMEM)
VMEM_SPEC = pl.BlockSpec(memory_space=pltpu.VMEM)


def gridded(time, kernel, steps, in_specs, out_specs, outs, operands, scratch=()):
    return pl.pallas_call(
        kernel,
        grid=(steps,),
        in_specs=in_specs,
        out_specs=out_specs,
        out_shape=outs,
        scratch_shapes=list(scratch),
        compiler_params=PARAMS,
        cost_estimate=cost(time),
    )(*operands)


def turn(values, places, scratch, out):
    groups = places.shape[0]
    each = scratch.shape[0] // groups
    turned = values.astype(f32).T
    for group in range(groups):
        place = pl.ds(pl.multiple_of(places[group], 8), each)
        scratch[place, :] = turned[group * each : (group + 1) * each]
    out[...] = scratch[: out.shape[0], :].astype(bf16)


ROWS = 512


def widen_kernel(x_ref, out_ref):
    out_ref[...] = x_ref[...].astype(f32)


def widened(values):
    rows, width = values.shape
    by_rows = pl.BlockSpec((ROWS, width), lambda step: (step, 0))
    return gridded(
        4, widen_kernel, rows // ROWS, [by_rows], (by_rows,), (jax.ShapeDtypeStruct((rows, width), f32),), (values,)
    )[0]


def turn_kernel(places_ref, x_ref, *refs):
    *narrow_refs, out_ref, scratch = refs
    for ref in narrow_refs:
        ref[...] = x_ref[...].astype(bf16)
    turn(x_ref[...], places_ref, scratch, out_ref)


def turned(values, places, narrow=False, part=2):
    rows, width = values.shape
    shape = jax.ShapeDtypeStruct
    by_rows = pl.BlockSpec((ROWS, width), lambda step: (step, 0))
    outs = ((by_rows,), (shape((rows, width), bf16),)) if narrow else ((), ())
    return gridded(
        4, turn_kernel, rows // ROWS,
        [SMEM_SPEC, by_rows],
        outs[0] + (pl.BlockSpec((width // part, ROWS), lambda step: (0, step)),),
        outs[1] + (shape((width // part, rows), bf16),),
        (places, values), [pltpu.VMEM((width, ROWS), f32)],
    )


def of_halves(refs):
    if len(refs) == 2:
        return refs[0][...] + refs[1][...]
    early = pl.program_id(0) < pl.num_programs(0) // 2
    return jnp.where(early, refs[0][...] + refs[2][...], refs[1][...] + refs[3][...])


def half_specs(pieces, rows, width):
    steps = rows // ROWS
    if pieces == 2:
        return [pl.BlockSpec((ROWS, width), lambda step: (step, 0))] * 2
    upper = pl.BlockSpec((ROWS, width), lambda step: (jnp.minimum(step, steps // 2 - 1), 0))
    lower = pl.BlockSpec((ROWS, width), lambda step: (jnp.maximum(step - steps // 2, 0), 0))
    return [upper, lower, upper, lower]


def middle_kernel(x_ref, *refs):
    gain_ref, middle_ref, normed_ref, wide_ref = refs[-4:]
    middle = x_ref[...].astype(f32) + of_halves(refs[:-4])
    scale = lax.rsqrt(jnp.mean(middle * middle, axis=-1, keepdims=True) + epsilon)
    normed = (middle * scale * gain_ref[...]).astype(bf16)
    middle_ref[...] = middle
    normed_ref[...] = normed
    wide_ref[...] = normed.astype(f32)


def middle_norm(inputs, one, two, gain):
    rows, width = inputs.shape
    by_rows = pl.BlockSpec((ROWS, width), lambda step: (step, 0))
    shape = jax.ShapeDtypeStruct
    return gridded(
        10, middle_kernel, rows // ROWS,
        [by_rows] + half_specs(len(one) + len(two), rows, width) + [whole((1, width))],
        (by_rows,) * 3,
        (shape((rows, width), f32), shape((rows, width), bf16), shape((rows, width), f32)),
        (inputs, *one, *two, gain[None, :]),
    )


def norm_back_kernel(parts, value_ref, direct_ref, *refs):
    grad = of_halves(refs[:parts])
    gain_ref, *out_refs, gain_grad_ref = refs[parts:]
    value = value_ref[...].astype(f32)
    scale = lax.rsqrt(jnp.mean(value * value, axis=-1, keepdims=True) + epsilon)
    unit = value * scale
    inner = grad * gain_ref[...]
    total = direct_ref[...].astype(f32) + scale * (inner - unit * jnp.mean(inner * unit, axis=-1, keepdims=True))
    for ref in out_refs:
        ref[...] = total.astype(ref.dtype)

    @pl.when(pl.program_id(0) == 0)
    def _():
        gain_grad_ref[...] = jnp.zeros_like(gain_grad_ref)

    gain_grad_ref[...] += jnp.sum(grad * unit, axis=0, keepdims=True)


def norm_back(value, direct, one, two, gain, types):
    rows, width = value.shape
    steps = rows // ROWS
    by_rows = pl.BlockSpec((ROWS, width), lambda step: (step, 0))
    shape = jax.ShapeDtypeStruct
    return gridded(
        9, functools.partial(norm_back_kernel, len(one) + len(two)), steps,
        [by_rows, by_rows] + half_specs(len(one) + len(two), rows, width) + [whole((1, width))],
        (by_rows,) * len(types) + (pl.BlockSpec((1, width), lambda step: (0, 0)),),
        tuple(shape((rows, width), kind) for kind in types) + (shape((1, width), f32),),
        (value, direct, *one, *two, gain[None, :]),
    )


FBLOCK = 256


def unit_gradients(normed, cotangent, wg_ref, wu_ref, wd_ref):
    gate = mm(normed, wg_ref[...])
    upper = mm(normed, wu_ref[...])
    grad = mm(cotangent, wd_ref[...])
    share = 0.5 * jnp.tanh(0.5 * gate) + 0.5
    swish = gate * share
    return (
        (swish * upper).astype(bf16),
        (grad * upper * (share + swish * (1.0 - share))).astype(bf16),
        (grad * swish).astype(bf16),
    )


def units_kernel(normed_ref, cot_ref, wg_ref, wu_ref, wd_ref, hidden_ref, gg_ref, gu_ref):
    hidden_ref[...], gg_ref[...], gu_ref[...] = unit_gradients(normed_ref[...], cot_ref[...], wg_ref, wu_ref, wd_ref)


def ffn_units(normed, cotangent, w_gate, w_up, w_down):
    rows, width = normed.shape
    total = w_gate.shape[1]
    units = pl.BlockSpec((rows, FBLOCK), lambda step: (0, step))
    weights = pl.BlockSpec((width, FBLOCK), lambda step: (0, step))
    return gridded(
        21, units_kernel, total // FBLOCK,
        [whole((rows, width))] * 2 + [weights] * 3,
        (units,) * 3,
        (jax.ShapeDtypeStruct((rows, total), bf16),) * 3,
        (normed, cotangent, w_gate, w_up, w_down),
    )


def partner_kernel(
    wide_ref, cot_ref, cot_t_ref, own_t_ref, own_ref, wg_ref, wu_ref, wd_ref,
    gg_ref, gu_ref, keep_ref, send_ref, normed_ref,
):
    half = keep_ref.shape[0]

    @pl.when(pl.program_id(0) == 0)
    def _():
        normed_ref[...] = wide_ref[...].astype(bf16)

    hidden, gg_ref[...], gu_ref[...] = unit_gradients(normed_ref[...], cot_ref[...], wg_ref, wu_ref, wd_ref)
    total = mm(own_t_ref[...], own_ref[...]) + mm(cot_t_ref[...], hidden)
    keep_ref[...] = total[:half]
    send_ref[...] = total[half:]


def partner_units(normed, cotangent, cotangent_t, own_t, own_hidden, w_gate, w_up, w_down):
    rows, width = normed.shape
    total = w_gate.shape[1]
    units = pl.BlockSpec((rows, FBLOCK), lambda step: (0, step))
    weights = pl.BlockSpec((width, FBLOCK), lambda step: (0, step))
    grads = pl.BlockSpec((width // 4, FBLOCK), lambda step: (0, step))
    shape = jax.ShapeDtypeStruct
    return gridded(
        27, partner_kernel, total // FBLOCK,
        [whole((rows, width))] * 2 + [whole((width // 2, rows))] * 2 + [units] + [weights] * 3,
        (units,) * 2 + (grads,) * 2,
        (shape((rows, total), bf16),) * 2 + (shape((width // 4, total), f32),) * 2,
        (normed, cotangent, cotangent_t, own_t, own_hidden, w_gate, w_up, w_down),
        [pltpu.VMEM((rows, width), bf16)],
    )


def pair_kernel(one_t_ref, two_t_ref, one_ref, two_ref, keep_ref, send_ref):
    half = keep_ref.shape[0]
    total = mm(one_t_ref[...], one_ref[...]) + mm(two_t_ref[...], two_ref[...])
    keep_ref[...] = total[:half]
    send_ref[...] = total[half:]


def pair_weights(one_t, two_t, one, two):
    half, rows = one_t.shape
    total = one.shape[1]
    block = 3 * FBLOCK
    units = pl.BlockSpec((rows, block), lambda step: (0, step))
    grads = pl.BlockSpec((half // 2, block), lambda step: (0, step))
    return gridded(
        10, pair_kernel, total // block,
        [whole((half, rows))] * 2 + [units] * 2, (grads,) * 2,
        (jax.ShapeDtypeStruct((half // 2, total), f32),) * 2, (one_t, two_t, one, two),
    )


def products_kernel(count, *refs):
    lefts, rights, outs = refs[:count], refs[count : 2 * count], refs[2 * count :]
    total = mm(lefts[0][...], rights[0][...], NT)
    for left, right in zip(lefts[1:], rights[1:]):
        total += mm(left[...], right[...], NT)
    each = total.shape[0] // len(outs)
    for number, ref in enumerate(outs):
        ref[...] = total[number * each : (number + 1) * each]


def products(lefts, rights, pieces, time=12):
    rows, columns = lefts[0].shape[0], rights[0].shape[0]
    out = pl.BlockSpec((rows // pieces, BLOCK), lambda step: (0, step))
    return gridded(
        time, functools.partial(products_kernel, len(lefts)), columns // BLOCK,
        [whole(item.shape) for item in lefts]
        + [pl.BlockSpec((BLOCK, item.shape[1]), lambda step: (step, 0)) for item in rights],
        (out,) * pieces, (jax.ShapeDtypeStruct((rows // pieces, columns), f32),) * pieces, tuple(lefts) + tuple(rights),
    )


def join_kernel(middle_ref, *refs):
    refs[-1][...] = (middle_ref[...] + of_halves(refs[:-1])).astype(bf16)


def joined(middle, one, two):
    rows, width = middle.shape
    by_rows = pl.BlockSpec((ROWS, width), lambda step: (step, 0))
    return gridded(
        7, join_kernel, rows // ROWS,
        [by_rows] + half_specs(len(one) + len(two), rows, width), (by_rows,),
        (jax.ShapeDtypeStruct((rows, width), bf16),), (middle, *one, *two),
    )[0]


def stacked_kernel(left_ref, *refs):
    rights, (keep_ref, send_ref) = refs[:-2], refs[-2:]
    half = keep_ref.shape[0]
    low = 0
    for right in rights:
        high = low + right.shape[1]
        total = mm(left_ref[...], right[...])
        keep_ref[:, low:high] = total[:half]
        send_ref[:, low:high] = total[half:]
        low = high


def stacked_weights(left_t, rights):
    width = left_t.shape[0]
    total = sum(item.shape[1] for item in rights)
    return pl.pallas_call(
        stacked_kernel,
        out_shape=(jax.ShapeDtypeStruct((width // 2, total), f32),) * 2,
        in_specs=[VMEM_SPEC] * (1 + len(rights)),
        out_specs=(VMEM_SPEC,) * 2,
        compiler_params=PARAMS,
        cost_estimate=cost(6),
    )(left_t, *rights)


def turned_kernel(places_ref, left_ref, *refs):
    rights, (keep_ref, send_ref, scratch, turned_ref) = refs[:-4], refs[-4:]
    half = keep_ref.shape[0]
    turn(left_ref[...], places_ref, scratch, turned_ref)
    low = 0
    for right in rights:
        high = low + right.shape[1]
        send_ref[:, low:high] = mm(turned_ref[half:, :], right[...])
        keep_ref[:, low:high] = mm(turned_ref[:half, :], right[...])
        low = high


def turned_weights(places, left, rights, time=6):
    rows, width = left.shape
    total = sum(item.shape[1] for item in rights)
    return pl.pallas_call(
        turned_kernel,
        out_shape=(jax.ShapeDtypeStruct((width // 2, total), f32),) * 2,
        in_specs=[SMEM_SPEC] + [VMEM_SPEC] * (1 + len(rights)),
        out_specs=(VMEM_SPEC,) * 2,
        scratch_shapes=[pltpu.VMEM((width, rows), f32), pltpu.VMEM((width, rows), bf16)],
        compiler_params=PARAMS,
        cost_estimate=cost(time),
    )(places, left, *rights)


def swap(values):
    return lax.ppermute(values, "tensor", [(0, 1), (1, 0)])


LABELS = ((0, 1, 2), (2, 0, 1))
DOWN_LABELS = ((0, 1, 2), (2, 0, 1))
LATE_LABELS = ((0, 1, 2), (2, 0, 1))


class Layout:
    def __init__(self, rows, labels):
        self.labels = labels
        self.devices = lax.axis_size("dp")
        self.bits = self.devices.bit_length() - 1
        core = lax.axis_index("tensor")
        self.mine = self.label(lax.axis_index("dp"), core)
        numbers = self.label(jnp.arange(self.devices, dtype=jnp.int32), core)
        each = rows // self.devices
        first = (numbers & 1) ^ self.bit(0)
        second = ((numbers >> 1) & 1) ^ self.bit(1)
        self.halves = (first * (self.devices // 2) + (numbers >> 1)) * each
        self.quarters = (first * (self.devices // 2) + second * (self.devices // 4) + (numbers >> 2)) * each

    def label(self, number, core):
        first, second = (
            (number & ~7) | functools.reduce(jnp.bitwise_or, [((number >> self.labels[one][bit]) & 1) << bit for bit in range(3)])
            for one in range(2)
        )
        return jnp.where(core == 1, second, first).astype(jnp.int32)

    def bit(self, bit):
        return (self.mine >> bit) & 1

    def exchange(self, values, bit):
        own = [self.labels[core][bit] if bit < 3 else bit for core in range(2)]
        pairs = [(2 * i + core, 2 * (i ^ (1 << own[core])) + core) for i in range(self.devices) for core in range(2)]
        return lax.ppermute(values, ("dp", "tensor"), pairs)


class Scatter:
    def __init__(self, layout, keep, send, first):
        self.layout = layout
        self.stage = first
        self.left = list(range(layout.bits - 1, first, -1))
        self.addends = [self.spread(keep)]
        self.send = self.spread(send)

    def spread(self, values):
        return values.reshape((2,) * len(self.left) + (-1, values.shape[1]))

    def exchange(self):
        self.addends.append(self.layout.exchange(self.send, self.stage))
        self.stage += 1

    def prepare(self, earlier=None):
        mine = self.layout.bit(self.stage)
        axis = self.left.index(self.stage)
        if earlier is not None:
            self.addends[-1] = after(self.addends[-1], earlier)

        def take(array, which):
            return lax.dynamic_index_in_dim(array, which, axis, keepdims=False)

        self.send = functools.reduce(jnp.add, [take(item, 1 - mine) for item in self.addends])
        self.addends = [take(item, mine) for item in self.addends]
        self.left.remove(self.stage)
        self.exchange()
        return self.send

    def result(self):
        return functools.reduce(jnp.add, self.addends)


def finish(scatter, earlier):
    while scatter.stage < scatter.layout.bits:
        earlier = scatter.prepare(earlier)
    scatter.addends[-1] = after(scatter.addends[-1], earlier)
    total = scatter.result()
    return total, total


def after(values, earlier):
    return lax.optimization_barrier((values, earlier))[0]


def per_device(
    inputs,
    cotangent,
    segment_ids,
    attn_gain,
    w_query,
    w_key,
    w_value,
    query_gain,
    key_gain,
    w_output,
    ffn_gain,
    w_gate,
    w_up,
    w_down,
):
    width = inputs.shape[1]
    units = w_gate.shape[1]
    layout = Layout(width, LABELS)
    layout_down = Layout(width, DOWN_LABELS)
    layout_late = Layout(width, LATE_LABELS)
    devices, bits = layout.devices, layout.bits
    each = width // devices
    me = lax.axis_index("dp")

    cotangent_wide = widened(cotangent)
    cotangent_far = layout.exchange(cotangent_wide, 0)
    *part, normed, linear, query, key, value, mixed, cosine, sine = attention_forward(
        after(inputs, cotangent_wide), attn_gain, w_query, w_key, w_value, query_gain, key_gain, segment_ids, w_output
    )
    part_swapped = [swap(item) for item in part]
    (cotangent_t,) = turned(after(cotangent, normed), layout_down.quarters)
    middle, normed_two, normed_wide = middle_norm(inputs, after(part, cotangent_t), part_swapped, ffn_gain)
    (normed_t,) = turned(after(normed, normed_wide), layout_late.halves, part=1)
    normed_far = layout.exchange(after(normed_wide, (cotangent_far, normed_t)), 0)
    hidden, gg, gu = ffn_units(after(normed_two, normed_wide), cotangent, w_gate, w_up, w_down)
    cotangent_far, cotangent_far_t = turned(after(cotangent_far, hidden), layout_down.quarters, True)
    grad_two = products((after(gg, cotangent_far_t), gu), (w_gate, w_up), 2)
    grad_two_swapped = [swap(item) for item in grad_two]
    (normed_two_t,) = turned(after(normed_two, grad_two), layout.quarters)
    far_gg, far_gu, keep, send = partner_units(
        after(normed_far, normed_two_t), cotangent_far, cotangent_far_t, cotangent_t, hidden, w_gate, w_up, w_down
    )
    down = Scatter(layout_down, keep, send, 1)
    down.exchange()
    (normed_far_t,) = turned(after(normed_far, send), layout.quarters)
    gate = Scatter(layout, *pair_weights(normed_two_t, normed_far_t, gg, far_gg), 1)
    gate.exchange()
    upper = Scatter(layout, *pair_weights(after(normed_two_t, gate.send), normed_far_t, gu, far_gu), 1)
    upper.exchange()
    grad_middle, grad_branch, grad_ffn_gain = norm_back(
        after(middle, upper.send), cotangent, grad_two, grad_two_swapped, ffn_gain, (f32, bf16)
    )
    token = down.prepare(grad_branch)

    def heads_back(k_pair, token):
        return attention_backward(
            k_pair, after(grad_branch, token), w_output, linear, query, key, value, query_gain, key_gain,
            (cosine, sine), segment_ids,
        )

    back = [heads_back(0, token)]
    ffn = products((after(hidden, back[0]),), (w_down,), 1)
    token = gate.prepare(ffn)
    token = down.prepare(token)
    for k_pair in range(1, w_key.shape[1] // LANES):
        back.append(heads_back(k_pair, token))
        token = back[-1]
    gq, gk, gv, gains = zip(*back)
    gains = sum(gains)
    three = Scatter(layout_late, *stacked_weights(normed_t, gq + gk + gv), 0)
    three.exchange()
    sum_down, token = finish(down, three.send)
    w_parts = [
        weight[:, at : at + piece.shape[1]]
        for weight, pieces in ((w_query, gq), (w_key, gk), (w_value, gv))
        for piece, at in zip(pieces, range(0, weight.shape[1], pieces[0].shape[1]))
    ]
    grad_one = products((after(gq[0], token),) + gq[1:] + gk + gv, w_parts, 1)
    grad_one_swapped = [swap(item) for item in grad_one]
    token = gate.prepare(grad_one)
    output = Scatter(layout_late, *turned_weights(layout_late.halves, after(grad_branch, token), (mixed,), 60), 0)
    output.exchange()
    token = upper.prepare(output.send)
    token = three.prepare(token)
    grad_inputs, grad_attn_gain = norm_back(
        inputs, after(grad_middle, token), grad_one, grad_one_swapped, attn_gain, (bf16,)
    )
    small = jnp.concatenate(
        [
            grad_attn_gain.reshape(-1, LANES) * 0.5,
            grad_ffn_gain.reshape(-1, LANES) * 0.5,
            jnp.pad(gains[:2, :HEAD_DIM] + gains[:2, HEAD_DIM:], ((0, 6), (0, LANES - HEAD_DIM))),
        ]
    )
    small_far = swap(small)
    sum_gate, token = finish(gate, small)
    token = three.prepare(token)
    token = upper.prepare(token)
    token = output.prepare(token)
    small = small + after(small_far, token)
    small_far = layout.exchange(small, 0)
    ffn_swapped = [swap(after(item, small)) for item in ffn]
    token = three.prepare(small)
    token = output.prepare(token)
    small = small + after(small_far, token)
    small_far = layout.exchange(small, 1)
    block_out = joined(after(middle, small), ffn, ffn_swapped)
    token = output.prepare(block_out)
    small = small + after(small_far, token)
    small_far = layout.exchange(small, 2)
    sum_upper, token = finish(upper, small)
    sum_output, token = finish(output, token)
    small = small + after(small_far, token)
    for bit in range(3, bits):
        small = small + layout.exchange(small, bit)
    sum_three, token = finish(three, token)
    lines = width // LANES
    sum_attn_gain = lax.dynamic_slice_in_dim(small[:lines].reshape(width), me * each, each)
    sum_ffn_gain = lax.dynamic_slice_in_dim(small[lines : 2 * lines].reshape(width), me * each, each)

    q_width, k_width = w_query.shape[1], w_key.shape[1]
    return (
        block_out,
        grad_inputs,
        sum_attn_gain,
        sum_three[:, :q_width],
        sum_three[:, q_width : q_width + k_width],
        sum_three[:, q_width + k_width :],
        small[2 * lines, :HEAD_DIM],
        small[2 * lines + 1, :HEAD_DIM],
        sum_output,
        sum_ffn_gain,
        sum_gate,
        sum_upper,
        sum_down,
    )


def solution(mesh):
    placed = (
        P("dp", None),
        P("dp", None),
        P("dp"),
        P(),
        P(None, "tensor"),
        P(None, "tensor"),
        P(None, "tensor"),
        P(),
        P(),
        P(None, "tensor"),
        P(),
        P(None, "tensor"),
        P(None, "tensor"),
        P(None, "tensor"),
    )
    return jax.shard_map(
        per_device,
        mesh=mesh,
        in_specs=placed,
        out_specs=(
            P("dp", None),
            P("dp", None),
            P("dp"),
            P("dp", "tensor"),
            P("dp", "tensor"),
            P("dp", "tensor"),
            P(),
            P(),
            P("dp", "tensor"),
            P("dp"),
            P("dp", "tensor"),
            P("dp", "tensor"),
            P("dp", "tensor"),
        ),
        check_vma=False,
    )
```
